128 devices in a mesh: seq: 16 (over y, x), grp: 8 (over z, core).
Axes of the slice: x: 4, y: 4, z: 4, core: 2. Of those that a mesh axis runs over, the one named last changes fastest.
Arguments:
- tokens: bfloat16 [2, 4096, 2048], P(None, 'seq'), may hold values from -6 to 6
- lengths: int32 [2], replicated, may hold values from 2048 to 4096, as said below
- norm_attn: float32 [2048], replicated, may hold values from 0.5 to 1.5
- w_query: bfloat16 [2048, 2048], P(None, 'grp'), may hold values from -0.125 to 0.125
- w_key: bfloat16 [2048, 1024], P(None, 'grp'), may hold values from -0.125 to 0.125
- w_value: bfloat16 [2048, 1024], P(None, 'grp'), may hold values from -0.125 to 0.125
- w_gate: bfloat16 [2048, 16], P(None, 'grp'), may hold values from -0.125 to 0.125
- norm_query: float32 [128], replicated, may hold values from 1 to 1.6
- norm_key: float32 [128], replicated, may hold values from 1 to 1.6
- w_out: bfloat16 [2048, 2048], P('grp'), may hold values from -2 to 2
- norm_ffn: float32 [2048], replicated, may hold values from 0.5 to 1.5
- w_ffn_gate: bfloat16 [2048, 6144], P(None, 'grp'), may hold values from -0.125 to 0.125
- w_ffn_up: bfloat16 [2048, 6144], P(None, 'grp'), may hold values from -0.125 to 0.125
- w_down: bfloat16 [6144, 2048], P('grp'), may hold values from -0.109375 to 0.109375
- cotangent: bfloat16 [2, 4096, 2048], P(None, 'seq'), may hold values from -6 to 6
Outputs:
- mixed: bfloat16 [2, 4096, 2048], P(None, 'seq')
- grad_tokens: bfloat16 [2, 4096, 2048], P(None, 'seq')
- grad_norm_attn: float32 [2048], replicated
- grad_w_query: float32 [2048, 2048], P(None, 'grp')
- grad_w_key: float32 [2048, 1024], P(None, 'grp')
- grad_w_value: float32 [2048, 1024], P(None, 'grp')
- grad_w_gate: float32 [2048, 16], P(None, 'grp')
- grad_norm_query: float32 [128], replicated
- grad_norm_key: float32 [128], replicated
- grad_w_out: float32 [2048, 2048], P('grp')
- grad_norm_ffn: float32 [2048], replicated
- grad_w_ffn_gate: float32 [2048, 6144], P(None, 'grp')
- grad_w_ffn_up: float32 [2048, 6144], P(None, 'grp')
- grad_w_down: float32 [6144, 2048], P('grp')
The draws below stay inside these ranges and needn't reach their ends.
Inputs may be any that keep to these rules, and one draw needn't show every extreme that they name: Bucket b holds one sequence of lengths[b] true tokens at its start, padding after it; exactly one bucket, drawn from the seed, is full with 4096 tokens.
All inputs are finite; a program needn't handle non-finite values.
Results may differ from the reference program's by a relative error of at most 0.025.
Values may be sent and summed in bfloat16 or wider, within the bound.
A program may use at most 192 MiB of HBM per device.

```python
import math
from functools import partial
import jax
import jax.numpy as jnp
from jax import lax

D = 2048
HEADS = 16
KV_HEADS = 8
HD = 128
FF = 6144
BUCKETS = 2
LEN = 4096


def draw_lengths(key, part):
    key = jax.random.fold_in(key, 1)
    drawn = jax.random.randint(jax.random.fold_in(key, 2), (BUCKETS,), LEN // 2, LEN)
    chosen = jax.random.randint(jax.random.fold_in(key, 3), (), 0, BUCKETS)
    return jnp.where(jnp.arange(BUCKETS) == chosen, LEN, drawn).astype(jnp.int32)


def shard_levels(stream_key, extent, cuts, low, largest):
    level = 1.0
    for dim, blocks in cuts:
        heights = jax.random.uniform(jax.random.fold_in(jax.random.fold_in(stream_key, 6), dim), (blocks,), jnp.float32, low / len(cuts), largest / len(cuts))
        level = level * jnp.repeat(jnp.exp(heights), extent[dim] // blocks).reshape((-1,) + (1,) * (len(extent) - 1 - dim))
    return level


def scatter_about(key, dims, width, reach, cuts=(), kind=jnp.bfloat16):
    values = width * jax.random.normal(key, dims, jnp.float32)
    if cuts:
        values = values * shard_levels(key, dims, cuts, -0.22, 0.18)
    return jnp.clip(values, -reach, reach).astype(kind)


def setup_inputs(seed: int = 0) -> dict:
    key_list = jax.random.split(jax.random.key(seed), 16)
    tokens = scatter_about(key_list[0], (BUCKETS, LEN, D), 1.0, 6.0, ((1, 16),))
    lengths = draw_lengths(jax.random.fold_in(key_list[15], 71), 0)
    norm_attn = jnp.clip(1.0 + 0.1 * jax.random.normal(key_list[2], (D,), jnp.float32), 0.5, 1.5)
    w_query = scatter_about(key_list[3], (D, HEADS * HD), D ** -0.5, 0.125, ((1, 8),))
    w_key = scatter_about(key_list[4], (D, KV_HEADS * HD), D ** -0.5, 0.125, ((1, 8),))
    w_value = scatter_about(key_list[5], (D, KV_HEADS * HD), D ** -0.5, 0.125, ((1, 8),))
    w_gate = scatter_about(key_list[6], (D, HEADS), D ** -0.5, 0.125, ((1, 8),))
    norm_query = jnp.clip(jnp.exp(jax.random.uniform(key_list[7], (HD,), jnp.float32, math.log(1.0), math.log(1.6))), 1.0, 1.6)
    norm_key = jnp.clip(jnp.exp(jax.random.uniform(key_list[8], (HD,), jnp.float32, math.log(1.0), math.log(1.6))), 1.0, 1.6)
    w_out = scatter_about(key_list[9], (HEADS * HD, D), (max(1, HEADS * HD // 256)) ** -0.5, 2.0, ((0, 8),))
    norm_ffn = jnp.clip(1.0 + 0.1 * jax.random.normal(key_list[10], (D,), jnp.float32), 0.5, 1.5)
    w_ffn_gate = scatter_about(key_list[11], (D, FF), D ** -0.5, 0.125, ((1, 8),))
    w_ffn_up = scatter_about(key_list[12], (D, FF), D ** -0.5, 0.125, ((1, 8),))
    w_down = scatter_about(key_list[13], (FF, D), (FF // 2) ** -0.5, 0.109375, ((0, 8),))
    cotangent = scatter_about(key_list[14], (BUCKETS, LEN, D), 1.0, 6.0, ((1, 16),))
    return dict(tokens=tokens, lengths=lengths, norm_attn=norm_attn, w_query=w_query, w_key=w_key, w_value=w_value, w_gate=w_gate, norm_query=norm_query, norm_key=norm_key, w_out=w_out, norm_ffn=norm_ffn, w_ffn_gate=w_ffn_gate, w_ffn_up=w_ffn_up, w_down=w_down, cotangent=cotangent)


epsilon = 1e-06
rope_base = 1000000.0

@jax.custom_vjp
def low(v):
    return lax.optimization_barrier(v.astype(jnp.bfloat16)).astype(jnp.float32)

@jax.custom_vjp
def low_back(v):
    return v

def low_keep(v):
    return (low(v), None)

def low_pass(kept, grad):
    return (grad,)

def back_keep(v):
    return (v, None)

def back_low(kept, grad):
    return (low(grad),)
low.defvjp(low_keep, low_pass)
low_back.defvjp(back_keep, back_low)

def rms_norm(values, gain):
    return values * lax.rsqrt(lax.optimization_barrier(jnp.mean(values * values, axis=-1, keepdims=True)) + epsilon) * gain

def rotate(values, positions, sign):
    half = values.shape[-1] // 2
    freq = rope_base ** (-jnp.arange(half, dtype=jnp.float32) * (2.0 / values.shape[-1]))
    angle = positions.astype(jnp.float32)[:, None] * freq[None, :]
    cosine = jnp.cos(angle)[:, None, :]
    sine = sign * jnp.sin(angle)[:, None, :]
    first = values[..., :half]
    second = values[..., half:]
    return jnp.concatenate([first * cosine - second * sine, second * cosine + first * sine], axis=-1)

def attend_block(query_block, block_start, keys_here, values_here, length, score_scale):
    scores = jnp.einsum('kgqd,kld->kgql', query_block, keys_here, precision=lax.Precision.HIGHEST) * score_scale
    scores = low_back(scores)
    rows_here = block_start + jnp.arange(query_block.shape[2], dtype=jnp.int32)
    columns = jnp.arange(keys_here.shape[1], dtype=jnp.int32)
    allowed = (columns[None, :] <= rows_here[:, None]) & (columns[None, :] < length)
    scores = jnp.where(allowed, scores, -1e+30)
    highest = lax.optimization_barrier(jnp.max(scores, axis=-1, keepdims=True))
    weights = jnp.exp(scores - highest)
    weights = low(weights / lax.optimization_barrier(jnp.sum(weights, axis=-1, keepdims=True)))
    return jnp.einsum('kgql,kld->kgqd', weights, values_here, precision=lax.Precision.HIGHEST)

def forward(tokens, norm_attn, w_query, w_key, w_value, w_gate, norm_query, norm_key, w_out, norm_ffn, w_ffn_gate, w_ffn_up, w_down, lengths):
    precise = lax.Precision.HIGHEST
    bucket_count, seq_len, model_width = tokens.shape
    rows_all = bucket_count * seq_len
    group_size = HEADS // KV_HEADS
    normed = low(rms_norm(tokens, norm_attn)).reshape(rows_all, model_width)
    query = low_back(jnp.dot(normed, w_query, precision=precise)).reshape(bucket_count, seq_len, HEADS, HD)
    keys = low_back(jnp.dot(normed, w_key, precision=precise)).reshape(bucket_count, seq_len, KV_HEADS, HD)
    values = low_back(low(jnp.dot(normed, w_value, precision=precise))).reshape(bucket_count, seq_len, KV_HEADS, HD)
    logits = low_back(jnp.dot(normed, w_gate, precision=precise)).reshape(bucket_count, seq_len, HEADS)
    positions = jnp.arange(seq_len, dtype=jnp.int32)
    query = low(rotate(rms_norm(query, norm_query), positions, 1.0))
    keys = low(rotate(rms_norm(keys, norm_key), positions, 1.0))
    block_rows = min(512, seq_len)
    block_count = seq_len // block_rows
    starts = jnp.arange(block_count, dtype=jnp.int32) * block_rows
    outputs = []
    for bucket in range(bucket_count):
        query_blocks = query[bucket].reshape(block_count, block_rows, KV_HEADS, group_size, HD).transpose(0, 2, 3, 1, 4)
        keys_here = keys[bucket].transpose(1, 0, 2)
        values_here = values[bucket].transpose(1, 0, 2)
        block_step = jax.checkpoint(partial(attend_block, keys_here=keys_here, values_here=values_here, length=lengths[bucket], score_scale=HD ** (-0.5)))
        blocks_out = lax.map(lambda pair: block_step(pair[0], pair[1]), (query_blocks, starts))
        outputs.append(blocks_out.transpose(0, 3, 1, 2, 4).reshape(seq_len, HEADS, HD))
    attended = low_back(jnp.stack(outputs))
    gated = low(attended * jax.nn.sigmoid(logits)[..., None]).reshape(rows_all, HEADS * HD)
    attn_out = low_back(jnp.dot(gated, w_out, precision=precise))
    middle = tokens.reshape(rows_all, model_width) + attn_out
    normed_two = low(rms_norm(middle, norm_ffn))
    gate_pre = low_back(jnp.dot(normed_two, w_ffn_gate, precision=precise))
    up_proj = low_back(jnp.dot(normed_two, w_ffn_up, precision=precise))
    hidden = low(jax.nn.silu(gate_pre) * up_proj)
    feed_out = low_back(jnp.dot(hidden, w_down, precision=precise))
    return (middle + feed_out).reshape(bucket_count, seq_len, model_width)

def reference(tokens, lengths, norm_attn, w_query, w_key, w_value, w_gate, norm_query, norm_key, w_out, norm_ffn, w_ffn_gate, w_ffn_up, w_down, cotangent):
    floats = [array.astype(jnp.float32) for array in (tokens, norm_attn, w_query, w_key, w_value, w_gate, norm_query, norm_key, w_out, norm_ffn, w_ffn_gate, w_ffn_up, w_down)]
    mixed, pullback = jax.vjp(lambda *params: forward(*params, lengths), *floats)
    positions = jnp.arange(LEN, dtype=jnp.int32)
    live_rows = (positions[None, :] < lengths[:, None]).astype(jnp.float32)
    loss_ratio = BUCKETS * LEN / jnp.sum(lengths).astype(jnp.float32)
    seeds = cotangent.astype(jnp.float32) * live_rows[:, :, None] * loss_ratio
    grads = pullback(seeds)
    return (mixed.astype(jnp.bfloat16), grads[0].astype(jnp.bfloat16), grads[1], grads[2], grads[3], grads[4], grads[5], grads[6], grads[7], grads[8], grads[9], grads[10], grads[11], grads[12])
```

```python
import functools

import jax
import jax.numpy as jnp
import numpy as np
from jax import lax
from jax.experimental import pallas as pl
from jax.experimental.pallas import tpu as pltpu
from jax.sharding import Mesh
from jax.sharding import PartitionSpec as P

GRP = ("grp_0", "grp_1")
SEQ = ("seq_0", "seq_1")
SEQ_GRP = ("seq_0", "seq_1", "grp_0", "grp_1")
MESH = pl.DeviceIdType.MESH
VMEM_LIMIT = 56 * 2**20

f32 = jnp.float32
bf16 = jnp.bfloat16


epsilon = 1e-06
rope_base = 1000000.0


def unit_scale(values):
    inverse = lax.rsqrt(jnp.mean(values * values, axis=-1, keepdims=True) + epsilon)
    return (values * inverse, inverse)


def norm_back(grad_unit, unit, inverse):
    return inverse * (grad_unit - unit * jnp.mean(grad_unit * unit, axis=-1, keepdims=True))


ROW_CONTRACT = (((1,), (1,)), ((), ()))
COL_CONTRACT = (((0,), (0,)), ((), ()))


def send(source, target, sems, slot, to):
    copy = pltpu.make_async_remote_copy(
        src_ref=source,
        dst_ref=target,
        send_sem=sems.at[0, slot],
        recv_sem=sems.at[1, slot],
        device_id=to,
        device_id_type=MESH,
    )
    copy.start()
    return copy


def group_places():
    z = lax.axis_index("grp_0")
    core = lax.axis_index("grp_1")
    ring = lax.axis_size("grp_0")
    above = {"grp_0": lax.rem(z + 1, ring)}
    below = {"grp_0": lax.rem(z + ring - 1, ring)}
    twin = {"grp_1": 1 - core}
    return z, core, above, below, twin


def greet(places):
    barrier = pltpu.get_barrier_semaphore()
    for place in places:
        pl.semaphore_signal(barrier, inc=1, device_id=place, device_id_type=MESH)
    return lambda: pl.semaphore_wait(barrier, len(places))


def group_rows(z, core, far, share):
    return pl.multiple_of((lax.rem(z + far, 4) * 2 + core) * share, share)


FAR = (2, 1, 3, 0)


def sum_rows(product, share, ready, scratch):
    mine, twin_out, twin_in, low, ring, twin_sems, ring_sems = scratch
    z, core, above, below, twin = group_places()
    half = share // 2
    top, bottom = pl.ds(0, half), pl.ds(half, half)

    def put_twin(cols, block):
        twin_out[:, :, cols] = block.astype(bf16)

    def put_mine(cols, block):
        mine[:, :, cols] = block

    product(1 - core, put_twin)
    ready()
    pairs = [send(twin_out.at[k], twin_in.at[k], twin_sems, k, twin) for k in range(4)]
    product(core, put_mine)

    def joined(k, rows):
        return mine[k, rows, :] + twin_in[k, rows, :].astype(f32)

    pairs[0].wait_recv()
    low[0] = joined(0, pl.ds(0, share)).astype(bf16)
    steps = [
        send(low.at[0, top], ring.at[0], ring_sems, 0, above),
        send(low.at[0, bottom], ring.at[1], ring_sems, 1, below),
    ]
    pairs[1].wait_recv()
    low[1, bottom, :] = joined(1, bottom).astype(bf16)
    steps.append(send(low.at[1, bottom], ring.at[2], ring_sems, 2, above))
    pairs[2].wait_recv()
    low[2, top, :] = joined(2, top).astype(bf16)
    steps.append(send(low.at[2, top], ring.at[3], ring_sems, 3, below))
    steps[0].wait_recv()
    low[1, top, :] = (joined(1, top) + ring[0].astype(f32)).astype(bf16)
    steps.append(send(low.at[1, top], ring.at[4], ring_sems, 4, above))
    steps[1].wait_recv()
    low[2, bottom, :] = (joined(2, bottom) + ring[1].astype(f32)).astype(bf16)
    steps.append(send(low.at[2, bottom], ring.at[5], ring_sems, 5, below))
    pairs[3].wait_recv()
    for step in steps[2:]:
        step.wait_recv()
    total = jnp.concatenate(
        [
            joined(3, top) + ring[3].astype(f32) + ring[4].astype(f32),
            joined(3, bottom) + ring[2].astype(f32) + ring[5].astype(f32),
        ],
        axis=0,
    )
    return total, pairs + steps


def join_rows(whole, share, twin_sems, ring_sems):
    z, core, above, below, twin = group_places()
    half = share // 2

    def part(far, side):
        start = group_rows(z, core, far, share)
        return whole.at[pl.ds(pl.multiple_of(start + side * half, half), half), :]

    def hand(far, side, sems, slot, to):
        block = part(far, side)
        return send(block, block, sems, slot, to)

    own = whole.at[pl.ds(group_rows(z, core, 0, share), share), :]
    up = [hand(0, 0, ring_sems, 0, above), hand(0, 1, ring_sems, 1, above)]
    down = [hand(0, 1, ring_sems, 2, below), hand(0, 0, ring_sems, 3, below)]
    across = [send(own, own, twin_sems, 0, twin)]
    up[0].wait_recv()
    up.append(hand(3, 0, ring_sems, 4, above))
    across.append(hand(3, 0, twin_sems, 1, twin))
    down[0].wait_recv()
    down.append(hand(1, 1, ring_sems, 5, below))
    across.append(hand(1, 1, twin_sems, 2, twin))
    up[1].wait_recv()
    across.append(hand(3, 1, twin_sems, 3, twin))
    down[1].wait_recv()
    across.append(hand(1, 0, twin_sems, 4, twin))
    up[2].wait_recv()
    across.append(hand(2, 0, twin_sems, 5, twin))
    down[2].wait_recv()
    across.append(hand(2, 1, twin_sems, 6, twin))
    for copy in across:
        copy.wait_recv()
    for copy in up + down + across:
        copy.wait_send()


def row_scratch(rows, share, width):
    return [
        pltpu.VMEM((4, share, width), f32),
        pltpu.VMEM((4, share, width), bf16),
        pltpu.VMEM((4, share, width), bf16),
        pltpu.VMEM((3, share, width), bf16),
        pltpu.VMEM((6, share // 2, width), bf16),
        pltpu.SemaphoreType.DMA((2, 4)),
        pltpu.SemaphoreType.DMA((2, 6)),
        pltpu.VMEM((rows, width), bf16),
        pltpu.SemaphoreType.DMA((2, 7)),
        pltpu.SemaphoreType.DMA((2, 6)),
        pltpu.SemaphoreType.DMA((1,)),
    ]


def group_product(lefts, rights, across, share, width):
    z = lax.axis_index("grp_0")
    step = 512

    def product(core, put):
        picked = []
        for left in lefts:
            blocks = [left[pl.ds(group_rows(z, core, far, share), share), :] for far in FAR]
            picked.append(jnp.concatenate(blocks, axis=0))
        for at in range(0, width, step):
            cols = pl.ds(at, step)
            total = None
            for left, right in zip(picked, rights):
                if across:
                    term = lax.dot_general(
                        left, right[cols, :], ROW_CONTRACT, preferred_element_type=f32
                    )
                else:
                    term = jnp.dot(left, right[:, cols], preferred_element_type=f32)
                total = term if total is None else total + term
            put(cols, total.reshape(4, share, step))

    return product


def row_kernel(n_pairs, across, finish, n_extra, n_out, share, width, *refs):
    lefts = refs[:n_pairs]
    rights = refs[n_pairs : 2 * n_pairs]
    extra = refs[2 * n_pairs : 2 * n_pairs + n_extra]
    at = 2 * n_pairs + n_extra
    outs = refs[at : at + n_out]
    whole_out = refs[at + n_out]
    scratch = refs[at + n_out + 1 :]
    z, core, above, below, twin = group_places()
    ready = greet((above, below, twin))
    product = group_product(lefts, rights, across, share, width)
    total, copies = sum_rows(product, share, ready, scratch[:7])
    whole, twin_sems, ring_sems, out_sem = scratch[7:]
    whole[pl.ds(group_rows(z, core, 0, share), share), :] = finish(total, extra, outs)
    for copy in copies:
        copy.wait_send()
    join_rows(whole, share, twin_sems, ring_sems)
    done = pltpu.make_async_copy(whole, whole_out, out_sem.at[0])
    done.start()
    done.wait()


def exchange_rows(name, call_id, lefts, rights, across, finish, extra, out_shapes):
    rows = lefts[0].shape[0]
    share = rows // 8
    width = rights[0].shape[0 if across else 1]
    vmem = pl.BlockSpec(memory_space=pltpu.VMEM)
    body = functools.partial(
        row_kernel, len(lefts), across, finish, len(extra), len(out_shapes), share, width
    )
    flops = 2 * rows * width * sum(left.shape[1] for left in lefts)
    return pl.pallas_call(
        body,
        name=name,
        out_shape=tuple(out_shapes) + (jax.ShapeDtypeStruct((rows, width), bf16),),
        in_specs=[vmem] * (2 * len(lefts) + len(extra)),
        out_specs=(vmem,) * len(out_shapes) + (pl.BlockSpec(memory_space=pl.ANY),),
        scratch_shapes=row_scratch(rows, share, width),
        compiler_params=pltpu.CompilerParams(
            collective_id=call_id, has_side_effects=True, vmem_limit_bytes=VMEM_LIMIT
        ),
        cost_estimate=pl.CostEstimate(
            flops=flops, bytes_accessed=16 * 2**20, transcendentals=0
        ),
    )(*lefts, *rights, *extra)


def finish_middle(total, extra, outs):
    base, gain = extra
    middle_out, scale_out = outs
    middle = base[...].astype(f32) + total
    unit, inverse = unit_scale(middle)
    middle_out[...] = middle
    scale_out[...] = inverse
    return (unit * gain[...]).astype(bf16)


def finish_plain(total, extra, outs):
    return (extra[0][...] + total).astype(bf16)


def finish_grad_middle(total, extra, outs):
    middle, inverse, gain, seed = extra
    grad_out, gain_out = outs
    unit = middle[...] * inverse[...]
    gain_out[...] = jnp.sum(total * unit, axis=0, keepdims=True)
    grad = seed[...] + norm_back(total * gain[...], unit, inverse[...])
    grad_out[...] = grad
    return grad.astype(bf16)


def finish_grad_tokens(total, extra, outs):
    base, gain, grad_middle = extra
    (gain_out,) = outs
    unit, inverse = unit_scale(base[...].astype(f32))
    gain_out[...] = jnp.sum(total * unit, axis=0, keepdims=True)
    return (grad_middle[...] + norm_back(total * gain[...], unit, inverse)).astype(bf16)


def feed_kernel(
    rows_ref,
    seed_ref,
    gate_ref,
    up_ref,
    down_ref,
    hidden_out,
    grad_gate_out,
    grad_up_out,
    w_down_out,
    w_gate_out,
    w_up_out,
    rows_across,
):
    @pl.when(pl.program_id(0) == 0)
    def _():
        rows_across[...] = rows_ref[...].T

    rows = rows_ref[...]
    seed = seed_ref[...]
    gate_pre = jnp.dot(rows, gate_ref[...], preferred_element_type=f32)
    up_proj = jnp.dot(rows, up_ref[...], preferred_element_type=f32)
    grad_hidden = lax.dot_general(seed, down_ref[...], ROW_CONTRACT, preferred_element_type=f32)
    gate_sig = jax.nn.sigmoid(gate_pre)
    silu = gate_pre * gate_sig
    hidden = (silu * up_proj).astype(bf16)
    grad_gate = (grad_hidden * up_proj * gate_sig * (1.0 + gate_pre * (1.0 - gate_sig))).astype(
        bf16
    )
    grad_up = (grad_hidden * silu).astype(bf16)
    hidden_out[...] = hidden
    grad_gate_out[...] = grad_gate
    grad_up_out[...] = grad_up
    w_down_out[...] = lax.dot_general(
        hidden, seed, COL_CONTRACT, preferred_element_type=f32
    ).astype(bf16)
    w_gate_out[...] = jnp.dot(rows_across[...], grad_gate, preferred_element_type=f32).astype(bf16)
    w_up_out[...] = jnp.dot(rows_across[...], grad_up, preferred_element_type=f32).astype(bf16)


def feed_forward(rows, seed, w_gate, w_up, w_down):
    count, width = rows.shape
    units = w_gate.shape[1]
    step = 256
    whole = pl.BlockSpec((count, width), lambda j: (0, 0))
    cols = pl.BlockSpec((width, step), lambda j: (0, j))
    strip = pl.BlockSpec((step, width), lambda j: (j, 0))
    narrow = pl.BlockSpec((count, step), lambda j: (0, j))
    thin = jax.ShapeDtypeStruct((count, units), bf16)
    return pl.pallas_call(
        feed_kernel,
        name="feed_forward",
        grid=(units // step,),
        in_specs=[whole, whole, cols, cols, strip],
        out_specs=(narrow, narrow, narrow, strip, cols, cols),
        out_shape=(
            thin,
            thin,
            thin,
            jax.ShapeDtypeStruct((units, width), bf16),
            jax.ShapeDtypeStruct((width, units), bf16),
            jax.ShapeDtypeStruct((width, units), bf16),
        ),
        scratch_shapes=[pltpu.VMEM((width, count), bf16)],
        compiler_params=pltpu.CompilerParams(vmem_limit_bytes=VMEM_LIMIT),
        cost_estimate=pl.CostEstimate(
            flops=12 * count * width * units, bytes_accessed=24 * 2**20, transcendentals=0
        ),
    )(rows, seed, w_gate, w_up, w_down)


LOG2_E = 1.4426950408889634
STAGES = (
    ((1, 0), (3, 0), (0, 1), (0, 3)),
    ((2, 0), (0, 2)),
    ((1, 1), (1, 3), (3, 1), (3, 3)),
    ((1, 2), (3, 2), (2, 1), (2, 3)),
    ((2, 2),),
)


def angle_tables(block, size, count):
    half = size // 2
    freq = rope_base ** (-np.arange(half, dtype=np.float64) * (2.0 / size))
    inner = np.arange(block)[:, None] * freq[None, :]
    outer = (np.arange(count) * block)[:, None] * freq[None, :]

    def table(angle):
        sine = np.sin(angle)
        cosine = np.cos(angle)
        both = np.stack(
            [
                np.concatenate([cosine, cosine], axis=1),
                np.concatenate([-sine, sine], axis=1),
            ]
        )
        return both.astype(np.float32)

    return table(inner), table(outer)


def local_angles(inner, outer, place):
    cos_in, sin_in = inner[0], inner[1]
    cos_out = outer[0, pl.ds(place, 1), :]
    sin_out = outer[1, pl.ds(place, 1), :]
    return cos_in * cos_out - sin_in * sin_out, sin_in * cos_out + cos_in * sin_out


def turned(values):
    return pltpu.roll(values, values.shape[-1] // 2, axis=values.ndim - 1)


def plane_place():
    return lax.axis_index("seq_0"), lax.axis_index("seq_1")


def plane_sides(axis):
    at = lax.axis_index(axis)
    size = lax.axis_size(axis)
    return {axis: lax.rem(at + 1, size)}, {axis: lax.rem(at + size - 1, size)}


AXES = (("seq_1", "seq_0"), ("seq_0", "seq_1"))


def place_at(path, first, second):
    y, x = plane_place()
    dx, dy = (first, second) if path == 0 else (second, first)
    return lax.rem(y + dy, 4) * 4 + lax.rem(x + dx, 4)


def pass_start(block, axis, sems, slot):
    up, down = plane_sides(axis)
    return [send(block, block, sems, slot, up), send(block, block, sems, slot + 1, down)]


def pass_on(copies, before, after, axis, sems, slot):
    up, down = plane_sides(axis)
    copies[0].wait_recv()
    copies.append(send(before.at[0], before.at[0], sems, slot + 2, up))
    copies[1].wait_recv()
    copies.append(send(after.at[1], after.at[1], sems, slot + 3, down))


def pass_end(copies):
    copies[2].wait_recv()
    copies[3].wait_recv()


class Gather:
    def __init__(self, buffer, sems):
        self.buffer, self.sems = buffer, sems
        self.rings = [{}, {}]

    def block(self, path, first, second):
        return self.buffer.at[place_at(path, first, second), path]

    def slot(self, path, ring):
        return path * 20 + (4 if ring == "first" else ring) * 4

    def begin(self, path, ring):
        axis = AXES[path][0] if ring == "first" else AXES[path][1]
        block = self.block(path, 0 if ring == "first" else ring, 0)
        self.rings[path][ring] = pass_start(block, axis, self.sems, self.slot(path, ring))

    def forward(self, path, ring):
        if ring == "first":
            axis, before, after = AXES[path][0], self.block(path, 3, 0), self.block(path, 1, 0)
        else:
            axis = AXES[path][1]
            before, after = self.block(path, ring, 3), self.block(path, ring, 1)
        pass_on(self.rings[path][ring], before, after, axis, self.sems, self.slot(path, ring))

    def end(self, path, ring):
        pass_end(self.rings[path][ring])

    def start(self):
        for path in (0, 1):
            self.begin(path, "first")
        for path in (0, 1):
            self.begin(path, 0)

    def stage(self, number):
        for path in (0, 1):
            if number == 0:
                self.forward(path, "first")
                self.begin(path, 1)
                self.begin(path, 3)
                self.forward(path, 0)
            elif number == 1:
                self.end(path, "first")
                self.begin(path, 2)
                self.end(path, 0)
            elif number == 2:
                self.forward(path, 1)
                self.forward(path, 3)
            elif number == 3:
                self.end(path, 1)
                self.end(path, 3)
                self.forward(path, 2)
            else:
                self.end(path, 2)

    def finish(self):
        for rings in self.rings:
            for copies in rings.values():
                for copy in copies:
                    copy.wait_send()


class Scatter:
    def __init__(self, buffer, recv, sems):
        self.buffer, self.recv, self.sems = buffer, recv, sems
        self.copies = {}

    def block(self, path, ring, step):
        if ring == 4:
            return self.buffer.at[place_at(path, step, 0), path]
        return self.buffer.at[place_at(path, ring, step), path]

    def sides(self, path, ring):
        return plane_sides(AXES[path][0] if ring == 4 else AXES[path][1])

    def push(self, path, ring, half_ref, slot, to):
        at = (path * 5 + ring) * 6 + slot
        copy = send(half_ref, self.recv.at[path, ring, slot], self.sems, at, to)
        self.copies.setdefault((path, ring), []).append(copy)

    def start(self, path, ring):
        up, down = self.sides(path, ring)
        far = self.block(path, ring, 2)
        self.push(path, ring, far.at[0], 0, up)
        self.push(path, ring, far.at[1], 1, down)
        self.push(path, ring, self.block(path, ring, 1).at[1], 2, up)
        self.push(path, ring, self.block(path, ring, 3).at[0], 3, down)

    def forward(self, path, ring):
        up, down = self.sides(path, ring)
        for slot, step, half, to in ((0, 1, 0, up), (1, 3, 1, down)):
            self.copies[path, ring][slot].wait_recv()
            part = self.block(path, ring, step).at[half]
            came = self.recv[path, ring, slot]
            part[...] = (part[...].astype(f32) + came.astype(f32)).astype(bf16)
            self.push(path, ring, part, slot + 4, to)

    def total(self, path, ring):
        for copy in self.copies[path, ring][2:]:
            copy.wait_recv()
        own = self.block(path, ring, 0)
        out = []
        for half, slots in ((0, (3, 4)), (1, (2, 5))):
            value = own[half].astype(f32)
            for slot in slots:
                value = value + self.recv[path, ring, slot].astype(f32)
            out.append(value)
        return out

    def settle(self, path, ring):
        own = self.block(path, ring, 0)
        for half, value in enumerate(self.total(path, ring)):
            own[half] = value.astype(bf16)

    def finish(self):
        for copies in self.copies.values():
            for copy in copies:
                copy.wait_send()


def greet_plane():
    places = [*plane_sides("seq_0"), *plane_sides("seq_1")]
    return greet(places)


def choose(index, options):
    value = options[-1]
    for n in range(len(options) - 2, -1, -1):
        value = jnp.where(index == n, options[n], value)
    return value


def attend_kernel(
    lengths_ref,
    tokens_ref,
    gain_ref,
    w_query_ref,
    w_key_ref,
    w_value_ref,
    w_gate_ref,
    gain_query_ref,
    gain_key_ref,
    inner_ref,
    outer_ref,
    normed_out,
    query_raw_out,
    key_raw_out,
    logits_out,
    query_out,
    keys_out,
    attended_out,
    lse_out,
    gated_out,
    normed,
    kv,
    sums,
    sems,
    out_sems,
):
    ready = greet_plane()
    y, x = plane_place()
    place = y * 4 + x
    rows, width = tokens_ref.shape
    buckets = kv.shape[1]
    block, size = kv.shape[3], kv.shape[4]
    heads = w_query_ref.shape[1] // size
    step = 64

    def norm_rows(n, carry):
        at = pl.ds(pl.multiple_of(n * step, step), step)
        unit, _ = unit_scale(tokens_ref[at, :].astype(f32))
        normed[at, :] = (unit * gain_ref[...]).astype(bf16)
        return carry

    lax.fori_loop(0, rows // step, norm_rows, 0)
    save_normed = pltpu.make_async_copy(normed, normed_out, out_sems.at[0])
    save_normed.start()
    cosine, sine = local_angles(inner_ref, outer_ref, place)

    def turn(values):
        return values * cosine + turned(values) * sine

    key_raw = jnp.dot(normed[...], w_key_ref[...], preferred_element_type=f32)
    value = jnp.dot(normed[...], w_value_ref[...], preferred_element_type=f32)
    key_raw_out[...] = key_raw
    spots = place * block + lax.broadcasted_iota(jnp.int32, (block, size), 0)
    for b in range(buckets):
        live = spots < lengths_ref[b]
        part = slice(b * block, (b + 1) * block)
        unit, _ = unit_scale(key_raw[part])
        kv[place, b, 0] = jnp.where(live, turn(unit * gain_key_ref[...]), 0.0).astype(bf16)
        kv[place, b, 1] = jnp.where(live, value[part], 0.0).astype(bf16)
    gather = Gather(kv, sems)
    ready()
    gather.start()
    query_raw = jnp.dot(normed[...], w_query_ref[...], preferred_element_type=f32)
    query_raw_out[...] = query_raw
    logits_out[...] = jnp.dot(normed[...], w_gate_ref[...], preferred_element_type=f32)
    for b in range(buckets):
        for h in range(heads):
            part = query_raw[b * block : (b + 1) * block, h * size : (h + 1) * size]
            unit, _ = unit_scale(part)
            query_out[b, h * block : (h + 1) * block, :] = turn(
                unit * gain_query_ref[...]
            ).astype(bf16)
    scale = size**-0.5 * LOG2_E

    def weigh(source, b, causal):
        keys, vals = kv[source, b, 0], kv[source, b, 1]
        scores = lax.dot_general(query_out[b], keys, ROW_CONTRACT, preferred_element_type=f32)
        weights = jnp.exp2(scores * scale)
        if causal:
            spot = lax.broadcasted_iota(jnp.int32, (heads * block, block), 0) % block
            column = lax.broadcasted_iota(jnp.int32, (heads * block, block), 1)
            weights = jnp.where(column <= spot, weights, 0.0)
        there = source * block + lax.broadcasted_iota(jnp.int32, (block, size), 0)
        ones = jnp.where(there < lengths_ref[b], 1.0, 0.0).astype(bf16)
        both = jnp.concatenate([vals, ones], axis=1)
        return jnp.dot(weights.astype(bf16), both, preferred_element_type=f32)

    for b in range(buckets):
        sums[b] = weigh(place, b, True)
    for number, offsets in enumerate(STAGES):
        gather.stage(number)

        def one(n, carry):
            which, b = n // buckets, n % buckets
            dx = choose(which, [o[0] for o in offsets])
            dy = choose(which, [o[1] for o in offsets])
            source = lax.rem(y + dy, 4) * 4 + lax.rem(x + dx, 4)

            @pl.when(source < place)
            def _():
                sums[b] = sums[b] + weigh(source, b, False)

            return carry

        lax.fori_loop(0, len(offsets) * buckets, one, 0)
    save_keys = pltpu.make_async_copy(kv, keys_out, out_sems.at[1])
    save_keys.start()
    gates = jax.nn.sigmoid(logits_out[...])
    for b in range(buckets):
        for h in range(heads):
            at = slice(h * block, (h + 1) * block)
            total = sums[b, at, size:]
            attended = sums[b, at, :size] / total
            here = (slice(b * block, (b + 1) * block), slice(h * size, (h + 1) * size))
            attended_out[here] = attended
            lse_out[b, at, :] = jnp.log2(total)
            gated_out[here] = (attended * gates[here[0], h : h + 1]).astype(bf16)
    gather.finish()
    save_normed.wait()
    save_keys.wait()


def attend(call_id, lengths, tokens, gain, w_query, w_key, w_value, w_gate, gain_q, gain_k, tables):
    rows, width = tokens.shape
    size = gain_q.shape[1]
    buckets = lengths.shape[0]
    block = rows // buckets
    heads = w_query.shape[1] // size
    places = lax.axis_size(SEQ)
    vmem = pl.BlockSpec(memory_space=pltpu.VMEM)
    hbm = pl.BlockSpec(memory_space=pl.ANY)
    shape = jax.ShapeDtypeStruct
    pairs = (places, buckets, 2, block, size)
    return pl.pallas_call(
        attend_kernel,
        name="attend",
        out_shape=(
            shape((rows, width), bf16),
            shape((rows, heads * size), f32),
            shape((rows, size), f32),
            shape((rows, heads), f32),
            shape((buckets, heads * block, size), bf16),
            shape(pairs, bf16),
            shape((rows, heads * size), f32),
            shape((buckets, heads * block, size), f32),
            shape((rows, heads * size), bf16),
        ),
        in_specs=[pl.BlockSpec(memory_space=pltpu.SMEM)] + [vmem] * 10,
        out_specs=(hbm, vmem, vmem, vmem, vmem, hbm, vmem, vmem, vmem),
        scratch_shapes=[
            pltpu.VMEM((rows, width), bf16),
            pltpu.VMEM(pairs, bf16),
            pltpu.VMEM((buckets, heads * block, 2 * size), f32),
            pltpu.SemaphoreType.DMA((2, 40)),
            pltpu.SemaphoreType.DMA((2,)),
        ],
        compiler_params=pltpu.CompilerParams(
            collective_id=call_id, has_side_effects=True, vmem_limit_bytes=VMEM_LIMIT
        ),
        cost_estimate=pl.CostEstimate(
            flops=4 * 2**30, bytes_accessed=16 * 2**20, transcendentals=2**22
        ),
    )(lengths, tokens, gain, w_query, w_key, w_value, w_gate, gain_q, gain_k, *tables)


def back_kernel(
    lengths_ref,
    grad_ref,
    w_out_ref,
    attended_ref,
    logits_ref,
    query_ref,
    lse_ref,
    query_raw_ref,
    key_raw_ref,
    gain_query_ref,
    gain_key_ref,
    inner_ref,
    outer_ref,
    kv_hbm,
    grad_query_out,
    grad_key_out,
    grad_value_out,
    grad_logits_out,
    gain_query_out,
    gain_key_out,
    kv,
    grads,
    recv,
    grad_attended,
    shift,
    delta,
    grad_turned,
    sems,
    in_sems,
):
    ready = greet_plane()
    load = pltpu.make_async_copy(kv_hbm, kv, in_sems.at[0])
    load.start()
    y, x = plane_place()
    place = y * 4 + x
    buckets = kv.shape[1]
    block, size = kv.shape[3], kv.shape[4]
    heads = w_out_ref.shape[0] // size
    grad_gated = lax.dot_general(
        grad_ref[...], w_out_ref[...], ROW_CONTRACT, preferred_element_type=f32
    )
    gates = jax.nn.sigmoid(logits_ref[...])
    for h in range(heads):
        cols = slice(h * size, (h + 1) * size)
        gate = gates[:, h : h + 1]
        part, attended = grad_gated[:, cols], attended_ref[:, cols]
        along = jnp.sum(part * attended, axis=1, keepdims=True)
        grad_logits_out[:, h : h + 1] = (along * gate * (1.0 - gate)).astype(bf16)
        low = (part * gate).astype(bf16)
        inner = jnp.sum(low.astype(f32) * attended, axis=1, keepdims=True)
        wide = jnp.broadcast_to(inner, (inner.shape[0], size))
        for b in range(buckets):
            rows = slice(b * block, (b + 1) * block)
            at = slice(h * block, (h + 1) * block)
            grad_attended[b, at, :] = low[rows]
            delta[b, :, at] = wide[rows].T[:8]
    for b in range(buckets):
        shift[b] = lse_ref[b].T[:8]
    grad_turned[...] = jnp.zeros_like(grad_turned)
    load.wait()
    ready()
    scale = size**-0.5

    def back(source, b, causal):
        keys, vals = kv[source, b, 0], kv[source, b, 1]
        query = query_ref[b]
        given = grad_attended[b]
        scores = lax.dot_general(keys, query, ROW_CONTRACT, preferred_element_type=f32)
        weights = jnp.exp2(scores * (scale * LOG2_E) - shift[b, 0:1, :])
        if causal:
            spot = lax.broadcasted_iota(jnp.int32, (block, heads * block), 1) % block
            key_spot = lax.broadcasted_iota(jnp.int32, (block, heads * block), 0)
            weights = jnp.where(key_spot <= spot, weights, 0.0)
        grad_weights = lax.dot_general(vals, given, ROW_CONTRACT, preferred_element_type=f32)
        grad_scores = (weights * (grad_weights - delta[b, 0:1, :])).astype(bf16)
        grad_keys = jnp.dot(grad_scores, query, preferred_element_type=f32) * scale
        grad_vals = jnp.dot(weights.astype(bf16), given, preferred_element_type=f32)
        grads[source, b, 0] = grad_keys.astype(bf16)
        grads[source, b, 1] = grad_vals.astype(bf16)
        grad_turned[b] += lax.dot_general(
            keys, grad_scores, COL_CONTRACT, preferred_element_type=f32
        )

    def visit(source, b):
        @pl.when(source < place)
        def _():
            back(source, b, False)

        @pl.when(source > place)
        def _():
            grads[source, b] = jnp.zeros_like(grads[source, b])

    scatter = Scatter(grads, recv, sems)
    order = (2, 1, 3, 0)
    for ring in order:
        for path in (0, 1):

            def one(n, carry):
                visit(place_at(path, ring, choose(n, [2, 1, 3])), path)
                return carry

            lax.fori_loop(0, 3, one, 0)
            scatter.start(path, ring)
        if ring != 2:
            previous = order[order.index(ring) - 1]
            for path in (0, 1):
                scatter.forward(path, previous)
    for path in (0, 1):

        def own(n, carry):
            visit(place_at(path, choose(n, [2, 1, 3]), 0), path)
            return carry

        lax.fori_loop(0, 3, own, 0)
    for path in (0, 1):
        scatter.forward(path, 0)
    for ring in (2, 1, 3):
        for path in (0, 1):
            scatter.settle(path, ring)
    for path in (0, 1):
        scatter.start(path, 4)
    for b in range(buckets):
        back(place, b, True)
    for path in (0, 1):
        scatter.settle(path, 0)
        scatter.forward(path, 4)
    cosine, sine = local_angles(inner_ref, outer_ref, place)

    def turn_back(values):
        return values * cosine - turned(values) * sine

    gain_sum = jnp.zeros((1, size), f32)
    for b in range(buckets):
        rows = slice(b * block, (b + 1) * block)
        grad_rot = grad_turned[b].T * scale
        for h in range(heads):
            cols = slice(h * size, (h + 1) * size)
            unit, inverse = unit_scale(query_raw_ref[rows, cols])
            straight = turn_back(grad_rot[h * block : (h + 1) * block])
            gain_sum += jnp.sum(straight * unit, axis=0, keepdims=True)
            grad_query_out[rows, cols] = norm_back(
                straight * gain_query_ref[...], unit, inverse
            ).astype(bf16)
    gain_query_out[...] = gain_sum
    gain_sum = jnp.zeros((1, size), f32)
    spots = place * block + lax.broadcasted_iota(jnp.int32, (block, size), 0)
    for b in range(buckets):
        rows = slice(b * block, (b + 1) * block)
        live = spots < lengths_ref[b]
        grad_keys, grad_vals = scatter.total(b, 4)
        grad_value_out[rows, :] = jnp.where(live, grad_vals, 0.0).astype(bf16)
        unit, inverse = unit_scale(key_raw_ref[rows, :])
        straight = turn_back(jnp.where(live, grad_keys, 0.0))
        gain_sum += jnp.sum(straight * unit, axis=0, keepdims=True)
        grad_key_out[rows, :] = norm_back(straight * gain_key_ref[...], unit, inverse).astype(bf16)
    gain_key_out[...] = gain_sum
    scatter.finish()


def attend_back(
    call_id, lengths, grad, w_out, attended, logits, query, lse, raws, gains, tables, kv
):
    rows = grad.shape[0]
    places, buckets, _, block, size = kv.shape
    heads = w_out.shape[0] // size
    vmem = pl.BlockSpec(memory_space=pltpu.VMEM)
    shape = jax.ShapeDtypeStruct
    return pl.pallas_call(
        back_kernel,
        name="attend_back",
        out_shape=(
            shape((rows, heads * size), bf16),
            shape((rows, size), bf16),
            shape((rows, size), bf16),
            shape((rows, heads), bf16),
            shape((1, size), f32),
            shape((1, size), f32),
        ),
        in_specs=[pl.BlockSpec(memory_space=pltpu.SMEM)]
        + [vmem] * 12
        + [pl.BlockSpec(memory_space=pl.ANY)],
        out_specs=(vmem,) * 6,
        scratch_shapes=[
            pltpu.VMEM(kv.shape, bf16),
            pltpu.VMEM(kv.shape, bf16),
            pltpu.VMEM((2, 5, 6, block, size), bf16),
            pltpu.VMEM((buckets, heads * block, size), bf16),
            pltpu.VMEM((buckets, 8, heads * block), f32),
            pltpu.VMEM((buckets, 8, heads * block), f32),
            pltpu.VMEM((buckets, size, heads * block), f32),
            pltpu.SemaphoreType.DMA((2, 60)),
            pltpu.SemaphoreType.DMA((1,)),
        ],
        compiler_params=pltpu.CompilerParams(
            collective_id=call_id, has_side_effects=True, vmem_limit_bytes=VMEM_LIMIT
        ),
        cost_estimate=pl.CostEstimate(
            flops=8 * 2**30, bytes_accessed=16 * 2**20, transcendentals=2**22
        ),
    )(lengths, grad, w_out, attended, logits, query, lse, *raws, *gains, *tables, kv)


def local(
    tokens,
    lengths,
    norm_attn,
    w_query,
    w_key,
    w_value,
    w_gate,
    norm_query,
    norm_key,
    w_out,
    norm_ffn,
    w_ffn_gate,
    w_ffn_up,
    w_down,
    cotangent,
):
    buckets, per_device, model_width = tokens.shape
    head_count = w_gate.shape[1]
    head_size = norm_query.shape[0]
    kv_count = w_key.shape[1] // head_size
    group_size = head_count // kv_count
    total_rows = buckets * per_device
    full_len = per_device * lax.axis_size(SEQ)
    positions = lax.axis_index(SEQ) * per_device + jnp.arange(per_device, dtype=jnp.int32)
    share_rows = total_rows // lax.axis_size(GRP)
    share_start = lax.axis_index(GRP) * share_rows

    def take_share(values):
        return lax.dynamic_slice_in_dim(values, share_start, share_rows, 0)

    flat = tokens.reshape(total_rows, model_width)
    tables = angle_tables(per_device, head_size, lax.axis_size(SEQ))
    gains_in = (norm_query.reshape(1, -1), norm_key.reshape(1, -1))
    normed, query_raw, key_raw, logits, query_low, pairs, attended, lse, gated = attend(
        5, lengths, flat, norm_attn.reshape(1, -1), w_query, w_key, w_value, w_gate, *gains_in, tables
    )
    base = take_share(flat)
    share = jax.ShapeDtypeStruct((share_rows, model_width), f32)
    scale = jax.ShapeDtypeStruct((share_rows, 1), f32)
    gain_row = jax.ShapeDtypeStruct((1, model_width), f32)
    middle, inverse_two, normed_two = exchange_rows(
        "attention_rows",
        1,
        (gated,),
        (w_out,),
        False,
        finish_middle,
        (base, norm_ffn.reshape(1, -1)),
        (share, scale),
    )
    live_rows = (positions[None, :] < lengths[:, None]).astype(f32)
    loss_ratio = buckets * full_len / jnp.sum(lengths).astype(f32)
    grad_out = (cotangent.astype(f32) * live_rows[:, :, None] * loss_ratio).reshape(
        total_rows, model_width
    )
    grad_out_low = grad_out.astype(bf16)
    hidden, grad_gate_pre, grad_up, grad_down, grad_ffn_gate, grad_ffn_up = feed_forward(
        normed_two, grad_out_low, w_ffn_gate, w_ffn_up, w_down
    )
    ffn_sums = lax.psum((grad_ffn_gate, grad_ffn_up, grad_down), SEQ)
    grad_middle, ffn_gain_part, grad_attn_low = exchange_rows(
        "feed_back_rows",
        2,
        (grad_gate_pre, grad_up),
        (w_ffn_gate, w_ffn_up),
        True,
        finish_grad_middle,
        (middle, inverse_two, norm_ffn.reshape(1, -1), take_share(grad_out)),
        (share, gain_row),
    )
    (mixed,) = exchange_rows(
        "mixed_rows", 3, (hidden,), (w_down,), False, finish_plain, (middle,), ()
    )
    mixed = mixed.reshape(buckets, per_device, model_width)
    grad_w_out = jnp.dot(gated.T, grad_attn_low, preferred_element_type=f32)
    grad_query_low, grad_key_low, grad_value_low, grad_logits, query_gain, key_gain = attend_back(
        6,
        lengths,
        grad_attn_low,
        w_out,
        attended,
        logits,
        query_low,
        lse,
        (query_raw, key_raw),
        gains_in,
        tables,
        pairs,
    )
    grad_w_query = jnp.dot(normed.T, grad_query_low, preferred_element_type=f32)
    grad_w_key = jnp.dot(normed.T, grad_key_low, preferred_element_type=f32)
    grad_w_value = jnp.dot(normed.T, grad_value_low, preferred_element_type=f32)
    grad_w_gate = jnp.dot(normed.T, grad_logits, preferred_element_type=f32)
    attn_gain_part, grad_tokens = exchange_rows(
        "token_rows",
        4,
        (grad_query_low, grad_key_low, grad_value_low, grad_logits),
        (w_query, w_key, w_value, w_gate),
        True,
        finish_grad_tokens,
        (base, norm_attn.reshape(1, -1), grad_middle),
        (gain_row,),
    )
    grad_tokens = grad_tokens.reshape(buckets, per_device, model_width)
    gains = jnp.concatenate(
        (ffn_gain_part[0], attn_gain_part[0], query_gain[0], key_gain[0])
    )
    grad_norm_ffn, grad_norm_attn, grad_norm_query, grad_norm_key = jnp.split(
        lax.psum(gains, SEQ_GRP),
        (model_width, 2 * model_width, 2 * model_width + head_size),
    )
    attn_parts = tuple(
        part.astype(bf16)
        for part in (grad_w_query, grad_w_key, grad_w_value, grad_w_gate, grad_w_out)
    )
    attn_parts, ffn_sums = lax.optimization_barrier((attn_parts, ffn_sums))
    attn_sums = tuple(part.astype(f32) for part in lax.psum(attn_parts, SEQ))
    ffn_sums = tuple(part.astype(f32) for part in ffn_sums)
    return (
        mixed,
        grad_tokens,
        grad_norm_attn,
        attn_sums[0],
        attn_sums[1],
        attn_sums[2],
        attn_sums[3],
        grad_norm_query,
        grad_norm_key,
        attn_sums[4],
        grad_norm_ffn,
        ffn_sums[0],
        ffn_sums[1],
        ffn_sums[2],
    )


def solution(mesh):
    finer = Mesh(mesh.devices.reshape(4, 4, 4, 2), ("seq_0", "seq_1", "grp_0", "grp_1"))
    return jax.shard_map(
        local,
        mesh=finer,
        in_specs=(
            P(None, SEQ, None),
            P(),
            P(),
            P(None, GRP),
            P(None, GRP),
            P(None, GRP),
            P(None, GRP),
            P(),
            P(),
            P(GRP, None),
            P(),
            P(None, GRP),
            P(None, GRP),
            P(GRP, None),
            P(None, SEQ, None),
        ),
        out_specs=(
            P(None, SEQ, None),
            P(None, SEQ, None),
            P(),
            P(None, GRP),
            P(None, GRP),
            P(None, GRP),
            P(None, GRP),
            P(),
            P(),
            P(GRP, None),
            P(),
            P(None, GRP),
            P(None, GRP),
            P(GRP, None),
        ),
        check_vma=False,
    )
```

```python
import functools

import jax
import jax.numpy as jnp
import numpy as np
from jax import lax
from jax.experimental import pallas as pl
from jax.experimental.pallas import tpu as pltpu
from jax.sharding import Mesh
from jax.sharding import PartitionSpec as P

GRP = ("grp_0", "grp_1")
SEQ = ("seq_0", "seq_1")
MESH = pl.DeviceIdType.MESH
VMEM_LIMIT = 56 * 2**20

f32 = jnp.float32
bf16 = jnp.bfloat16


epsilon = 1e-06
rope_base = 1000000.0


def unit_scale(values):
    inverse = lax.rsqrt(jnp.mean(values * values, axis=-1, keepdims=True) + epsilon)
    return (values * inverse, inverse)


def norm_back(grad_unit, unit, inverse):
    return inverse * (grad_unit - unit * jnp.mean(grad_unit * unit, axis=-1, keepdims=True))


ROW_CONTRACT = (((1,), (1,)), ((), ()))
COL_CONTRACT = (((0,), (0,)), ((), ()))


def send(source, target, sems, slot, to):
    copy = pltpu.make_async_remote_copy(
        src_ref=source,
        dst_ref=target,
        send_sem=sems.at[0, slot],
        recv_sem=sems.at[1, slot],
        device_id=to,
        device_id_type=MESH,
    )
    copy.start()
    return copy


def group_places():
    z = lax.axis_index("grp_0")
    core = lax.axis_index("grp_1")
    ring = lax.axis_size("grp_0")
    above = {"grp_0": lax.rem(z + 1, ring)}
    below = {"grp_0": lax.rem(z + ring - 1, ring)}
    twin = {"grp_1": 1 - core}
    return z, core, above, below, twin


def greet(places):
    barrier = pltpu.get_barrier_semaphore()
    for place in places:
        pl.semaphore_signal(barrier, inc=1, device_id=place, device_id_type=MESH)
    return lambda: pl.semaphore_wait(barrier, len(places))


def group_rows(z, core, far, share):
    return pl.multiple_of((lax.rem(z + far, 4) * 2 + core) * share, share)


FAR = (2, 1, 3, 0)


def run_together(tasks):
    tasks = list(tasks)
    while tasks:
        for task in list(tasks):
            try:
                next(task)
            except StopIteration:
                tasks.remove(task)


def sum_rows(product, share, ready, scratch):
    mine, twin_out, twin_in, low, ring, twin_sems, ring_sems = scratch
    z, core, above, below, twin = group_places()
    half = share // 2
    top, bottom = pl.ds(0, half), pl.ds(half, half)

    def put_twin(cols, block):
        twin_out[:, :, cols] = block.astype(bf16)

    def put_mine(cols, block):
        mine[:, :, cols] = block

    product(1 - core, put_twin)
    ready()
    pairs = [send(twin_out.at[k], twin_in.at[k], twin_sems, k, twin) for k in range(4)]
    product(core, put_mine)

    def joined(k, rows):
        return mine[k, rows, :] + twin_in[k, rows, :].astype(f32)

    yield
    pairs[0].wait_recv()
    low[0] = joined(0, pl.ds(0, share)).astype(bf16)
    steps = [
        send(low.at[0, top], ring.at[0], ring_sems, 0, above),
        send(low.at[0, bottom], ring.at[1], ring_sems, 1, below),
    ]
    pairs[1].wait_recv()
    low[1, bottom, :] = joined(1, bottom).astype(bf16)
    steps.append(send(low.at[1, bottom], ring.at[2], ring_sems, 2, above))
    pairs[2].wait_recv()
    low[2, top, :] = joined(2, top).astype(bf16)
    steps.append(send(low.at[2, top], ring.at[3], ring_sems, 3, below))
    yield
    steps[0].wait_recv()
    low[1, top, :] = (joined(1, top) + ring[0].astype(f32)).astype(bf16)
    steps.append(send(low.at[1, top], ring.at[4], ring_sems, 4, above))
    yield
    steps[1].wait_recv()
    low[2, bottom, :] = (joined(2, bottom) + ring[1].astype(f32)).astype(bf16)
    steps.append(send(low.at[2, bottom], ring.at[5], ring_sems, 5, below))
    pairs[3].wait_recv()
    yield
    for step in steps[2:]:
        step.wait_recv()
    total = jnp.concatenate(
        [
            joined(3, top) + ring[3].astype(f32) + ring[4].astype(f32),
            joined(3, bottom) + ring[2].astype(f32) + ring[5].astype(f32),
        ],
        axis=0,
    )
    return total, pairs + steps


def join_rows(whole, share, twin_sems, ring_sems):
    z, core, above, below, twin = group_places()
    half = share // 2

    def part(far, side):
        start = group_rows(z, core, far, share)
        return whole.at[pl.ds(pl.multiple_of(start + side * half, half), half), :]

    def hand(far, side, sems, slot, to):
        block = part(far, side)
        return send(block, block, sems, slot, to)

    own = whole.at[pl.ds(group_rows(z, core, 0, share), share), :]
    up = [hand(0, 0, ring_sems, 0, above), hand(0, 1, ring_sems, 1, above)]
    down = [hand(0, 1, ring_sems, 2, below), hand(0, 0, ring_sems, 3, below)]
    across = [send(own, own, twin_sems, 0, twin)]
    yield
    up[0].wait_recv()
    up.append(hand(3, 0, ring_sems, 4, above))
    across.append(hand(3, 0, twin_sems, 1, twin))
    yield
    down[0].wait_recv()
    down.append(hand(1, 1, ring_sems, 5, below))
    across.append(hand(1, 1, twin_sems, 2, twin))
    yield
    up[1].wait_recv()
    across.append(hand(3, 1, twin_sems, 3, twin))
    down[1].wait_recv()
    across.append(hand(1, 0, twin_sems, 4, twin))
    yield
    up[2].wait_recv()
    across.append(hand(2, 0, twin_sems, 5, twin))
    down[2].wait_recv()
    across.append(hand(2, 1, twin_sems, 6, twin))
    yield
    for copy in across:
        copy.wait_recv()
    for copy in up + down + across:
        copy.wait_send()


def row_scratch(rows, share, width):
    return [
        pltpu.VMEM((4, share, width), f32),
        pltpu.VMEM((4, share, width), bf16),
        pltpu.VMEM((4, share, width), bf16),
        pltpu.VMEM((3, share, width), bf16),
        pltpu.VMEM((6, share // 2, width), bf16),
        pltpu.SemaphoreType.DMA((2, 4)),
        pltpu.SemaphoreType.DMA((2, 6)),
        pltpu.VMEM((rows, width), bf16),
        pltpu.SemaphoreType.DMA((2, 7)),
        pltpu.SemaphoreType.DMA((2, 6)),
        pltpu.SemaphoreType.DMA((1,)),
    ]


def group_product(lefts, rights, across, share, width):
    z = lax.axis_index("grp_0")
    step = 512

    def product(core, put):
        picked = []
        for left in lefts:
            blocks = [left[pl.ds(group_rows(z, core, far, share), share), :] for far in FAR]
            picked.append(jnp.concatenate(blocks, axis=0))
        for at in range(0, width, step):
            cols = pl.ds(at, step)
            total = None
            for left, right in zip(picked, rights):
                if across:
                    term = lax.dot_general(
                        left, right[cols, :], ROW_CONTRACT, preferred_element_type=f32
                    )
                else:
                    term = jnp.dot(left, right[:, cols], preferred_element_type=f32)
                total = term if total is None else total + term
            put(cols, total.reshape(4, share, step))

    return product


def row_kernel(n_pairs, across, finish, n_extra, n_out, share, width, *refs):
    lefts = refs[:n_pairs]
    rights = refs[n_pairs : 2 * n_pairs]
    extra = refs[2 * n_pairs : 2 * n_pairs + n_extra]
    at = 2 * n_pairs + n_extra
    outs = refs[at : at + n_out]
    whole_out = refs[at + n_out]
    scratch = refs[at + n_out + 1 :]
    z, core, above, below, twin = group_places()
    ready = greet((above, below, twin))
    product = group_product(lefts, rights, across, share, width)
    whole, twin_sems, ring_sems, out_sem = scratch[7:]

    def task():
        total, copies = yield from sum_rows(product, share, ready, scratch[:7])
        whole[pl.ds(group_rows(z, core, 0, share), share), :] = finish(total, extra, outs)
        yield from join_rows(whole, share, twin_sems, ring_sems)
        for copy in copies:
            copy.wait_send()

    run_together([task()])
    done = pltpu.make_async_copy(whole, whole_out, out_sem.at[0])
    done.start()
    done.wait()


def exchange_rows(name, call_id, lefts, rights, across, finish, extra, out_shapes):
    rows = lefts[0].shape[0]
    share = rows // 8
    width = rights[0].shape[0 if across else 1]
    vmem = pl.BlockSpec(memory_space=pltpu.VMEM)
    body = functools.partial(
        row_kernel, len(lefts), across, finish, len(extra), len(out_shapes), share, width
    )
    flops = 2 * rows * width * sum(left.shape[1] for left in lefts)
    return pl.pallas_call(
        body,
        name=name,
        out_shape=tuple(out_shapes) + (jax.ShapeDtypeStruct((rows, width), bf16),),
        in_specs=[vmem] * (2 * len(lefts) + len(extra)),
        out_specs=(vmem,) * len(out_shapes) + (pl.BlockSpec(memory_space=pl.ANY),),
        scratch_shapes=row_scratch(rows, share, width),
        compiler_params=pltpu.CompilerParams(
            collective_id=call_id, has_side_effects=True, vmem_limit_bytes=VMEM_LIMIT
        ),
        cost_estimate=pl.CostEstimate(
            flops=flops, bytes_accessed=16 * 2**20, transcendentals=0
        ),
    )(*lefts, *rights, *extra)


def finish_middle(total, extra, outs):
    base, gain = extra
    middle_out, scale_out = outs
    middle = base[...].astype(f32) + total
    unit, inverse = unit_scale(middle)
    middle_out[...] = middle
    scale_out[...] = inverse
    return (unit * gain[...]).astype(bf16)


def finish_grad_middle(total, extra, outs):
    middle, inverse, gain, seed = extra
    grad_out, gain_out = outs
    unit = middle[...] * inverse[...]
    gain_out[...] = jnp.sum(total * unit, axis=0, keepdims=True)
    grad = seed[...] + norm_back(total * gain[...], unit, inverse[...])
    grad_out[...] = grad
    return grad.astype(bf16)


def feed_kernel(
    rows_ref,
    seed_ref,
    gate_ref,
    up_ref,
    down_ref,
    hidden_out,
    grad_gate_out,
    grad_up_out,
    w_down_out,
    w_gate_out,
    w_up_out,
    rows_across,
):
    @pl.when(pl.program_id(0) == 0)
    def _():
        rows_across[...] = rows_ref[...].T

    rows = rows_ref[...]
    seed = seed_ref[...]
    gate_pre = jnp.dot(rows, gate_ref[...], preferred_element_type=f32)
    up_proj = jnp.dot(rows, up_ref[...], preferred_element_type=f32)
    grad_hidden = lax.dot_general(seed, down_ref[...], ROW_CONTRACT, preferred_element_type=f32)
    gate_sig = jax.nn.sigmoid(gate_pre)
    silu = gate_pre * gate_sig
    hidden = (silu * up_proj).astype(bf16)
    grad_gate = (grad_hidden * up_proj * gate_sig * (1.0 + gate_pre * (1.0 - gate_sig))).astype(
        bf16
    )
    grad_up = (grad_hidden * silu).astype(bf16)
    hidden_out[...] = hidden
    grad_gate_out[...] = grad_gate
    grad_up_out[...] = grad_up
    w_down_out[...] = lax.dot_general(
        hidden, seed, COL_CONTRACT, preferred_element_type=f32
    ).astype(bf16)
    w_gate_out[...] = jnp.dot(rows_across[...], grad_gate, preferred_element_type=f32).astype(bf16)
    w_up_out[...] = jnp.dot(rows_across[...], grad_up, preferred_element_type=f32).astype(bf16)


def feed_forward(rows, seed, w_gate, w_up, w_down):
    count, width = rows.shape
    units = w_gate.shape[1]
    step = 256
    whole = pl.BlockSpec((count, width), lambda j: (0, 0))
    cols = pl.BlockSpec((width, step), lambda j: (0, j))
    strip = pl.BlockSpec((step, width), lambda j: (j, 0))
    narrow = pl.BlockSpec((count, step), lambda j: (0, j))
    thin = jax.ShapeDtypeStruct((count, units), bf16)
    return pl.pallas_call(
        feed_kernel,
        name="feed_forward",
        grid=(units // step,),
        in_specs=[whole, whole, cols, cols, strip],
        out_specs=(narrow, narrow, narrow, strip, cols, cols),
        out_shape=(
            thin,
            thin,
            thin,
            jax.ShapeDtypeStruct((units, width), bf16),
            jax.ShapeDtypeStruct((width, units), bf16),
            jax.ShapeDtypeStruct((width, units), bf16),
        ),
        scratch_shapes=[pltpu.VMEM((width, count), bf16)],
        compiler_params=pltpu.CompilerParams(vmem_limit_bytes=VMEM_LIMIT),
        cost_estimate=pl.CostEstimate(
            flops=12 * count * width * units, bytes_accessed=24 * 2**20, transcendentals=0
        ),
    )(rows, seed, w_gate, w_up, w_down)


LOG2_E = 1.4426950408889634
STAGES = (
    ((1, 0), (3, 0), (0, 1), (0, 3)),
    ((2, 0), (0, 2)),
    ((1, 1), (1, 3), (3, 1), (3, 3)),
    ((1, 2), (3, 2), (2, 1), (2, 3)),
    ((2, 2),),
)


def angle_tables(block, size, count):
    half = size // 2
    freq = rope_base ** (-np.arange(half, dtype=np.float64) * (2.0 / size))
    inner = np.arange(block)[:, None] * freq[None, :]
    outer = (np.arange(count) * block)[:, None] * freq[None, :]

    def table(angle):
        sine = np.sin(angle)
        cosine = np.cos(angle)
        both = np.stack(
            [
                np.concatenate([cosine, cosine], axis=1),
                np.concatenate([-sine, sine], axis=1),
            ]
        )
        return both.astype(np.float32)

    return table(inner), table(outer)


def local_angles(inner, outer, place):
    cos_in, sin_in = inner[0], inner[1]
    cos_out = outer[0, pl.ds(place, 1), :]
    sin_out = outer[1, pl.ds(place, 1), :]
    return cos_in * cos_out - sin_in * sin_out, sin_in * cos_out + cos_in * sin_out


def turned(values):
    return pltpu.roll(values, values.shape[-1] // 2, axis=values.ndim - 1)


def plane_place():
    return lax.axis_index("seq_0"), lax.axis_index("seq_1")


def plane_sides(axis):
    at = lax.axis_index(axis)
    size = lax.axis_size(axis)
    return {axis: lax.rem(at + 1, size)}, {axis: lax.rem(at + size - 1, size)}


AXES = (("seq_1", "seq_0"), ("seq_0", "seq_1"))


def place_at(path, first, second):
    y, x = plane_place()
    dx, dy = (first, second) if path == 0 else (second, first)
    return lax.rem(y + dy, 4) * 4 + lax.rem(x + dx, 4)


def pass_start(block, axis, sems, slot):
    up, down = plane_sides(axis)
    return [send(block, block, sems, slot, up), send(block, block, sems, slot + 1, down)]


def pass_on(copies, before, after, axis, sems, slot):
    up, down = plane_sides(axis)
    copies[0].wait_recv()
    copies.append(send(before.at[0], before.at[0], sems, slot + 2, up))
    copies[1].wait_recv()
    copies.append(send(after.at[1], after.at[1], sems, slot + 3, down))


def pass_end(copies):
    copies[2].wait_recv()
    copies[3].wait_recv()


class Gather:
    def __init__(self, buffer, sems):
        self.buffer, self.sems = buffer, sems
        self.rings = [{}, {}]

    def block(self, path, first, second):
        return self.buffer.at[place_at(path, first, second), path]

    def slot(self, path, ring):
        return path * 20 + (4 if ring == "first" else ring) * 4

    def begin(self, path, ring):
        axis = AXES[path][0] if ring == "first" else AXES[path][1]
        block = self.block(path, 0 if ring == "first" else ring, 0)
        self.rings[path][ring] = pass_start(block, axis, self.sems, self.slot(path, ring))

    def forward(self, path, ring):
        if ring == "first":
            axis, before, after = AXES[path][0], self.block(path, 3, 0), self.block(path, 1, 0)
        else:
            axis = AXES[path][1]
            before, after = self.block(path, ring, 3), self.block(path, ring, 1)
        pass_on(self.rings[path][ring], before, after, axis, self.sems, self.slot(path, ring))

    def end(self, path, ring):
        pass_end(self.rings[path][ring])

    def start(self):
        for path in (0, 1):
            self.begin(path, "first")
        for path in (0, 1):
            self.begin(path, 0)

    def stage_task(self, number):
        for path in (0, 1):
            yield
            if number == 0:
                self.forward(path, "first")
                self.begin(path, 1)
                self.begin(path, 3)
                self.forward(path, 0)
            elif number == 1:
                self.end(path, "first")
                self.begin(path, 2)
                self.end(path, 0)
            elif number == 2:
                self.forward(path, 1)
                self.forward(path, 3)
            elif number == 3:
                self.end(path, 1)
                self.end(path, 3)
                self.forward(path, 2)
            else:
                self.end(path, 2)

    def finish(self):
        for rings in self.rings:
            for copies in rings.values():
                for copy in copies:
                    copy.wait_send()


class Scatter:
    def __init__(self, buffer, recv, sems):
        self.buffer, self.recv, self.sems = buffer, recv, sems
        self.copies = {}

    def block(self, path, ring, step):
        if ring == 4:
            return self.buffer.at[place_at(path, step, 0), path]
        return self.buffer.at[place_at(path, ring, step), path]

    def sides(self, path, ring):
        return plane_sides(AXES[path][0] if ring == 4 else AXES[path][1])

    def push(self, path, ring, half_ref, slot, to):
        at = (path * 5 + ring) * 6 + slot
        copy = send(half_ref, self.recv.at[path, ring, slot], self.sems, at, to)
        self.copies.setdefault((path, ring), []).append(copy)

    def start(self, path, ring):
        up, down = self.sides(path, ring)
        far = self.block(path, ring, 2)
        self.push(path, ring, far.at[0], 0, up)
        self.push(path, ring, far.at[1], 1, down)
        self.push(path, ring, self.block(path, ring, 1).at[1], 2, up)
        self.push(path, ring, self.block(path, ring, 3).at[0], 3, down)

    def forward(self, path, ring):
        up, down = self.sides(path, ring)
        for slot, step, half, to in ((0, 1, 0, up), (1, 3, 1, down)):
            self.copies[path, ring][slot].wait_recv()
            part = self.block(path, ring, step).at[half]
            came = self.recv[path, ring, slot]
            part[...] = (part[...].astype(f32) + came.astype(f32)).astype(bf16)
            self.push(path, ring, part, slot + 4, to)

    def total(self, path, ring):
        for copy in self.copies[path, ring][2:]:
            copy.wait_recv()
        own = self.block(path, ring, 0)
        out = []
        for half, slots in ((0, (3, 4)), (1, (2, 5))):
            value = own[half].astype(f32)
            for slot in slots:
                value = value + self.recv[path, ring, slot].astype(f32)
            out.append(value)
        return out

    def settle(self, path, ring):
        own = self.block(path, ring, 0)
        for half, value in enumerate(self.total(path, ring)):
            own[half] = value.astype(bf16)

    def finish(self):
        for copies in self.copies.values():
            for copy in copies:
                copy.wait_send()


def greet_plane():
    places = [*plane_sides("seq_0"), *plane_sides("seq_1")]
    return greet(places)


def choose(index, options):
    value = options[-1]
    for n in range(len(options) - 2, -1, -1):
        value = jnp.where(index == n, options[n], value)
    return value


def attend_kernel(
    lengths_ref,
    tokens_ref,
    gain_ref,
    w_query_ref,
    w_key_ref,
    w_value_ref,
    w_gate_ref,
    gain_query_ref,
    gain_key_ref,
    inner_ref,
    outer_ref,
    normed_out,
    query_raw_out,
    key_raw_out,
    logits_out,
    query_out,
    keys_out,
    attended_out,
    lse_out,
    gated_out,
    normed,
    kv,
    sums,
    sems,
    out_sems,
):
    ready = greet_plane()
    y, x = plane_place()
    place = y * 4 + x
    rows, width = tokens_ref.shape
    buckets = kv.shape[1]
    block, size = kv.shape[3], kv.shape[4]
    heads = w_query_ref.shape[1] // size
    step = 64

    def norm_rows(n, carry):
        at = pl.ds(pl.multiple_of(n * step, step), step)
        unit, _ = unit_scale(tokens_ref[at, :].astype(f32))
        normed[at, :] = (unit * gain_ref[...]).astype(bf16)
        return carry

    lax.fori_loop(0, rows // step, norm_rows, 0)
    save_normed = pltpu.make_async_copy(normed, normed_out, out_sems.at[0])
    save_normed.start()
    cosine, sine = local_angles(inner_ref, outer_ref, place)

    def turn(values):
        return values * cosine + turned(values) * sine

    key_raw = jnp.dot(normed[...], w_key_ref[...], preferred_element_type=f32)
    value = jnp.dot(normed[...], w_value_ref[...], preferred_element_type=f32)
    key_raw_out[...] = key_raw
    spots = place * block + lax.broadcasted_iota(jnp.int32, (block, size), 0)
    for b in range(buckets):
        live = spots < lengths_ref[b]
        part = slice(b * block, (b + 1) * block)
        unit, _ = unit_scale(key_raw[part])
        kv[place, b, 0] = jnp.where(live, turn(unit * gain_key_ref[...]), 0.0).astype(bf16)
        kv[place, b, 1] = jnp.where(live, value[part], 0.0).astype(bf16)
    gather = Gather(kv, sems)
    ready()
    gather.start()
    query_raw = jnp.dot(normed[...], w_query_ref[...], preferred_element_type=f32)
    query_raw_out[...] = query_raw
    logits_out[...] = jnp.dot(normed[...], w_gate_ref[...], preferred_element_type=f32)
    for b in range(buckets):
        for h in range(heads):
            part = query_raw[b * block : (b + 1) * block, h * size : (h + 1) * size]
            unit, _ = unit_scale(part)
            query_out[b, h * block : (h + 1) * block, :] = turn(
                unit * gain_query_ref[...]
            ).astype(bf16)
    scale = size**-0.5 * LOG2_E

    def weigh(source, b, causal):
        keys, vals = kv[source, b, 0], kv[source, b, 1]
        scores = lax.dot_general(query_out[b], keys, ROW_CONTRACT, preferred_element_type=f32)
        weights = jnp.exp2(scores * scale)
        if causal:
            spot = lax.broadcasted_iota(jnp.int32, (heads * block, block), 0) % block
            column = lax.broadcasted_iota(jnp.int32, (heads * block, block), 1)
            weights = jnp.where(column <= spot, weights, 0.0)
        there = source * block + lax.broadcasted_iota(jnp.int32, (block, size), 0)
        ones = jnp.where(there < lengths_ref[b], 1.0, 0.0).astype(bf16)
        both = jnp.concatenate([vals, ones], axis=1)
        return jnp.dot(weights.astype(bf16), both, preferred_element_type=f32)

    for b in range(buckets):
        sums[b] = weigh(place, b, True)
    for number, offsets in enumerate(STAGES):
        run_together([gather.stage_task(number)])

        def one(n, carry):
            which, b = n // buckets, n % buckets
            dx = choose(which, [o[0] for o in offsets])
            dy = choose(which, [o[1] for o in offsets])
            source = lax.rem(y + dy, 4) * 4 + lax.rem(x + dx, 4)

            @pl.when(source < place)
            def _():
                sums[b] = sums[b] + weigh(source, b, False)

            return carry

        lax.fori_loop(0, len(offsets) * buckets, one, 0)
    save_keys = pltpu.make_async_copy(kv, keys_out, out_sems.at[1])
    save_keys.start()
    gates = jax.nn.sigmoid(logits_out[...])
    for b in range(buckets):
        for h in range(heads):
            at = slice(h * block, (h + 1) * block)
            total = sums[b, at, size:]
            attended = sums[b, at, :size] / total
            here = (slice(b * block, (b + 1) * block), slice(h * size, (h + 1) * size))
            attended_out[here] = attended
            lse_out[b, at, :] = jnp.log2(total)
            gated_out[here] = (attended * gates[here[0], h : h + 1]).astype(bf16)
    gather.finish()
    save_normed.wait()
    save_keys.wait()


def attend(call_id, lengths, tokens, gain, w_query, w_key, w_value, w_gate, gain_q, gain_k, tables):
    rows, width = tokens.shape
    size = gain_q.shape[1]
    buckets = lengths.shape[0]
    block = rows // buckets
    heads = w_query.shape[1] // size
    places = lax.axis_size(SEQ)
    vmem = pl.BlockSpec(memory_space=pltpu.VMEM)
    hbm = pl.BlockSpec(memory_space=pl.ANY)
    shape = jax.ShapeDtypeStruct
    pairs = (places, buckets, 2, block, size)
    return pl.pallas_call(
        attend_kernel,
        name="attend",
        out_shape=(
            shape((rows, width), bf16),
            shape((rows, heads * size), f32),
            shape((rows, size), f32),
            shape((rows, heads), f32),
            shape((buckets, heads * block, size), bf16),
            shape(pairs, bf16),
            shape((rows, heads * size), f32),
            shape((buckets, heads * block, size), f32),
            shape((rows, heads * size), bf16),
        ),
        in_specs=[pl.BlockSpec(memory_space=pltpu.SMEM)] + [vmem] * 10,
        out_specs=(hbm, vmem, vmem, vmem, vmem, hbm, vmem, vmem, vmem),
        scratch_shapes=[
            pltpu.VMEM((rows, width), bf16),
            pltpu.VMEM(pairs, bf16),
            pltpu.VMEM((buckets, heads * block, 2 * size), f32),
            pltpu.SemaphoreType.DMA((2, 40)),
            pltpu.SemaphoreType.DMA((2,)),
        ],
        compiler_params=pltpu.CompilerParams(
            collective_id=call_id, has_side_effects=True, vmem_limit_bytes=VMEM_LIMIT
        ),
        cost_estimate=pl.CostEstimate(
            flops=4 * 2**30, bytes_accessed=16 * 2**20, transcendentals=2**22
        ),
    )(lengths, tokens, gain, w_query, w_key, w_value, w_gate, gain_q, gain_k, *tables)


def back_kernel(
    lengths_ref,
    grad_ref,
    w_out_ref,
    attended_ref,
    logits_ref,
    query_ref,
    lse_ref,
    query_raw_ref,
    key_raw_ref,
    gain_query_ref,
    gain_key_ref,
    inner_ref,
    outer_ref,
    kv_hbm,
    grad_query_out,
    grad_key_out,
    grad_value_out,
    grad_logits_out,
    gain_query_out,
    gain_key_out,
    kv,
    grads,
    recv,
    grad_attended,
    shift,
    delta,
    grad_turned,
    sems,
    in_sems,
):
    ready = greet_plane()
    load = pltpu.make_async_copy(kv_hbm, kv, in_sems.at[0])
    load.start()
    y, x = plane_place()
    place = y * 4 + x
    buckets = kv.shape[1]
    block, size = kv.shape[3], kv.shape[4]
    heads = w_out_ref.shape[0] // size
    grad_gated = lax.dot_general(
        grad_ref[...], w_out_ref[...], ROW_CONTRACT, preferred_element_type=f32
    )
    gates = jax.nn.sigmoid(logits_ref[...])
    for h in range(heads):
        cols = slice(h * size, (h + 1) * size)
        gate = gates[:, h : h + 1]
        part, attended = grad_gated[:, cols], attended_ref[:, cols]
        along = jnp.sum(part * attended, axis=1, keepdims=True)
        grad_logits_out[:, h : h + 1] = (along * gate * (1.0 - gate)).astype(bf16)
        low = (part * gate).astype(bf16)
        inner = jnp.sum(low.astype(f32) * attended, axis=1, keepdims=True)
        wide = jnp.broadcast_to(inner, (inner.shape[0], size))
        for b in range(buckets):
            rows = slice(b * block, (b + 1) * block)
            at = slice(h * block, (h + 1) * block)
            grad_attended[b, at, :] = low[rows]
            delta[b, :, at] = wide[rows].T[:8]
    for b in range(buckets):
        shift[b] = lse_ref[b].T[:8]
    grad_turned[...] = jnp.zeros_like(grad_turned)
    load.wait()
    ready()
    scale = size**-0.5

    def back(source, b, causal):
        keys, vals = kv[source, b, 0], kv[source, b, 1]
        query = query_ref[b]
        given = grad_attended[b]
        scores = lax.dot_general(keys, query, ROW_CONTRACT, preferred_element_type=f32)
        weights = jnp.exp2(scores * (scale * LOG2_E) - shift[b, 0:1, :])
        if causal:
            spot = lax.broadcasted_iota(jnp.int32, (block, heads * block), 1) % block
            key_spot = lax.broadcasted_iota(jnp.int32, (block, heads * block), 0)
            weights = jnp.where(key_spot <= spot, weights, 0.0)
        grad_weights = lax.dot_general(vals, given, ROW_CONTRACT, preferred_element_type=f32)
        grad_scores = (weights * (grad_weights - delta[b, 0:1, :])).astype(bf16)
        grad_keys = jnp.dot(grad_scores, query, preferred_element_type=f32) * scale
        grad_vals = jnp.dot(weights.astype(bf16), given, preferred_element_type=f32)
        grads[source, b, 0] = grad_keys.astype(bf16)
        grads[source, b, 1] = grad_vals.astype(bf16)
        grad_turned[b] += lax.dot_general(
            keys, grad_scores, COL_CONTRACT, preferred_element_type=f32
        )

    def visit(source, b):
        @pl.when(source < place)
        def _():
            back(source, b, False)

        @pl.when(source > place)
        def _():
            grads[source, b] = jnp.zeros_like(grads[source, b])

    scatter = Scatter(grads, recv, sems)
    order = (2, 1, 3, 0)
    for ring in order:
        for path in (0, 1):

            def one(n, carry):
                visit(place_at(path, ring, choose(n, [2, 1, 3])), path)
                return carry

            lax.fori_loop(0, 3, one, 0)
            scatter.start(path, ring)
        if ring != 2:
            previous = order[order.index(ring) - 1]
            for path in (0, 1):
                scatter.forward(path, previous)
    for path in (0, 1):

        def own(n, carry):
            visit(place_at(path, choose(n, [2, 1, 3]), 0), path)
            return carry

        lax.fori_loop(0, 3, own, 0)
    for path in (0, 1):
        scatter.forward(path, 0)
    for ring in (2, 1, 3):
        for path in (0, 1):
            scatter.settle(path, ring)
    for path in (0, 1):
        scatter.start(path, 4)
    for b in range(buckets):
        back(place, b, True)
    for path in (0, 1):
        scatter.settle(path, 0)
        scatter.forward(path, 4)
    cosine, sine = local_angles(inner_ref, outer_ref, place)

    def turn_back(values):
        return values * cosine - turned(values) * sine

    gain_sum = jnp.zeros((1, size), f32)
    for b in range(buckets):
        rows = slice(b * block, (b + 1) * block)
        grad_rot = grad_turned[b].T * scale
        for h in range(heads):
            cols = slice(h * size, (h + 1) * size)
            unit, inverse = unit_scale(query_raw_ref[rows, cols])
            straight = turn_back(grad_rot[h * block : (h + 1) * block])
            gain_sum += jnp.sum(straight * unit, axis=0, keepdims=True)
            grad_query_out[rows, cols] = norm_back(
                straight * gain_query_ref[...], unit, inverse
            ).astype(bf16)
    gain_query_out[...] = gain_sum
    gain_sum = jnp.zeros((1, size), f32)
    spots = place * block + lax.broadcasted_iota(jnp.int32, (block, size), 0)
    for b in range(buckets):
        rows = slice(b * block, (b + 1) * block)
        live = spots < lengths_ref[b]
        grad_keys, grad_vals = scatter.total(b, 4)
        grad_value_out[rows, :] = jnp.where(live, grad_vals, 0.0).astype(bf16)
        unit, inverse = unit_scale(key_raw_ref[rows, :])
        straight = turn_back(jnp.where(live, grad_keys, 0.0))
        gain_sum += jnp.sum(straight * unit, axis=0, keepdims=True)
        grad_key_out[rows, :] = norm_back(straight * gain_key_ref[...], unit, inverse).astype(bf16)
    gain_key_out[...] = gain_sum
    scatter.finish()


def attend_back(
    call_id, lengths, grad, w_out, attended, logits, query, lse, raws, gains, tables, kv
):
    rows = grad.shape[0]
    places, buckets, _, block, size = kv.shape
    heads = w_out.shape[0] // size
    vmem = pl.BlockSpec(memory_space=pltpu.VMEM)
    shape = jax.ShapeDtypeStruct
    return pl.pallas_call(
        back_kernel,
        name="attend_back",
        out_shape=(
            shape((rows, heads * size), bf16),
            shape((rows, size), bf16),
            shape((rows, size), bf16),
            shape((rows, heads), bf16),
            shape((1, size), f32),
            shape((1, size), f32),
        ),
        in_specs=[pl.BlockSpec(memory_space=pltpu.SMEM)]
        + [vmem] * 12
        + [pl.BlockSpec(memory_space=pl.ANY)],
        out_specs=(vmem,) * 6,
        scratch_shapes=[
            pltpu.VMEM(kv.shape, bf16),
            pltpu.VMEM(kv.shape, bf16),
            pltpu.VMEM((2, 5, 6, block, size), bf16),
            pltpu.VMEM((buckets, heads * block, size), bf16),
            pltpu.VMEM((buckets, 8, heads * block), f32),
            pltpu.VMEM((buckets, 8, heads * block), f32),
            pltpu.VMEM((buckets, size, heads * block), f32),
            pltpu.SemaphoreType.DMA((2, 60)),
            pltpu.SemaphoreType.DMA((1,)),
        ],
        compiler_params=pltpu.CompilerParams(
            collective_id=call_id, has_side_effects=True, vmem_limit_bytes=VMEM_LIMIT
        ),
        cost_estimate=pl.CostEstimate(
            flops=8 * 2**30, bytes_accessed=16 * 2**20, transcendentals=2**22
        ),
    )(lengths, grad, w_out, attended, logits, query, lse, *raws, *gains, *tables, kv)


def scatter_task(scatter, finish):
    order = (2, 1, 3, 0)
    for ring in order:
        for path in (0, 1):
            scatter.start(path, ring)
    for ring in order:
        for path in (0, 1):
            yield
            scatter.forward(path, ring)
    for ring in order:
        for path in (0, 1):
            yield
            scatter.settle(path, ring)
            if ring == 0:
                scatter.start(path, 4)
    for path in (0, 1):
        yield
        scatter.forward(path, 4)
    for path in (0, 1):
        yield
        finish(path, scatter.total(path, 4))


def gather_task(gather):
    gather.start()
    for number in range(len(STAGES)):
        yield
        yield from gather.stage_task(number)


def spread_small(value, own, came, sems):
    first = lax.broadcasted_iota(jnp.int32, value.shape, 0) < 3
    slot = 0
    for axis in ("grp_1", "grp_0", "seq_1", "seq_0"):
        size = lax.axis_size(axis)
        at = lax.axis_index(axis)
        own[...] = value
        copies = []
        for far in range(1, size):
            to = {axis: lax.rem(at + far, size)}
            copies.append(send(own, came.at[slot], sems, slot, to))
            slot += 1
        yield
        for n, copy in enumerate(copies):
            copy.wait_recv()
            part = came[slot - len(copies) + n]
            value = value + (part if axis in SEQ else jnp.where(first, part, 0.0))
        for copy in copies:
            copy.wait_send()
    return value


def tail_kernel(
    hidden_ref,
    w_down_ref,
    middle_ref,
    grad_query_ref,
    grad_key_ref,
    grad_value_ref,
    grad_logits_ref,
    w_query_ref,
    w_key_ref,
    w_value_ref,
    w_gate_ref,
    base_ref,
    gain_ref,
    grad_middle_ref,
    normed_ref,
    gated_ref,
    grad_rows_ref,
    small_ref,
    mixed_out,
    tokens_out,
    sums_out,
    small_out,
    *scratch,
):
    mixed_scratch, token_scratch = scratch[:11], scratch[11:22]
    terms, came, scatter_sems, whole, gather_sems, own, small_came, small_sems, out_sem = scratch[22:]
    y, x = plane_place()
    z, core, above, below, twin = group_places()
    places = [*plane_sides("seq_0"), *plane_sides("seq_1"), above, below, twin]
    for axis in ("seq_0", "seq_1", "grp_0"):
        places.append({axis: lax.rem(lax.axis_index(axis) + 2, 4)})
    arrive = greet(places)
    entered = []

    def ready():
        if not entered:
            entered.append(True)
            arrive()

    rows, width = normed_ref.shape
    share = rows // 8
    state = {}
    ahead = jnp.concatenate([grad_query_ref[...], grad_key_ref[...], grad_value_ref[...]], axis=1)
    split = ahead.shape[1]

    def weight_terms(n, carry):
        cols = pl.ds(pl.multiple_of(n * 256, 256), 256)
        block = lax.dot_general(
            normed_ref[:, cols], ahead, COL_CONTRACT, preferred_element_type=f32
        )
        at = pl.ds(n * 2, 2)
        terms[at, :, :, :, 0:split] = block.astype(bf16).reshape(2, 2, 2, 32, split)
        block = lax.dot_general(
            gated_ref[...], grad_rows_ref[:, cols], COL_CONTRACT, preferred_element_type=f32
        ).astype(bf16)
        for piece in range(2):
            part = block[:, piece * 128 : (piece + 1) * 128].reshape(2, 2, 2, 32, 128)
            for side in range(2):
                low = split + side * 128
                terms[n * 2 + piece, :, :, :, low : low + 128] = part[:, :, side]
        return carry

    lax.fori_loop(0, width // 256, weight_terms, 0)
    ready()
    scatter = Scatter(terms, came, scatter_sems)
    gather = Gather(whole, gather_sems)

    def weights():
        place = y * 4 + x

        def finish(path, halves):
            for half, value in enumerate(halves):
                whole[place, path, half] = value.astype(bf16)

        yield from scatter_task(scatter, finish)
        yield from gather_task(gather)
        done = pltpu.make_async_copy(whole, sums_out, out_sem.at[0])
        done.start()
        gather.finish()
        scatter.finish()
        yield
        done.wait()

    def token_rows():
        product = group_product(
            (grad_query_ref, grad_key_ref, grad_value_ref, grad_logits_ref),
            (w_query_ref, w_key_ref, w_value_ref, w_gate_ref),
            True,
            share,
            width,
        )
        total, copies = yield from sum_rows(product, share, ready, token_scratch[:7])
        buffer, twin_sems, ring_sems, done_sem = token_scratch[7:]
        unit, inverse = unit_scale(base_ref[...].astype(f32))
        state["gain"] = jnp.sum(total * unit, axis=0, keepdims=True)
        buffer[pl.ds(group_rows(z, core, 0, share), share), :] = (
            grad_middle_ref[...] + norm_back(total * gain_ref[...], unit, inverse)
        ).astype(bf16)
        yield from join_rows(buffer, share, twin_sems, ring_sems)
        done = pltpu.make_async_copy(buffer, tokens_out, done_sem.at[0])
        done.start()
        for copy in copies:
            copy.wait_send()
        yield
        done.wait()

    def mixed_rows():
        product = group_product((hidden_ref,), (w_down_ref,), False, share, width)
        total, copies = yield from sum_rows(product, share, ready, mixed_scratch[:7])
        buffer, twin_sems, ring_sems, done_sem = mixed_scratch[7:]
        buffer[pl.ds(group_rows(z, core, 0, share), share), :] = (
            middle_ref[...] + total
        ).astype(bf16)
        yield from join_rows(buffer, share, twin_sems, ring_sems)
        done = pltpu.make_async_copy(buffer, mixed_out, done_sem.at[0])
        done.start()
        for copy in copies:
            copy.wait_send()
        yield
        done.wait()

    def small_sums():
        gates = lax.dot_general(
            grad_logits_ref[...], normed_ref[...], COL_CONTRACT, preferred_element_type=f32
        )
        while "gain" not in state:
            yield
        given = small_ref[...]
        value = jnp.concatenate([given[0:1], state["gain"], given[1:2], gates, given[2:5]], axis=0)
        small_out[...] = yield from spread_small(value, own, small_came, small_sems)

    run_together([weights(), token_rows(), mixed_rows(), small_sums()])


def finish_backward(call_id, operands, rows, width, places, heads_width):
    vmem = pl.BlockSpec(memory_space=pltpu.VMEM)
    hbm = pl.BlockSpec(memory_space=pl.ANY)
    shape = jax.ShapeDtypeStruct
    share = rows // 8
    pieces = (places, 2, 2, 32, heads_width)
    return pl.pallas_call(
        tail_kernel,
        name="finish_backward",
        out_shape=(
            shape((rows, width), bf16),
            shape((rows, width), bf16),
            shape(pieces, bf16),
            shape((8, width), f32),
        ),
        in_specs=[vmem] * len(operands),
        out_specs=(hbm, hbm, hbm, vmem),
        scratch_shapes=row_scratch(rows, share, width)
        + row_scratch(rows, share, width)
        + [
            pltpu.VMEM(pieces, bf16),
            pltpu.VMEM((2, 5, 6, 32, heads_width), bf16),
            pltpu.SemaphoreType.DMA((2, 60)),
            pltpu.VMEM(pieces, bf16),
            pltpu.SemaphoreType.DMA((2, 40)),
            pltpu.VMEM((8, width), f32),
            pltpu.VMEM((10, 8, width), f32),
            pltpu.SemaphoreType.DMA((2, 10)),
            pltpu.SemaphoreType.DMA((1,)),
        ],
        compiler_params=pltpu.CompilerParams(
            collective_id=call_id, has_side_effects=True, vmem_limit_bytes=VMEM_LIMIT
        ),
        cost_estimate=pl.CostEstimate(
            flops=6 * 2**30, bytes_accessed=32 * 2**20, transcendentals=0
        ),
    )(*operands)


def local(
    tokens,
    lengths,
    norm_attn,
    w_query,
    w_key,
    w_value,
    w_gate,
    norm_query,
    norm_key,
    w_out,
    norm_ffn,
    w_ffn_gate,
    w_ffn_up,
    w_down,
    cotangent,
):
    buckets, per_device, model_width = tokens.shape
    head_count = w_gate.shape[1]
    head_size = norm_query.shape[0]
    kv_count = w_key.shape[1] // head_size
    group_size = head_count // kv_count
    total_rows = buckets * per_device
    full_len = per_device * lax.axis_size(SEQ)
    positions = lax.axis_index(SEQ) * per_device + jnp.arange(per_device, dtype=jnp.int32)
    share_rows = total_rows // lax.axis_size(GRP)
    share_start = lax.axis_index(GRP) * share_rows

    def take_share(values):
        return lax.dynamic_slice_in_dim(values, share_start, share_rows, 0)

    flat = tokens.reshape(total_rows, model_width)
    tables = angle_tables(per_device, head_size, lax.axis_size(SEQ))
    gains_in = (norm_query.reshape(1, -1), norm_key.reshape(1, -1))
    normed, query_raw, key_raw, logits, query_low, pairs, attended, lse, gated = attend(
        5, lengths, flat, norm_attn.reshape(1, -1), w_query, w_key, w_value, w_gate, *gains_in, tables
    )
    base = take_share(flat)
    share = jax.ShapeDtypeStruct((share_rows, model_width), f32)
    scale = jax.ShapeDtypeStruct((share_rows, 1), f32)
    gain_row = jax.ShapeDtypeStruct((1, model_width), f32)
    middle, inverse_two, normed_two = exchange_rows(
        "attention_rows",
        1,
        (gated,),
        (w_out,),
        False,
        finish_middle,
        (base, norm_ffn.reshape(1, -1)),
        (share, scale),
    )
    live_rows = (positions[None, :] < lengths[:, None]).astype(f32)
    loss_ratio = buckets * full_len / jnp.sum(lengths).astype(f32)
    grad_out = (cotangent.astype(f32) * live_rows[:, :, None] * loss_ratio).reshape(
        total_rows, model_width
    )
    grad_out_low = grad_out.astype(bf16)
    hidden, grad_gate_pre, grad_up, grad_down, grad_ffn_gate, grad_ffn_up = feed_forward(
        normed_two, grad_out_low, w_ffn_gate, w_ffn_up, w_down
    )
    ffn_sums = lax.psum((grad_ffn_gate, grad_ffn_up, grad_down), SEQ)
    grad_middle, ffn_gain_part, grad_attn_low = exchange_rows(
        "feed_back_rows",
        2,
        (grad_gate_pre, grad_up),
        (w_ffn_gate, w_ffn_up),
        True,
        finish_grad_middle,
        (middle, inverse_two, norm_ffn.reshape(1, -1), take_share(grad_out)),
        (share, gain_row),
    )
    grad_query_low, grad_key_low, grad_value_low, grad_logits, query_gain, key_gain = attend_back(
        6,
        lengths,
        grad_attn_low,
        w_out,
        attended,
        logits,
        query_low,
        lse,
        (query_raw, key_raw),
        gains_in,
        tables,
        pairs,
    )
    small = jnp.concatenate(
        (
            ffn_gain_part,
            jnp.pad(
                jnp.concatenate((query_gain, key_gain), axis=1),
                ((0, 0), (0, model_width - 2 * head_size)),
            ),
            jnp.zeros((3, model_width), f32),
        )
    )
    mixed, grad_tokens, pieces, small = finish_backward(
        7,
        (
            hidden,
            w_down,
            middle,
            grad_query_low,
            grad_key_low,
            grad_value_low,
            grad_logits,
            w_query,
            w_key,
            w_value,
            w_gate,
            base,
            norm_attn.reshape(1, -1),
            grad_middle,
            normed,
            gated,
            grad_attn_low,
            small,
        ),
        total_rows,
        model_width,
        lax.axis_size(SEQ),
        (head_count + 2 * kv_count) * head_size + w_out.shape[0],
    )
    mixed = mixed.reshape(buckets, per_device, model_width)
    grad_tokens = grad_tokens.reshape(buckets, per_device, model_width)
    grad_norm_ffn, grad_norm_attn = small[0], small[1]
    grad_norm_query, grad_norm_key = small[2, :head_size], small[2, head_size : 2 * head_size]
    query_cols = head_count * head_size
    key_cols = query_cols + kv_count * head_size
    value_cols = key_cols + kv_count * head_size
    cols = pieces.reshape(model_width, -1).astype(f32)
    out_cols = pieces[..., value_cols:].reshape(lax.axis_size(SEQ), 4, 32, 2, head_size)
    out_cols = out_cols.transpose(1, 3, 2, 0, 4).reshape(w_out.shape).astype(f32)
    attn_sums = (
        cols[:, :query_cols],
        cols[:, query_cols:key_cols],
        cols[:, key_cols:value_cols],
        small[3 : 3 + head_count].T,
        out_cols,
    )
    ffn_sums = tuple(part.astype(f32) for part in (ffn_sums[0], ffn_sums[1], ffn_sums[2]))
    return (
        mixed,
        grad_tokens,
        grad_norm_attn,
        attn_sums[0],
        attn_sums[1],
        attn_sums[2],
        attn_sums[3],
        grad_norm_query,
        grad_norm_key,
        attn_sums[4],
        grad_norm_ffn,
        ffn_sums[0],
        ffn_sums[1],
        ffn_sums[2],
    )


def solution(mesh):
    finer = Mesh(mesh.devices.reshape(4, 4, 4, 2), ("seq_0", "seq_1", "grp_0", "grp_1"))
    return jax.shard_map(
        local,
        mesh=finer,
        in_specs=(
            P(None, SEQ, None),
            P(),
            P(),
            P(None, GRP),
            P(None, GRP),
            P(None, GRP),
            P(None, GRP),
            P(),
            P(),
            P(GRP, None),
            P(),
            P(None, GRP),
            P(None, GRP),
            P(GRP, None),
            P(None, SEQ, None),
        ),
        out_specs=(
            P(None, SEQ, None),
            P(None, SEQ, None),
            P(),
            P(None, GRP),
            P(None, GRP),
            P(None, GRP),
            P(None, GRP),
            P(),
            P(),
            P(GRP, None),
            P(),
            P(None, GRP),
            P(None, GRP),
            P(GRP, None),
        ),
        check_vma=False,
    )
```

```python
import jax
import jax.numpy as jnp
import numpy as np
from jax import lax
from jax.experimental import pallas as pl
from jax.experimental.pallas import tpu as pltpu
from jax.sharding import Mesh
from jax.sharding import PartitionSpec as P

GRP = ("grp_0", "grp_1")
SEQ = ("seq_0", "seq_1")
MESH = pl.DeviceIdType.MESH
VMEM_LIMIT = 60 * 2**20

f32 = jnp.float32
bf16 = jnp.bfloat16


epsilon = 1e-06
rope_base = 1000000.0


def unit_scale(values):
    inverse = lax.rsqrt(jnp.mean(values * values, axis=-1, keepdims=True) + epsilon)
    return (values * inverse, inverse)


def norm_back(grad_unit, unit, inverse):
    return inverse * (grad_unit - unit * jnp.mean(grad_unit * unit, axis=-1, keepdims=True))


ROW_CONTRACT = (((1,), (1,)), ((), ()))
COL_CONTRACT = (((0,), (0,)), ((), ()))


def send(source, target, sems, slot, to):
    copy = pltpu.make_async_remote_copy(
        src_ref=source,
        dst_ref=target,
        send_sem=sems.at[0, slot],
        recv_sem=sems.at[1, slot],
        device_id=to,
        device_id_type=MESH,
    )
    copy.start()
    return copy


def group_places():
    z = lax.axis_index("grp_0")
    core = lax.axis_index("grp_1")
    ring = lax.axis_size("grp_0")
    above = {"grp_0": lax.rem(z + 1, ring)}
    below = {"grp_0": lax.rem(z + ring - 1, ring)}
    twin = {"grp_1": 1 - core}
    return z, core, above, below, twin


def greet(places):
    barrier = pltpu.get_barrier_semaphore()
    for place in places:
        pl.semaphore_signal(barrier, inc=1, device_id=place, device_id_type=MESH)
    return lambda: pl.semaphore_wait(barrier, len(places))


def group_rows(z, core, far, share):
    return pl.multiple_of((lax.rem(z + far, 4) * 2 + core) * share, share)


FAR = (2, 1, 3, 0)


def run_together(tasks, urgent=None, pace=1):
    tasks = list(tasks)
    while tasks:
        for task in list(tasks):
            if urgent is not None:
                for _ in range(pace):
                    next(urgent, None)
            if next(task, tasks) is tasks:
                tasks.remove(task)
    for _ in urgent or ():
        pass


def in_turn(tasks):
    tasks = list(tasks)
    while tasks:
        for task in list(tasks):
            try:
                next(task)
            except StopIteration:
                tasks.remove(task)
            yield


def sum_rows(product, share, ready, scratch):
    mine, twin_out, twin_in, low, ring, twin_sems, ring_sems = scratch
    z, core, above, below, twin = group_places()
    half = share // 2
    top, bottom = pl.ds(0, half), pl.ds(half, half)

    def put_twin(cols, block):
        twin_out[:, :, cols] = block.astype(bf16)

    def put_mine(cols, block):
        mine[:, :, cols] = block

    product(1 - core, put_twin)
    ready()
    pairs = [send(twin_out.at[k], twin_in.at[k], twin_sems, k, twin) for k in range(4)]
    product(core, put_mine)

    def joined(k, rows):
        return mine[k, rows, :] + twin_in[k, rows, :].astype(f32)

    yield
    pairs[0].wait_recv()
    low[0] = joined(0, pl.ds(0, share)).astype(bf16)
    steps = [
        send(low.at[0, top], ring.at[0], ring_sems, 0, above),
        send(low.at[0, bottom], ring.at[1], ring_sems, 1, below),
    ]
    pairs[1].wait_recv()
    low[1, bottom, :] = joined(1, bottom).astype(bf16)
    steps.append(send(low.at[1, bottom], ring.at[2], ring_sems, 2, above))
    pairs[2].wait_recv()
    low[2, top, :] = joined(2, top).astype(bf16)
    steps.append(send(low.at[2, top], ring.at[3], ring_sems, 3, below))
    yield
    steps[0].wait_recv()
    low[1, top, :] = (joined(1, top) + ring[0].astype(f32)).astype(bf16)
    steps.append(send(low.at[1, top], ring.at[4], ring_sems, 4, above))
    yield
    steps[1].wait_recv()
    low[2, bottom, :] = (joined(2, bottom) + ring[1].astype(f32)).astype(bf16)
    steps.append(send(low.at[2, bottom], ring.at[5], ring_sems, 5, below))
    pairs[3].wait_recv()
    yield
    for step in steps[2:]:
        step.wait_recv()
    total = jnp.concatenate(
        [
            joined(3, top) + ring[3].astype(f32) + ring[4].astype(f32),
            joined(3, bottom) + ring[2].astype(f32) + ring[5].astype(f32),
        ],
        axis=0,
    )
    return total, pairs + steps


def join_rows(whole, share, twin_sems, ring_sems):
    z, core, above, below, twin = group_places()
    half = share // 2

    def part(far, side):
        start = group_rows(z, core, far, share)
        return whole.at[pl.ds(pl.multiple_of(start + side * half, half), half), :]

    def hand(far, side, sems, slot, to):
        block = part(far, side)
        return send(block, block, sems, slot, to)

    own = whole.at[pl.ds(group_rows(z, core, 0, share), share), :]
    up = [hand(0, 0, ring_sems, 0, above), hand(0, 1, ring_sems, 1, above)]
    down = [hand(0, 1, ring_sems, 2, below), hand(0, 0, ring_sems, 3, below)]
    across = [send(own, own, twin_sems, 0, twin)]
    yield
    up[0].wait_recv()
    up.append(hand(3, 0, ring_sems, 4, above))
    across.append(hand(3, 0, twin_sems, 1, twin))
    yield
    down[0].wait_recv()
    down.append(hand(1, 1, ring_sems, 5, below))
    across.append(hand(1, 1, twin_sems, 2, twin))
    yield
    up[1].wait_recv()
    across.append(hand(3, 1, twin_sems, 3, twin))
    down[1].wait_recv()
    across.append(hand(1, 0, twin_sems, 4, twin))
    yield
    up[2].wait_recv()
    across.append(hand(2, 0, twin_sems, 5, twin))
    down[2].wait_recv()
    across.append(hand(2, 1, twin_sems, 6, twin))
    yield
    for copy in across:
        copy.wait_recv()
    for copy in up + down + across:
        copy.wait_send()


def row_scratch(rows, share, width):
    return [
        pltpu.VMEM((4, share, width), f32),
        pltpu.VMEM((4, share, width), bf16),
        pltpu.VMEM((4, share, width), bf16),
        pltpu.VMEM((3, share, width), bf16),
        pltpu.VMEM((6, share // 2, width), bf16),
        pltpu.SemaphoreType.DMA((2, 4)),
        pltpu.SemaphoreType.DMA((2, 6)),
        pltpu.VMEM((rows, width), bf16),
        pltpu.SemaphoreType.DMA((2, 7)),
        pltpu.SemaphoreType.DMA((2, 6)),
        pltpu.SemaphoreType.DMA((1,)),
    ]


def group_product(lefts, rights, across, share, width):
    z = lax.axis_index("grp_0")
    step = 512

    def product(core, put):
        picked = []
        for left in lefts:
            blocks = [left[pl.ds(group_rows(z, core, far, share), share), :] for far in FAR]
            picked.append(jnp.concatenate(blocks, axis=0))
        for at in range(0, width, step):
            cols = pl.ds(at, step)
            total = None
            for left, right, flip in zip(picked, rights, across):
                if flip:
                    term = lax.dot_general(
                        left, right[cols, :], ROW_CONTRACT, preferred_element_type=f32
                    )
                else:
                    term = jnp.dot(left, right[:, cols], preferred_element_type=f32)
                total = term if total is None else total + term
            put(cols, total.reshape(4, share, step))

    return product


LOG2_E = 1.4426950408889634
STAGES = (
    ((1, 0), (3, 0), (0, 1), (0, 3)),
    ((2, 0), (0, 2)),
    ((1, 1), (1, 3), (3, 1), (3, 3)),
    ((1, 2), (3, 2), (2, 1), (2, 3)),
    ((2, 2),),
)


def angle_tables(block, size, count):
    half = size // 2
    freq = rope_base ** (-np.arange(half, dtype=np.float64) * (2.0 / size))
    inner = np.arange(block)[:, None] * freq[None, :]
    outer = (np.arange(count) * block)[:, None] * freq[None, :]

    def table(angle):
        sine = np.sin(angle)
        cosine = np.cos(angle)
        both = np.stack(
            [
                np.concatenate([cosine, cosine], axis=1),
                np.concatenate([-sine, sine], axis=1),
            ]
        )
        return both.astype(np.float32)

    return table(inner), table(outer)


def local_angles(inner, outer, place):
    cos_in, sin_in = inner[0], inner[1]
    cos_out = outer[0, pl.ds(place, 1), :]
    sin_out = outer[1, pl.ds(place, 1), :]
    return cos_in * cos_out - sin_in * sin_out, sin_in * cos_out + cos_in * sin_out


def turned(values):
    return pltpu.roll(values, values.shape[-1] // 2, axis=values.ndim - 1)


def plane_place():
    return lax.axis_index("seq_0"), lax.axis_index("seq_1")


def plane_sides(axis):
    at = lax.axis_index(axis)
    size = lax.axis_size(axis)
    return {axis: lax.rem(at + 1, size)}, {axis: lax.rem(at + size - 1, size)}


AXES = (("seq_1", "seq_0"), ("seq_0", "seq_1"))


def place_at(path, first, second):
    y, x = plane_place()
    dx, dy = (first, second) if path == 0 else (second, first)
    return lax.rem(y + dy, 4) * 4 + lax.rem(x + dx, 4)


def pass_start(block, axis, sems, slot):
    up, down = plane_sides(axis)
    return [send(block, block, sems, slot, up), send(block, block, sems, slot + 1, down)]


def pass_on(copies, before, after, axis, sems, slot):
    up, down = plane_sides(axis)
    copies[0].wait_recv()
    copies.append(send(before.at[0], before.at[0], sems, slot + 2, up))
    copies[1].wait_recv()
    copies.append(send(after.at[1], after.at[1], sems, slot + 3, down))


def pass_end(copies):
    copies[2].wait_recv()
    copies[3].wait_recv()


class Gather:
    def __init__(self, buffer, sems):
        self.buffer, self.sems = buffer, sems
        self.rings = [{}, {}]

    def block(self, path, first, second):
        return self.buffer.at[place_at(path, first, second), path]

    def slot(self, path, ring):
        return path * 20 + (4 if ring == "first" else ring) * 4

    def begin(self, path, ring):
        axis = AXES[path][0] if ring == "first" else AXES[path][1]
        block = self.block(path, 0 if ring == "first" else ring, 0)
        self.rings[path][ring] = pass_start(block, axis, self.sems, self.slot(path, ring))

    def forward(self, path, ring):
        if ring == "first":
            axis, before, after = AXES[path][0], self.block(path, 3, 0), self.block(path, 1, 0)
        else:
            axis = AXES[path][1]
            before, after = self.block(path, ring, 3), self.block(path, ring, 1)
        pass_on(self.rings[path][ring], before, after, axis, self.sems, self.slot(path, ring))

    def end(self, path, ring):
        pass_end(self.rings[path][ring])

    def start(self):
        for path in (0, 1):
            self.begin(path, "first")
        for path in (0, 1):
            self.begin(path, 0)

    def stage(self, number):
        for path in (0, 1):
            if number == 0:
                self.forward(path, "first")
                self.begin(path, 1)
                self.begin(path, 3)
                self.forward(path, 0)
            elif number == 1:
                self.end(path, "first")
                self.begin(path, 2)
                self.end(path, 0)
            elif number == 2:
                self.forward(path, 1)
                self.forward(path, 3)
            elif number == 3:
                self.end(path, 1)
                self.end(path, 3)
                self.forward(path, 2)
            else:
                self.end(path, 2)

    def finish(self):
        for rings in self.rings:
            for copies in rings.values():
                for copy in copies:
                    copy.wait_send()


class Scatter:
    def __init__(self, buffer, recv, sems):
        self.buffer, self.recv, self.sems = buffer, recv, sems
        self.copies = {}

    def block(self, path, ring, step):
        if ring == 4:
            return self.buffer.at[place_at(path, step, 0), path]
        return self.buffer.at[place_at(path, ring, step), path]

    def sides(self, path, ring):
        return plane_sides(AXES[path][0] if ring == 4 else AXES[path][1])

    def push(self, path, ring, half_ref, slot, to):
        at = (path * 5 + ring) * 6 + slot
        copy = send(half_ref, self.recv.at[path, ring, slot], self.sems, at, to)
        self.copies.setdefault((path, ring), []).append(copy)

    def start(self, path, ring):
        up, down = self.sides(path, ring)
        far = self.block(path, ring, 2)
        self.push(path, ring, far.at[0], 0, up)
        self.push(path, ring, far.at[1], 1, down)
        self.push(path, ring, self.block(path, ring, 1).at[1], 2, up)
        self.push(path, ring, self.block(path, ring, 3).at[0], 3, down)

    def forward(self, path, ring):
        up, down = self.sides(path, ring)
        for slot, step, half, to in ((0, 1, 0, up), (1, 3, 1, down)):
            self.copies[path, ring][slot].wait_recv()
            part = self.block(path, ring, step).at[half]
            came = self.recv[path, ring, slot]
            part[...] = (part[...].astype(f32) + came.astype(f32)).astype(bf16)
            self.push(path, ring, part, slot + 4, to)

    def total(self, path, ring):
        for copy in self.copies[path, ring][2:]:
            copy.wait_recv()
        own = self.block(path, ring, 0)
        out = []
        for half, slots in ((0, (3, 4)), (1, (2, 5))):
            value = own[half].astype(f32)
            for slot in slots:
                value = value + self.recv[path, ring, slot].astype(f32)
            out.append(value)
        return out

    def settle(self, path, ring):
        own = self.block(path, ring, 0)
        for half, value in enumerate(self.total(path, ring)):
            own[half] = value.astype(bf16)

    def finish(self):
        for copies in self.copies.values():
            for copy in copies:
                copy.wait_send()


def greet_plane():
    places = [*plane_sides("seq_0"), *plane_sides("seq_1")]
    return greet(places)


def choose(index, options):
    value = options[-1]
    for n in range(len(options) - 2, -1, -1):
        value = jnp.where(index == n, options[n], value)
    return value


def once(action):
    done = []

    def call():
        if not done:
            done.append(True)
            action()

    return call


def greet_sides():
    z, core, above, below, twin = group_places()
    places = [*plane_sides("seq_0"), *plane_sides("seq_1"), above, below, twin]
    return once(greet(places))


def exchange_task(product, finish, share, ready, out, scratch):
    z, core, *_ = group_places()
    total, copies = yield from sum_rows(product, share, ready, scratch[:7])
    whole, twin_sems, ring_sems, out_sem = scratch[7:11]
    whole[pl.ds(group_rows(z, core, 0, share), share), :] = finish(total)
    yield from join_rows(whole, share, twin_sems, ring_sems)
    done = pltpu.make_async_copy(whole, out, out_sem.at[0])
    done.start()
    for copy in copies:
        copy.wait_send()
    yield
    done.wait()


def forward_kernel(
    lengths_ref,
    tokens_ref,
    gain_ref,
    w_query_ref,
    w_key_ref,
    w_value_ref,
    w_gate_ref,
    gain_query_ref,
    gain_key_ref,
    inner_ref,
    outer_ref,
    w_out_ref,
    gain_two_ref,
    normed_out,
    query_raw_out,
    key_raw_out,
    logits_out,
    query_out,
    keys_out,
    attended_out,
    lse_out,
    gated_out,
    middle_out,
    inverse_out,
    normed_two_out,
    normed,
    kv,
    sums,
    sems,
    out_sems,
    *row_refs,
):
    ready = greet_sides()
    y, x = plane_place()
    place = y * 4 + x
    rows, width = tokens_ref.shape
    buckets = kv.shape[1]
    block, size = kv.shape[3], kv.shape[4]
    heads = w_query_ref.shape[1] // size
    step = 64

    def norm_rows(n, carry):
        at = pl.ds(pl.multiple_of(n * step, step), step)
        unit, _ = unit_scale(tokens_ref[at, :].astype(f32))
        normed[at, :] = (unit * gain_ref[...]).astype(bf16)
        return carry

    lax.fori_loop(0, rows // step, norm_rows, 0)
    save_normed = pltpu.make_async_copy(normed, normed_out, out_sems.at[0])
    save_normed.start()
    cosine, sine = local_angles(inner_ref, outer_ref, place)

    def turn(values):
        return values * cosine + turned(values) * sine

    key_raw = jnp.dot(normed[...], w_key_ref[...], preferred_element_type=f32)
    value = jnp.dot(normed[...], w_value_ref[...], preferred_element_type=f32)
    key_raw_out[...] = key_raw
    spots = place * block + lax.broadcasted_iota(jnp.int32, (block, size), 0)
    for b in range(buckets):
        live = spots < lengths_ref[b]
        part = slice(b * block, (b + 1) * block)
        unit, _ = unit_scale(key_raw[part])
        kv[place, b, 0] = jnp.where(live, turn(unit * gain_key_ref[...]), 0.0).astype(bf16)
        kv[place, b, 1] = jnp.where(live, value[part], 0.0).astype(bf16)
    gather = Gather(kv, sems)
    ready()
    gather.start()
    query_raw = jnp.dot(normed[...], w_query_ref[...], preferred_element_type=f32)
    query_raw_out[...] = query_raw
    logits_out[...] = lax.dot_general(
        normed[...], w_gate_ref[...], ROW_CONTRACT, preferred_element_type=f32
    )
    for b in range(buckets):
        for h in range(heads):
            part = query_raw[b * block : (b + 1) * block, h * size : (h + 1) * size]
            unit, _ = unit_scale(part)
            query_out[b, h * block : (h + 1) * block, :] = turn(
                unit * gain_query_ref[...]
            ).astype(bf16)
    scale = size**-0.5 * LOG2_E

    def weigh(source, b, causal):
        keys, vals = kv[source, b, 0], kv[source, b, 1]
        scores = lax.dot_general(query_out[b], keys, ROW_CONTRACT, preferred_element_type=f32)
        weights = jnp.exp2(scores * scale)
        if causal:
            spot = lax.broadcasted_iota(jnp.int32, (heads * block, block), 0) % block
            column = lax.broadcasted_iota(jnp.int32, (heads * block, block), 1)
            weights = jnp.where(column <= spot, weights, 0.0)
        there = source * block + lax.broadcasted_iota(jnp.int32, (block, size), 0)
        ones = jnp.where(there < lengths_ref[b], 1.0, 0.0).astype(bf16)
        both = jnp.concatenate([vals, ones], axis=1)
        return jnp.dot(weights.astype(bf16), both, preferred_element_type=f32)

    for b in range(buckets):
        sums[b] = weigh(place, b, True)
    for number, offsets in enumerate(STAGES):
        gather.stage(number)

        def one(n, carry):
            which, b = n // buckets, n % buckets
            dx = choose(which, [o[0] for o in offsets])
            dy = choose(which, [o[1] for o in offsets])
            source = lax.rem(y + dy, 4) * 4 + lax.rem(x + dx, 4)

            @pl.when(source < place)
            def _():
                sums[b] = sums[b] + weigh(source, b, False)

            return carry

        lax.fori_loop(0, len(offsets) * buckets, one, 0)
    save_keys = pltpu.make_async_copy(kv, keys_out, out_sems.at[1])
    save_keys.start()
    gates = jax.nn.sigmoid(logits_out[...])
    for b in range(buckets):
        for h in range(heads):
            at = slice(h * block, (h + 1) * block)
            total = sums[b, at, size:]
            attended = sums[b, at, :size] / total
            here = (slice(b * block, (b + 1) * block), slice(h * size, (h + 1) * size))
            attended_out[here] = attended
            lse_out[b, at, :] = jnp.log2(total)
            gated_out[here] = (attended * gates[here[0], h : h + 1]).astype(bf16)
    share = rows // 8
    z, core, *_ = group_places()
    product = group_product((gated_out,), (w_out_ref,), (False,), share, width)

    def finish(total):
        mine = tokens_ref[pl.ds(group_rows(z, core, 0, share), share), :]
        middle = mine.astype(f32) + total
        unit, inverse = unit_scale(middle)
        middle_out[...] = middle
        inverse_out[...] = inverse
        return (unit * gain_two_ref[...]).astype(bf16)

    run_together([exchange_task(product, finish, share, ready, normed_two_out, row_refs)])
    gather.finish()
    save_normed.wait()
    save_keys.wait()


def params(call_id):
    return pltpu.CompilerParams(
        collective_id=call_id, has_side_effects=True, vmem_limit_bytes=VMEM_LIMIT
    )


def forward(call_id, lengths, tokens, gain, w_query, w_key, w_value, w_gate, gains, tables, w_out, gain_two):
    rows, width = tokens.shape
    size = gains[0].shape[1]
    buckets = lengths.shape[0]
    block = rows // buckets
    heads = w_query.shape[1] // size
    places = lax.axis_size(SEQ)
    share = rows // 8
    vmem = pl.BlockSpec(memory_space=pltpu.VMEM)
    hbm = pl.BlockSpec(memory_space=pl.ANY)
    shape = jax.ShapeDtypeStruct
    pairs = (places, buckets, 2, block, size)
    return pl.pallas_call(
        forward_kernel,
        name="forward",
        out_shape=(
            shape((rows, width), bf16),
            shape((rows, heads * size), f32),
            shape((rows, size), f32),
            shape((rows, heads), f32),
            shape((buckets, heads * block, size), bf16),
            shape(pairs, bf16),
            shape((rows, heads * size), f32),
            shape((buckets, heads * block, size), f32),
            shape((rows, heads * size), bf16),
            shape((share, width), f32),
            shape((share, 1), f32),
            shape((rows, width), bf16),
        ),
        in_specs=[pl.BlockSpec(memory_space=pltpu.SMEM)] + [vmem] * 12,
        out_specs=(hbm, vmem, vmem, vmem, vmem, hbm, vmem, vmem, vmem, vmem, vmem, hbm),
        scratch_shapes=[
            pltpu.VMEM((rows, width), bf16),
            pltpu.VMEM(pairs, bf16),
            pltpu.VMEM((buckets, heads * block, 2 * size), f32),
            pltpu.SemaphoreType.DMA((2, 40)),
            pltpu.SemaphoreType.DMA((2,)),
        ]
        + row_scratch(rows, share, width),
        compiler_params=params(call_id),
        cost_estimate=pl.CostEstimate(
            flops=5 * 2**30, bytes_accessed=16 * 2**20, transcendentals=2**22
        ),
    )(lengths, tokens, gain, w_query, w_key, w_value, w_gate, *gains, *tables, w_out, gain_two)


def feed_kernel(
    lengths_ref,
    rows_ref,
    given_hbm,
    gate_hbm,
    up_hbm,
    down_hbm,
    middle_ref,
    inverse_ref,
    gain_ref,
    grad_middle_out,
    gain_out,
    shares_out,
    rows_out,
    feed_out,
    given,
    seed,
    own_seed,
    gates,
    ups,
    downs,
    rows_across,
    hidden,
    grad_gate,
    grad_up,
    terms,
    came,
    scatter_sems,
    load_sems,
    *row_refs,
):
    rows, width = rows_ref.shape
    count = gates.shape[0]
    step = gates.shape[2]
    load_given = pltpu.make_async_copy(given_hbm, given, load_sems.at[0])
    load_given.start()
    loads = []
    for n in range(count):
        cols = pl.ds(n * step, step)
        parts = (
            (gate_hbm.at[:, cols], gates.at[n]),
            (up_hbm.at[:, cols], ups.at[n]),
            (down_hbm.at[cols, :], downs.at[n]),
        )
        for k, (source, target) in enumerate(parts):
            loads.append(pltpu.make_async_copy(source, target, load_sems.at[1 + n * 3 + k]))
            loads[-1].start()
    ready = greet_sides()
    share = rows // 8
    rows_across[...] = rows_ref[...].T
    load_given.wait()
    make_seed(lengths_ref, given, seed, own_seed)
    def activations(n):
        for copy in loads[3 * n : 3 * n + 3]:
            copy.wait()
        cols = slice(n * step, (n + 1) * step)
        gate_pre = jnp.dot(rows_ref[...], gates[n], preferred_element_type=f32)
        up_proj = jnp.dot(rows_ref[...], ups[n], preferred_element_type=f32)
        grad_hidden = lax.dot_general(
            seed[...], downs[n], ROW_CONTRACT, preferred_element_type=f32
        )
        gate_sig = jax.nn.sigmoid(gate_pre)
        silu = gate_pre * gate_sig
        hidden[:, cols] = (silu * up_proj).astype(bf16)
        grad_gate[n] = (
            grad_hidden * up_proj * gate_sig * (1.0 + gate_pre * (1.0 - gate_sig))
        ).astype(bf16)
        grad_up[n] = (grad_hidden * silu).astype(bf16)

    def weight_task(n):
        across = hidden[:, n * step : (n + 1) * step].T

        def weight_terms(k, carry):
            here = pl.ds(pl.multiple_of(k * 256, 256), 256)
            at = pl.ds(k * 2, 2)
            for side, grad in ((0, grad_gate), (1, grad_up)):
                part = jnp.dot(rows_across[here, :], grad[n], preferred_element_type=f32)
                terms[n, at, :, :, :, side * step : (side + 1) * step] = part.astype(
                    bf16
                ).reshape(2, 2, 2, 32, step)
            part = jnp.dot(across, seed[:, here], preferred_element_type=f32).astype(bf16)
            place_sides(terms.at[n], k, part, 2 * step)
            return carry

        for first in range(0, width // 256, 4):
            lax.fori_loop(first, first + 4, weight_terms, 0)
            yield
        ready()
        scatter = Scatter(terms.at[n], came.at[n], scatter_sems.at[n])
        scatters.append(scatter)

        def keep(path, halves):
            for half, value in enumerate(halves):
                shares_out[n, path, half] = value.astype(bf16)

        yield from scatter_task(scatter, keep)

    def finish_rows(total):
        unit = middle_ref[...] * inverse_ref[...]
        gain_out[...] = jnp.sum(total * unit, axis=0, keepdims=True)
        grad = own_seed[...] + norm_back(total * gain_ref[...], unit, inverse_ref[...])
        grad_middle_out[...] = grad
        return grad.astype(bf16)

    pairs = range(count)
    product = group_product(
        [grad_gate.at[n] for n in pairs] + [grad_up.at[n] for n in pairs],
        [gates.at[n] for n in pairs] + [ups.at[n] for n in pairs],
        (True,) * (2 * count),
        share,
        width,
    )
    scatters = []
    tasks = []
    for n in range(count):
        activations(n)
        tasks.append(weight_task(n))
        for _ in range(3):
            next(tasks[n])
    exchange = exchange_task(product, finish_rows, share, ready, rows_out, row_refs)
    next(exchange)
    next(tasks[0])

    z, core, *_ = group_places()

    def feed_rows(k, carry):
        cols = pl.ds(pl.multiple_of(k * 512, 512), 512)
        total = None
        for n in pairs:
            left = hidden[:, n * step : (n + 1) * step]
            term = jnp.dot(left, downs[n, :, cols], preferred_element_type=f32)
            total = term if total is None else total + term
        feed_out[:, cols] = total.astype(bf16)
        at = pl.ds(group_rows(z, core, 0, share), share)
        feed_out[at, cols] = (feed_out[at, cols].astype(f32) + middle_ref[:, cols]).astype(bf16)
        return carry

    lax.fori_loop(0, width // 512, feed_rows, 0)
    run_together(tasks, exchange, 3)
    for scatter in scatters:
        scatter.finish()


def make_seed(lengths_ref, given_ref, seed, own_seed):
    rows = given_ref.shape[0]
    buckets = lengths_ref.shape[0]
    block = rows // buckets
    share = rows // 8
    y, x = plane_place()
    z, core, *_ = group_places()
    total = lengths_ref[0]
    for b in range(1, buckets):
        total = total + lengths_ref[b]
    places = lax.axis_size("seq_0") * lax.axis_size("seq_1")
    ratio = float(buckets * places * block) / jnp.full((1, 1), total, jnp.int32).astype(f32)

    def weighted(start):
        spots = (
            (y * 4 + x) * block
            + start % block
            + lax.broadcasted_iota(jnp.int32, (share, 1), 0)
        )
        live = (spots < lengths_ref[start // block]).astype(f32)
        at = pl.ds(pl.multiple_of(start, share), share)
        return at, given_ref[at, :].astype(f32) * live * ratio

    own_seed[...] = weighted(group_rows(z, core, 0, share))[1]

    def round_rows(n, carry):
        at, values = weighted(n * share)
        seed[at, :] = values.astype(bf16)
        return carry

    lax.fori_loop(0, 8, round_rows, 0)


def place_sides(target, k, block, low):
    for piece in range(2):
        part = block[:, piece * 128 : (piece + 1) * 128].reshape(2, 2, 2, 32, 128)
        for side in range(2):
            at = low + side * 128
            target[k * 2 + piece, :, :, :, at : at + 128] = part[:, :, side]


def feed_forward(call_id, lengths, rows, given, w_gate, w_up, w_down, middle, inverse, gain):
    count, width = rows.shape
    units = w_gate.shape[1]
    step = 256
    parts = units // step
    places = lax.axis_size(SEQ)
    share = count // 8
    vmem = pl.BlockSpec(memory_space=pltpu.VMEM)
    hbm = pl.BlockSpec(memory_space=pl.ANY)
    shape = jax.ShapeDtypeStruct
    pieces = (places, 2, 2, 32, 3 * step)
    return pl.pallas_call(
        feed_kernel,
        name="feed_forward",
        out_shape=(
            shape((share, width), f32),
            shape((1, width), f32),
            shape((parts, *pieces[1:]), bf16),
            shape((count, width), bf16),
            shape((count, width), bf16),
        ),
        in_specs=[pl.BlockSpec(memory_space=pltpu.SMEM), vmem, hbm, hbm, hbm, hbm]
        + [vmem] * 3,
        out_specs=(vmem, vmem, vmem, hbm, vmem),
        scratch_shapes=[
            pltpu.VMEM((count, width), bf16),
            pltpu.VMEM((count, width), bf16),
            pltpu.VMEM((share, width), f32),
            pltpu.VMEM((parts, width, step), bf16),
            pltpu.VMEM((parts, width, step), bf16),
            pltpu.VMEM((parts, step, width), bf16),
            pltpu.VMEM((width, count), bf16),
            pltpu.VMEM((count, units), bf16),
            pltpu.VMEM((parts, count, step), bf16),
            pltpu.VMEM((parts, count, step), bf16),
            pltpu.VMEM((parts, *pieces), bf16),
            pltpu.VMEM((parts, 2, 5, 6, *pieces[3:]), bf16),
            pltpu.SemaphoreType.DMA((parts, 2, 60)),
            pltpu.SemaphoreType.DMA((1 + 3 * parts,)),
        ]
        + row_scratch(count, share, width),
        compiler_params=params(call_id),
        cost_estimate=pl.CostEstimate(
            flops=16 * count * width * units, bytes_accessed=32 * 2**20, transcendentals=0
        ),
    )(lengths, rows, given, w_gate, w_up, w_down, middle, inverse, gain)


def back_kernel(
    lengths_ref,
    grad_ref,
    w_out_ref,
    attended_ref,
    logits_ref,
    query_ref,
    lse_ref,
    query_raw_ref,
    key_raw_ref,
    gain_query_ref,
    gain_key_ref,
    inner_ref,
    outer_ref,
    gain_ref,
    grad_middle_ref,
    gated_ref,
    ffn_gain_ref,
    shares_ref,
    w_gate_ref,
    kv_hbm,
    normed_hbm,
    tokens_hbm,
    w_query_hbm,
    w_key_hbm,
    w_value_hbm,
    tokens_out,
    sums_out,
    near_out,
    pair_out,
    small_out,
    kv,
    grads,
    recv,
    grad_attended,
    shift,
    delta,
    grad_turned,
    ahead,
    grad_logits,
    near_terms,
    near_came,
    near_share,
    pair_terms,
    pair_came,
    pair_share,
    normed,
    base,
    w_query,
    w_key,
    w_value,
    small_own,
    small_came,
    kv_sems,
    near_sems,
    pair_sems,
    gather_sems,
    small_sems,
    load_sems,
    save_sems,
    *row_refs,
):
    ready = greet_sides()
    y, x = plane_place()
    z, core, *_ = group_places()
    share, width = grad_middle_ref.shape
    mine = pl.ds(group_rows(z, core, 0, share), share)
    loads = {}
    for n, (name, source, target) in enumerate(
        (
            ("kv", kv_hbm, kv),
            ("normed", normed_hbm, normed),
            ("base", tokens_hbm.at[mine, :], base),
            ("w_query", w_query_hbm, w_query),
            ("w_key", w_key_hbm, w_key),
            ("w_value", w_value_hbm, w_value),
        )
    ):
        loads[name] = pltpu.make_async_copy(source, target, load_sems.at[n])
        loads[name].start()
    place = y * 4 + x
    buckets = kv.shape[1]
    block, size = kv.shape[3], kv.shape[4]
    heads = w_out_ref.shape[0] // size
    parts = sums_out.shape[0]
    targets = [sums_out.at[n] for n in range(parts)] + [near_out, pair_out]
    sums = [Gather(spot, gather_sems.at[n]) for n, spot in enumerate(targets)]

    def put_share(n, source):
        copy = pltpu.make_async_copy(source, targets[n].at[place], save_sems.at[n])
        copy.start()
        return copy

    puts = [put_share(n, shares_ref.at[n]) for n in range(parts)]

    def earlier_sums(n):
        puts[n].wait()
        yield from gather_task(sums[n])

    def own_weights(n, scatter, share_ref):
        def keep(path, halves):
            for half, value in enumerate(halves):
                share_ref[path, half] = value.astype(bf16)

        yield from scatter_task(scatter, keep)
        put_share(n, share_ref).wait()
        yield from gather_task(sums[n])

    ready()
    beside = in_turn([earlier_sums(0), earlier_sums(1)])

    def advance(steps):
        for _ in range(steps):
            next(beside, None)

    advance(1)
    grad_gated = lax.dot_general(
        grad_ref[...], w_out_ref[...], ROW_CONTRACT, preferred_element_type=f32
    )
    gates = jax.nn.sigmoid(logits_ref[...])
    for h in range(heads):
        cols = slice(h * size, (h + 1) * size)
        gate = gates[:, h : h + 1]
        part, attended = grad_gated[:, cols], attended_ref[:, cols]
        along = jnp.sum(part * attended, axis=1, keepdims=True)
        grad_logits[:, h : h + 1] = (along * gate * (1.0 - gate)).astype(bf16)
        low = (part * gate).astype(bf16)
        inner = jnp.sum(low.astype(f32) * attended, axis=1, keepdims=True)
        wide = jnp.broadcast_to(inner, (inner.shape[0], size))
        for b in range(buckets):
            rows = slice(b * block, (b + 1) * block)
            at = slice(h * block, (h + 1) * block)
            grad_attended[b, at, :] = low[rows]
            delta[b, :, at] = wide[rows].T[:8]
    for b in range(buckets):
        shift[b] = lse_ref[b].T[:8]
    grad_turned[...] = jnp.zeros_like(grad_turned)
    advance(2)
    loads["kv"].wait()
    scale = size**-0.5

    def back(source, b, causal):
        keys, vals = kv[source, b, 0], kv[source, b, 1]
        query = query_ref[b]
        given = grad_attended[b]
        scores = lax.dot_general(keys, query, ROW_CONTRACT, preferred_element_type=f32)
        weights = jnp.exp2(scores * (scale * LOG2_E) - shift[b, 0:1, :])
        if causal:
            spot = lax.broadcasted_iota(jnp.int32, (block, heads * block), 1) % block
            key_spot = lax.broadcasted_iota(jnp.int32, (block, heads * block), 0)
            weights = jnp.where(key_spot <= spot, weights, 0.0)
        grad_weights = lax.dot_general(vals, given, ROW_CONTRACT, preferred_element_type=f32)
        grad_scores = (weights * (grad_weights - delta[b, 0:1, :])).astype(bf16)
        grad_keys = jnp.dot(grad_scores, query, preferred_element_type=f32) * scale
        grad_vals = jnp.dot(weights.astype(bf16), given, preferred_element_type=f32)
        grads[source, b, 0] = grad_keys.astype(bf16)
        grads[source, b, 1] = grad_vals.astype(bf16)
        grad_turned[b] += lax.dot_general(
            keys, grad_scores, COL_CONTRACT, preferred_element_type=f32
        )

    def visit(source, b):
        @pl.when(source < place)
        def _():
            back(source, b, False)

        @pl.when(source > place)
        def _():
            grads[source, b] = jnp.zeros_like(grads[source, b])

    scatter = Scatter(grads, recv, kv_sems)
    order = (2, 1, 3, 0)
    for ring in order:
        for path in (0, 1):

            def one(n, carry):
                visit(place_at(path, ring, choose(n, [2, 1, 3])), path)
                return carry

            lax.fori_loop(0, 3, one, 0)
            scatter.start(path, ring)
        advance(1 if ring == 2 else 3)
        if ring != 2:
            previous = order[order.index(ring) - 1]
            for path in (0, 1):
                scatter.forward(path, previous)
    for path in (0, 1):

        def own(n, carry):
            visit(place_at(path, choose(n, [2, 1, 3]), 0), path)
            return carry

        lax.fori_loop(0, 3, own, 0)
    for path in (0, 1):
        scatter.forward(path, 0)
    advance(4)
    for ring in (2, 1, 3):
        for path in (0, 1):
            scatter.settle(path, ring)
    for path in (0, 1):
        scatter.start(path, 4)
    for b in range(buckets):
        back(place, b, True)
    advance(4)
    for path in (0, 1):
        scatter.settle(path, 0)
        scatter.forward(path, 4)
    cosine, sine = local_angles(inner_ref, outer_ref, place)

    def turn_back(values):
        return values * cosine - turned(values) * sine

    gain_sum = jnp.zeros((1, size), f32)
    for b in range(buckets):
        rows = slice(b * block, (b + 1) * block)
        grad_rot = grad_turned[b].T * scale
        for h in range(heads):
            cols = slice(h * size, (h + 1) * size)
            unit, inverse = unit_scale(query_raw_ref[rows, cols])
            straight = turn_back(grad_rot[h * block : (h + 1) * block])
            gain_sum += jnp.sum(straight * unit, axis=0, keepdims=True)
            ahead[rows, cols] = norm_back(
                straight * gain_query_ref[...], unit, inverse
            ).astype(bf16)
    query_gain = gain_sum
    loads["normed"].wait()
    near = heads * size

    def near_weights(n, carry):
        cols = pl.ds(pl.multiple_of(n * 256, 256), 256)
        block = lax.dot_general(
            normed[:, cols], ahead[:, :near], COL_CONTRACT, preferred_element_type=f32
        )
        near_terms[pl.ds(n * 2, 2), :, :, :, 0:near] = block.astype(bf16).reshape(
            2, 2, 2, 32, near
        )
        block = lax.dot_general(
            gated_ref[...], grad_ref[:, cols], COL_CONTRACT, preferred_element_type=f32
        ).astype(bf16)
        place_sides(near_terms, n, block, near)
        return carry

    for n in range(4):
        lax.fori_loop(2 * n, 2 * n + 2, near_weights, 0)
        advance(2)
    near_scatter = Scatter(near_terms, near_came, near_sems)
    near_task = own_weights(parts, near_scatter, near_share)
    next(near_task)
    gain_sum = jnp.zeros((1, size), f32)
    spots = place * block + lax.broadcasted_iota(jnp.int32, (block, size), 0)
    for b in range(buckets):
        rows = slice(b * block, (b + 1) * block)
        live = spots < lengths_ref[b]
        grad_keys, grad_vals = scatter.total(b, 4)
        ahead[rows, (heads + 1) * size :] = jnp.where(live, grad_vals, 0.0).astype(bf16)
        unit, inverse = unit_scale(key_raw_ref[rows, :])
        straight = turn_back(jnp.where(live, grad_keys, 0.0))
        gain_sum += jnp.sum(straight * unit, axis=0, keepdims=True)
        ahead[rows, heads * size : (heads + 1) * size] = norm_back(
            straight * gain_key_ref[...], unit, inverse
        ).astype(bf16)
    key_gain = gain_sum
    split = ahead.shape[1]

    def pair_weights(n, carry):
        cols = pl.ds(pl.multiple_of(n * 256, 256), 256)
        block = lax.dot_general(
            normed[:, cols], ahead[:, near:], COL_CONTRACT, preferred_element_type=f32
        )
        pair_terms[pl.ds(n * 2, 2)] = block.astype(bf16).reshape(2, 2, 2, 32, split - near)
        return carry

    lax.fori_loop(0, width // 256, pair_weights, 0)
    pair_scatter = Scatter(pair_terms, pair_came, pair_sems)
    pair_task = own_weights(parts + 1, pair_scatter, pair_share)
    state = {}

    def token_rows():
        for name in ("w_query", "w_key", "w_value", "base"):
            loads[name].wait()
        cuts = (0, heads * size, (heads + 1) * size, split)
        lefts = [ahead.at[:, a:b] for a, b in zip(cuts, cuts[1:])]
        product = group_product(
            (*lefts, grad_logits),
            (w_query, w_key, w_value, w_gate_ref),
            (True, True, True, False),
            share,
            width,
        )

        def finish(total):
            unit, inverse = unit_scale(base[...].astype(f32))
            state["gain"] = jnp.sum(total * unit, axis=0, keepdims=True)
            back_rows = norm_back(total * gain_ref[...], unit, inverse)
            return (grad_middle_ref[...] + back_rows).astype(bf16)

        yield from exchange_task(product, finish, share, ready, tokens_out, row_refs)

    def small_sums():
        gates = lax.dot_general(
            grad_logits[...], normed[...], COL_CONTRACT, preferred_element_type=f32
        )
        while "gain" not in state:
            yield
        filler = jnp.zeros((1, width - 2 * size), f32)
        both = jnp.concatenate([query_gain, key_gain, filler], axis=1)
        unused = jnp.zeros((5 - gates.shape[0], width), f32)
        value = jnp.concatenate([ffn_gain_ref[...], state["gain"], both, gates, unused], axis=0)
        small_out[...] = yield from spread_small(value, small_own, small_came, small_sems)

    tasks = [pair_task, token_rows(), near_task, beside, earlier_sums(2), small_sums()]
    run_together(tasks)
    scatter.finish()
    near_scatter.finish()
    pair_scatter.finish()
    for gather in sums:
        gather.finish()


def attend_back(call_id, small_operands, large_operands, lengths, query, kv, shares):
    places, buckets, _, block, size = kv.shape
    rows = buckets * block
    heads = query.shape[1] // block
    width = small_operands[0].shape[1]
    share = rows // 8
    vmem = pl.BlockSpec(memory_space=pltpu.VMEM)
    hbm = pl.BlockSpec(memory_space=pl.ANY)
    shape = jax.ShapeDtypeStruct
    parts = shares.shape[0]
    ahead = (heads + 2) * size
    near = (places, *shares.shape[1:4], 2 * heads * size)
    pair = (places, *shares.shape[1:4], 2 * size)
    dma = pltpu.SemaphoreType.DMA
    return pl.pallas_call(
        back_kernel,
        name="attend_back",
        out_shape=(
            shape((rows, width), bf16),
            shape((parts, places, *shares.shape[1:]), bf16),
            shape(near, bf16),
            shape(pair, bf16),
            shape((8, width), f32),
        ),
        in_specs=[pl.BlockSpec(memory_space=pltpu.SMEM)]
        + [vmem] * len(small_operands)
        + [hbm] * len(large_operands),
        out_specs=(hbm,) * 4 + (vmem,),
        scratch_shapes=[
            pltpu.VMEM(kv.shape, bf16),
            pltpu.VMEM(kv.shape, bf16),
            pltpu.VMEM((2, 5, 6, block, size), bf16),
            pltpu.VMEM((buckets, heads * block, size), bf16),
            pltpu.VMEM((buckets, 8, heads * block), f32),
            pltpu.VMEM((buckets, 8, heads * block), f32),
            pltpu.VMEM((buckets, size, heads * block), f32),
            pltpu.VMEM((rows, ahead), bf16),
            pltpu.VMEM((rows, heads), bf16),
            pltpu.VMEM(near, bf16),
            pltpu.VMEM((2, 5, 6, *near[3:]), bf16),
            pltpu.VMEM(near[1:], bf16),
            pltpu.VMEM(pair, bf16),
            pltpu.VMEM((2, 5, 6, *pair[3:]), bf16),
            pltpu.VMEM(pair[1:], bf16),
            pltpu.VMEM((rows, width), bf16),
            pltpu.VMEM((share, width), bf16),
            pltpu.VMEM((width, heads * size), bf16),
            pltpu.VMEM((width, size), bf16),
            pltpu.VMEM((width, size), bf16),
            pltpu.VMEM((8, width), f32),
            pltpu.VMEM((10, 8, width), f32),
            dma((2, 60)),
            dma((2, 60)),
            dma((2, 60)),
            dma((parts + 2, 2, 40)),
            dma((2, 10)),
            dma((6,)),
            dma((parts + 2,)),
        ]
        + row_scratch(rows, share, width),
        compiler_params=params(call_id),
        cost_estimate=pl.CostEstimate(
            flops=12 * 2**30, bytes_accessed=2**26, transcendentals=2**22
        ),
    )(lengths, *small_operands, *large_operands)


def scatter_task(scatter, finish):
    order = (2, 1, 3, 0)
    both = (0, 1)
    for ring in order:
        for path in both:
            scatter.start(path, ring)
    yield
    for ring in order:
        for path in both:
            scatter.forward(path, ring)
    yield
    for ring in order:
        for path in both:
            scatter.settle(path, ring)
    for path in both:
        scatter.start(path, 4)
    yield
    for path in both:
        scatter.forward(path, 4)
    yield
    for path in both:
        finish(path, scatter.total(path, 4))


def gather_task(gather):
    gather.start()
    for number in range(len(STAGES)):
        yield
        gather.stage(number)


def spread_small(value, own, came, sems):
    first = lax.broadcasted_iota(jnp.int32, value.shape, 0) < 3
    slot = 0
    for axis in ("grp_1", "grp_0", "seq_1", "seq_0"):
        size = lax.axis_size(axis)
        at = lax.axis_index(axis)
        own[...] = value
        copies = []
        for far in range(1, size):
            to = {axis: lax.rem(at + far, size)}
            copies.append(send(own, came.at[slot], sems, slot, to))
            slot += 1
        yield
        for n, copy in enumerate(copies):
            copy.wait_recv()
            part = came[slot - len(copies) + n]
            value = value + (part if axis in SEQ else jnp.where(first, part, 0.0))
        for copy in copies:
            copy.wait_send()
    return value


def spread_kernel(
    feed_ref,
    near_ref,
    pair_ref,
    small_ref,
    gate_out,
    up_out,
    down_out,
    query_out,
    key_out,
    value_out,
    out_out,
    norm_two_out,
    norm_one_out,
    norm_query_out,
    norm_key_out,
    logits_out,
):
    step = feed_ref.shape[-1] // 3
    for n in range(3):
        cols = slice(n * step, (n + 1) * step)
        part = feed_ref[n, 0].reshape(128, 3 * step).astype(f32)
        gate_out[:, cols] = part[:, :step]
        up_out[:, cols] = part[:, step : 2 * step]
        down_out[cols, :] = unplaced(part[:, 2 * step :])
    near = query_out.shape[1]
    part = near_ref[0].reshape(128, 2 * near).astype(f32)
    query_out[...] = part[:, :near]
    out_out[...] = unplaced(part[:, near:])
    part = pair_ref[0].reshape(128, 2 * key_out.shape[1]).astype(f32)
    key_out[...] = part[:, : key_out.shape[1]]
    value_out[...] = part[:, key_out.shape[1] :]
    size = norm_query_out.shape[1]
    norm_two_out[...] = small_ref[0:1]
    norm_one_out[...] = small_ref[1:2]
    norm_query_out[...] = small_ref[2:3, :size]
    norm_key_out[...] = small_ref[2:3, size : 2 * size]
    logits_out[...] = small_ref[3 : 3 + logits_out.shape[0]]


def unplaced(part):
    pairs = part.reshape(4, 32, 256)
    return jnp.stack([pairs[:, :, :128], pairs[:, :, 128:]], axis=1).reshape(256, 128)


def spread(parts, near, pair, small, units, query_cols, key_cols, heads):
    count, places = parts.shape[:2]
    width = small.shape[1]
    block = width // places
    shape = jax.ShapeDtypeStruct

    def strip(cols):
        return pl.BlockSpec((block, cols), lambda s: (s, 0))

    def fixed(rows, cols):
        return pl.BlockSpec((rows, cols), lambda s: (0, 0))

    def column(rows):
        return pl.BlockSpec((rows, block), lambda s: (0, s))

    return pl.pallas_call(
        spread_kernel,
        name="spread",
        grid=(places,),
        in_specs=[
            pl.BlockSpec((count, 1, *parts.shape[2:]), lambda s: (0, s, 0, 0, 0, 0)),
            pl.BlockSpec((1, *near.shape[1:]), lambda s: (s, 0, 0, 0, 0)),
            pl.BlockSpec((1, *pair.shape[1:]), lambda s: (s, 0, 0, 0, 0)),
            fixed(*small.shape),
        ],
        out_specs=(
            strip(units),
            strip(units),
            column(units),
            strip(query_cols),
            strip(key_cols),
            strip(key_cols),
            column(query_cols),
            fixed(1, width),
            fixed(1, width),
            fixed(1, key_cols),
            fixed(1, key_cols),
            fixed(heads, width),
        ),
        out_shape=(
            shape((width, units), f32),
            shape((width, units), f32),
            shape((units, width), f32),
            shape((width, query_cols), f32),
            shape((width, key_cols), f32),
            shape((width, key_cols), f32),
            shape((query_cols, width), f32),
            shape((1, width), f32),
            shape((1, width), f32),
            shape((1, key_cols), f32),
            shape((1, key_cols), f32),
            shape((heads, width), f32),
        ),
        compiler_params=pltpu.CompilerParams(vmem_limit_bytes=VMEM_LIMIT),
        cost_estimate=pl.CostEstimate(flops=0, bytes_accessed=36 * 2**20, transcendentals=0),
    )(parts, near, pair, small)


def local(
    tokens,
    lengths,
    norm_attn,
    w_query,
    w_key,
    w_value,
    w_gate,
    norm_query,
    norm_key,
    w_out,
    norm_ffn,
    w_ffn_gate,
    w_ffn_up,
    w_down,
    cotangent,
):
    buckets, per_device, model_width = tokens.shape
    head_count = w_gate.shape[1]
    head_size = norm_query.shape[0]
    total_rows = buckets * per_device
    share_rows = total_rows // lax.axis_size(GRP)
    flat = tokens.reshape(total_rows, model_width)
    tables = angle_tables(per_device, head_size, lax.axis_size(SEQ))
    gains = (norm_query.reshape(1, -1), norm_key.reshape(1, -1))
    gain_one = norm_attn.reshape(1, -1)
    gain_two = norm_ffn.reshape(1, -1)
    gate_rows = w_gate.T
    (
        normed,
        query_raw,
        key_raw,
        logits,
        query_low,
        pairs,
        attended,
        lse,
        gated,
        middle,
        inverse_two,
        normed_two,
    ) = forward(
        1,
        lengths,
        flat,
        gain_one,
        w_query,
        w_key,
        w_value,
        gate_rows,
        gains,
        tables,
        w_out,
        gain_two,
    )
    grad_middle, ffn_gain, shares, grad_attn_low, feed_rows = feed_forward(
        2,
        lengths,
        normed_two,
        cotangent.reshape(total_rows, model_width),
        w_ffn_gate,
        w_ffn_up,
        w_down,
        middle,
        inverse_two,
        gain_two,
    )
    mixed = lax.psum(feed_rows, GRP)
    grad_tokens, feed_sums, near_sums, pair_sums, small = attend_back(
        3,
        (
            grad_attn_low,
            w_out,
            attended,
            logits,
            query_low,
            lse,
            query_raw,
            key_raw,
            *gains,
            *tables,
            gain_one,
            grad_middle,
            gated,
            ffn_gain,
            shares,
            gate_rows,
        ),
        (pairs, normed, flat, w_query, w_key, w_value),
        lengths,
        query_low,
        pairs,
        shares,
    )
    (
        grad_gate,
        grad_up,
        grad_down,
        grad_w_query,
        grad_w_key,
        grad_w_value,
        grad_w_out,
        grad_norm_ffn,
        grad_norm_attn,
        grad_norm_query,
        grad_norm_key,
        grad_w_gate,
    ) = spread(
        feed_sums,
        near_sums,
        pair_sums,
        small,
        w_down.shape[0],
        w_query.shape[1],
        w_key.shape[1],
        head_count,
    )
    return (
        mixed.reshape(buckets, per_device, model_width),
        grad_tokens.reshape(buckets, per_device, model_width),
        grad_norm_attn.reshape(-1),
        grad_w_query,
        grad_w_key,
        grad_w_value,
        grad_w_gate.T,
        grad_norm_query.reshape(-1),
        grad_norm_key.reshape(-1),
        grad_w_out,
        grad_norm_ffn.reshape(-1),
        grad_gate,
        grad_up,
        grad_down,
    )


def solution(mesh):
    finer = Mesh(mesh.devices.reshape(4, 4, 4, 2), ("seq_0", "seq_1", "grp_0", "grp_1"))
    return jax.shard_map(
        local,
        mesh=finer,
        in_specs=(
            P(None, SEQ, None),
            P(),
            P(),
            P(None, GRP),
            P(None, GRP),
            P(None, GRP),
            P(None, GRP),
            P(),
            P(),
            P(GRP, None),
            P(),
            P(None, GRP),
            P(None, GRP),
            P(GRP, None),
            P(None, SEQ, None),
        ),
        out_specs=(
            P(None, SEQ, None),
            P(None, SEQ, None),
            P(),
            P(None, GRP),
            P(None, GRP),
            P(None, GRP),
            P(None, GRP),
            P(),
            P(),
            P(GRP, None),
            P(),
            P(None, GRP),
            P(None, GRP),
            P(GRP, None),
        ),
        check_vma=False,
    )
```

```python
import jax
import jax.numpy as jnp
import numpy as np
from jax import lax
from jax.experimental import pallas as pl
from jax.experimental.pallas import tpu as pltpu
from jax.sharding import Mesh
from jax.sharding import PartitionSpec as P

GRP = ("grp_0", "grp_1")
SEQ = ("seq_0", "seq_1")
MESH = pl.DeviceIdType.MESH
VMEM_LIMIT = 60 * 2**20

f32 = jnp.float32
bf16 = jnp.bfloat16


epsilon = 1e-06
rope_base = 1000000.0


def unit_scale(values):
    inverse = lax.rsqrt(jnp.mean(values * values, axis=-1, keepdims=True) + epsilon)
    return (values * inverse, inverse)


def norm_back(grad_unit, unit, inverse):
    return inverse * (grad_unit - unit * jnp.mean(grad_unit * unit, axis=-1, keepdims=True))


ROW_CONTRACT = (((1,), (1,)), ((), ()))
COL_CONTRACT = (((0,), (0,)), ((), ()))


def send(source, target, sems, slot, to):
    copy = pltpu.make_async_remote_copy(
        src_ref=source,
        dst_ref=target,
        send_sem=sems.at[0, slot],
        recv_sem=sems.at[1, slot],
        device_id=to,
        device_id_type=MESH,
    )
    copy.start()
    return copy


def group_places():
    z = lax.axis_index("grp_0")
    core = lax.axis_index("grp_1")
    ring = lax.axis_size("grp_0")
    above = {"grp_0": lax.rem(z + 1, ring)}
    below = {"grp_0": lax.rem(z + ring - 1, ring)}
    twin = {"grp_1": 1 - core}
    return z, core, above, below, twin


def greet(places):
    barrier = pltpu.get_barrier_semaphore()
    for place in places:
        pl.semaphore_signal(barrier, inc=1, device_id=place, device_id_type=MESH)
    return lambda: pl.semaphore_wait(barrier, len(places))


def group_rows(z, core, far, share):
    return pl.multiple_of((lax.rem(z + far, 4) * 2 + core) * share, share)


FAR = (2, 1, 3, 0)


def run_together(tasks, urgent=None, pace=1):
    tasks = list(tasks)
    while tasks:
        for task in list(tasks):
            if urgent is not None:
                for _ in range(pace):
                    next(urgent, None)
            if next(task, tasks) is tasks:
                tasks.remove(task)
    for _ in urgent or ():
        pass


def in_turn(tasks):
    tasks = list(tasks)
    while tasks:
        for task in list(tasks):
            try:
                next(task)
            except StopIteration:
                tasks.remove(task)
            yield


def sum_rows(product, share, ready, scratch):
    mine, twin_out, twin_in, low, ring, twin_sems, ring_sems = scratch
    z, core, above, below, twin = group_places()
    half = share // 2
    top, bottom = pl.ds(0, half), pl.ds(half, half)

    def put_twin(cols, block):
        twin_out[:, :, cols] = block.astype(bf16)

    def put_mine(cols, block):
        mine[:, :, cols] = block

    product(1 - core, put_twin)
    ready()
    pairs = [send(twin_out.at[k], twin_in.at[k], twin_sems, k, twin) for k in range(4)]
    product(core, put_mine)

    def joined(k, rows):
        return mine[k, rows, :] + twin_in[k, rows, :].astype(f32)

    yield
    pairs[0].wait_recv()
    low[0] = joined(0, pl.ds(0, share)).astype(bf16)
    steps = [
        send(low.at[0, top], ring.at[0], ring_sems, 0, above),
        send(low.at[0, bottom], ring.at[1], ring_sems, 1, below),
    ]
    pairs[1].wait_recv()
    low[1, bottom, :] = joined(1, bottom).astype(bf16)
    steps.append(send(low.at[1, bottom], ring.at[2], ring_sems, 2, above))
    pairs[2].wait_recv()
    low[2, top, :] = joined(2, top).astype(bf16)
    steps.append(send(low.at[2, top], ring.at[3], ring_sems, 3, below))
    yield
    steps[0].wait_recv()
    low[1, top, :] = (joined(1, top) + ring[0].astype(f32)).astype(bf16)
    steps.append(send(low.at[1, top], ring.at[4], ring_sems, 4, above))
    yield
    steps[1].wait_recv()
    low[2, bottom, :] = (joined(2, bottom) + ring[1].astype(f32)).astype(bf16)
    steps.append(send(low.at[2, bottom], ring.at[5], ring_sems, 5, below))
    pairs[3].wait_recv()
    yield
    for step in steps[2:]:
        step.wait_recv()
    total = jnp.concatenate(
        [
            joined(3, top) + ring[3].astype(f32) + ring[4].astype(f32),
            joined(3, bottom) + ring[2].astype(f32) + ring[5].astype(f32),
        ],
        axis=0,
    )
    return total, pairs + steps


def join_rows(whole, share, twin_sems, ring_sems):
    z, core, above, below, twin = group_places()
    half = share // 2

    def part(far, side):
        start = group_rows(z, core, far, share)
        return whole.at[pl.ds(pl.multiple_of(start + side * half, half), half), :]

    def hand(far, side, sems, slot, to):
        block = part(far, side)
        return send(block, block, sems, slot, to)

    own = whole.at[pl.ds(group_rows(z, core, 0, share), share), :]
    up = [hand(0, 0, ring_sems, 0, above), hand(0, 1, ring_sems, 1, above)]
    down = [hand(0, 1, ring_sems, 2, below), hand(0, 0, ring_sems, 3, below)]
    across = [send(own, own, twin_sems, 0, twin)]
    yield
    up[0].wait_recv()
    up.append(hand(3, 0, ring_sems, 4, above))
    across.append(hand(3, 0, twin_sems, 1, twin))
    yield
    down[0].wait_recv()
    down.append(hand(1, 1, ring_sems, 5, below))
    across.append(hand(1, 1, twin_sems, 2, twin))
    yield
    up[1].wait_recv()
    across.append(hand(3, 1, twin_sems, 3, twin))
    down[1].wait_recv()
    across.append(hand(1, 0, twin_sems, 4, twin))
    yield
    up[2].wait_recv()
    across.append(hand(2, 0, twin_sems, 5, twin))
    down[2].wait_recv()
    across.append(hand(2, 1, twin_sems, 6, twin))
    yield
    for copy in across:
        copy.wait_recv()
    for copy in up + down + across:
        copy.wait_send()


def row_scratch(rows, share, width):
    return [
        pltpu.VMEM((4, share, width), f32),
        pltpu.VMEM((4, share, width), bf16),
        pltpu.VMEM((4, share, width), bf16),
        pltpu.VMEM((3, share, width), bf16),
        pltpu.VMEM((6, share // 2, width), bf16),
        pltpu.SemaphoreType.DMA((2, 4)),
        pltpu.SemaphoreType.DMA((2, 6)),
        pltpu.VMEM((rows, width), bf16),
        pltpu.SemaphoreType.DMA((2, 7)),
        pltpu.SemaphoreType.DMA((2, 6)),
        pltpu.SemaphoreType.DMA((1,)),
    ]


def group_product(lefts, rights, across, share, width):
    z = lax.axis_index("grp_0")
    step = 512

    def product(core, put):
        picked = []
        for left in lefts:
            blocks = [left[pl.ds(group_rows(z, core, far, share), share), :] for far in FAR]
            picked.append(jnp.concatenate(blocks, axis=0))
        for at in range(0, width, step):
            cols = pl.ds(at, step)
            total = None
            for left, right, flip in zip(picked, rights, across):
                if flip:
                    term = lax.dot_general(
                        left, right[cols, :], ROW_CONTRACT, preferred_element_type=f32
                    )
                else:
                    term = jnp.dot(left, right[:, cols], preferred_element_type=f32)
                total = term if total is None else total + term
            put(cols, total.reshape(4, share, step))

    return product


LOG2_E = 1.4426950408889634
STAGES = (
    ((1, 0), (3, 0), (0, 1), (0, 3)),
    ((2, 0), (0, 2)),
    ((1, 1), (1, 3), (3, 1), (3, 3)),
    ((1, 2), (3, 2), (2, 1), (2, 3)),
    ((2, 2),),
)


def angle_tables(block, size, count):
    half = size // 2
    freq = rope_base ** (-np.arange(half, dtype=np.float64) * (2.0 / size))
    inner = np.arange(block)[:, None] * freq[None, :]
    outer = (np.arange(count) * block)[:, None] * freq[None, :]

    def table(angle):
        sine = np.sin(angle)
        cosine = np.cos(angle)
        both = np.stack(
            [
                np.concatenate([cosine, cosine], axis=1),
                np.concatenate([-sine, sine], axis=1),
            ]
        )
        return both.astype(np.float32)

    return table(inner), table(outer)


def local_angles(inner, outer, place):
    cos_in, sin_in = inner[0], inner[1]
    cos_out = outer[0, pl.ds(place, 1), :]
    sin_out = outer[1, pl.ds(place, 1), :]
    return cos_in * cos_out - sin_in * sin_out, sin_in * cos_out + cos_in * sin_out


def turned(values):
    return pltpu.roll(values, values.shape[-1] // 2, axis=values.ndim - 1)


def plane_place():
    return lax.axis_index("seq_0"), lax.axis_index("seq_1")


def plane_sides(axis):
    at = lax.axis_index(axis)
    size = lax.axis_size(axis)
    return {axis: lax.rem(at + 1, size)}, {axis: lax.rem(at + size - 1, size)}


AXES = (("seq_1", "seq_0"), ("seq_0", "seq_1"))


def place_at(path, first, second):
    y, x = plane_place()
    dx, dy = (first, second) if path == 0 else (second, first)
    return lax.rem(y + dy, 4) * 4 + lax.rem(x + dx, 4)


def pass_start(block, axis, sems, slot):
    up, down = plane_sides(axis)
    return [send(block, block, sems, slot, up), send(block, block, sems, slot + 1, down)]


def pass_on(copies, before, after, axis, sems, slot):
    up, down = plane_sides(axis)
    copies[0].wait_recv()
    copies.append(send(before.at[0], before.at[0], sems, slot + 2, up))
    copies[1].wait_recv()
    copies.append(send(after.at[1], after.at[1], sems, slot + 3, down))


def pass_end(copies):
    copies[2].wait_recv()
    copies[3].wait_recv()


class Gather:
    def __init__(self, buffer, sems):
        self.buffer, self.sems = buffer, sems
        self.rings = [{}, {}]

    def block(self, path, first, second):
        return self.buffer.at[place_at(path, first, second), path]

    def slot(self, path, ring):
        return path * 20 + (4 if ring == "first" else ring) * 4

    def begin(self, path, ring):
        axis = AXES[path][0] if ring == "first" else AXES[path][1]
        block = self.block(path, 0 if ring == "first" else ring, 0)
        self.rings[path][ring] = pass_start(block, axis, self.sems, self.slot(path, ring))

    def forward(self, path, ring):
        if ring == "first":
            axis, before, after = AXES[path][0], self.block(path, 3, 0), self.block(path, 1, 0)
        else:
            axis = AXES[path][1]
            before, after = self.block(path, ring, 3), self.block(path, ring, 1)
        pass_on(self.rings[path][ring], before, after, axis, self.sems, self.slot(path, ring))

    def end(self, path, ring):
        pass_end(self.rings[path][ring])

    def start(self):
        for path in (0, 1):
            self.begin(path, "first")
        for path in (0, 1):
            self.begin(path, 0)

    def stage(self, number):
        for path in (0, 1):
            if number == 0:
                self.forward(path, "first")
                self.begin(path, 1)
                self.begin(path, 3)
                self.forward(path, 0)
            elif number == 1:
                self.end(path, "first")
                self.begin(path, 2)
                self.end(path, 0)
            elif number == 2:
                self.forward(path, 1)
                self.forward(path, 3)
            elif number == 3:
                self.end(path, 1)
                self.end(path, 3)
                self.forward(path, 2)
            else:
                self.end(path, 2)

    def finish(self):
        for rings in self.rings:
            for copies in rings.values():
                for copy in copies:
                    copy.wait_send()


class Scatter:
    def __init__(self, buffer, recv, sems):
        self.buffer, self.recv, self.sems = buffer, recv, sems
        self.copies = {}

    def block(self, path, ring, step):
        if ring == 4:
            return self.buffer.at[place_at(path, step, 0), path]
        return self.buffer.at[place_at(path, ring, step), path]

    def sides(self, path, ring):
        return plane_sides(AXES[path][0] if ring == 4 else AXES[path][1])

    def push(self, path, ring, half_ref, slot, to):
        at = (path * 5 + ring) * 6 + slot
        copy = send(half_ref, self.recv.at[path, ring, slot], self.sems, at, to)
        self.copies.setdefault((path, ring), []).append(copy)

    def start(self, path, ring):
        up, down = self.sides(path, ring)
        far = self.block(path, ring, 2)
        self.push(path, ring, far.at[0], 0, up)
        self.push(path, ring, far.at[1], 1, down)
        self.push(path, ring, self.block(path, ring, 1).at[1], 2, up)
        self.push(path, ring, self.block(path, ring, 3).at[0], 3, down)

    def forward(self, path, ring):
        up, down = self.sides(path, ring)
        for slot, step, half, to in ((0, 1, 0, up), (1, 3, 1, down)):
            self.copies[path, ring][slot].wait_recv()
            part = self.block(path, ring, step).at[half]
            came = self.recv[path, ring, slot]
            part[...] = (part[...].astype(f32) + came.astype(f32)).astype(bf16)
            self.push(path, ring, part, slot + 4, to)

    def total(self, path, ring):
        for copy in self.copies[path, ring][2:]:
            copy.wait_recv()
        own = self.block(path, ring, 0)
        out = []
        for half, slots in ((0, (3, 4)), (1, (2, 5))):
            value = own[half].astype(f32)
            for slot in slots:
                value = value + self.recv[path, ring, slot].astype(f32)
            out.append(value)
        return out

    def settle(self, path, ring):
        own = self.block(path, ring, 0)
        for half, value in enumerate(self.total(path, ring)):
            own[half] = value.astype(bf16)

    def finish(self):
        for copies in self.copies.values():
            for copy in copies:
                copy.wait_send()


def greet_plane():
    places = [*plane_sides("seq_0"), *plane_sides("seq_1")]
    return greet(places)


def choose(index, options):
    value = options[-1]
    for n in range(len(options) - 2, -1, -1):
        value = jnp.where(index == n, options[n], value)
    return value


def once(action):
    done = []

    def call():
        if not done:
            done.append(True)
            action()

    return call


def greet_sides():
    z, core, above, below, twin = group_places()
    places = [*plane_sides("seq_0"), *plane_sides("seq_1"), above, below, twin]
    return once(greet(places))


def exchange_task(product, finish, share, ready, out, scratch):
    z, core, *_ = group_places()
    total, copies = yield from sum_rows(product, share, ready, scratch[:7])
    whole, twin_sems, ring_sems, out_sem = scratch[7:11]
    whole[pl.ds(group_rows(z, core, 0, share), share), :] = finish(total)
    yield from join_rows(whole, share, twin_sems, ring_sems)
    done = pltpu.make_async_copy(whole, out, out_sem.at[0])
    done.start()
    for copy in copies:
        copy.wait_send()
    yield
    done.wait()


def forward_kernel(
    lengths_ref,
    tokens_ref,
    gain_ref,
    w_query_ref,
    w_key_ref,
    w_value_ref,
    w_gate_ref,
    gain_query_ref,
    gain_key_ref,
    inner_ref,
    outer_ref,
    w_out_ref,
    gain_two_ref,
    given_hbm,
    normed_out,
    query_raw_out,
    key_raw_out,
    logits_out,
    query_out,
    keys_out,
    attended_out,
    lse_out,
    gated_out,
    middle_out,
    inverse_out,
    normed_two_out,
    seed_out,
    own_seed_out,
    normed,
    kv,
    sums,
    sems,
    out_sems,
    given,
    seed,
    *row_refs,
):
    ready = greet_sides()
    load_given = pltpu.make_async_copy(given_hbm, given, out_sems.at[2])
    load_given.start()
    y, x = plane_place()
    place = y * 4 + x
    rows, width = tokens_ref.shape
    buckets = kv.shape[1]
    block, size = kv.shape[3], kv.shape[4]
    heads = w_query_ref.shape[1] // size
    step = 64

    def norm_rows(n, carry):
        at = pl.ds(pl.multiple_of(n * step, step), step)
        unit, _ = unit_scale(tokens_ref[at, :].astype(f32))
        normed[at, :] = (unit * gain_ref[...]).astype(bf16)
        return carry

    lax.fori_loop(0, rows // step, norm_rows, 0)
    save_normed = pltpu.make_async_copy(normed, normed_out, out_sems.at[0])
    save_normed.start()
    cosine, sine = local_angles(inner_ref, outer_ref, place)

    def turn(values):
        return values * cosine + turned(values) * sine

    key_raw = jnp.dot(normed[...], w_key_ref[...], preferred_element_type=f32)
    value = jnp.dot(normed[...], w_value_ref[...], preferred_element_type=f32)
    key_raw_out[...] = key_raw
    spots = place * block + lax.broadcasted_iota(jnp.int32, (block, size), 0)
    for b in range(buckets):
        live = spots < lengths_ref[b]
        part = slice(b * block, (b + 1) * block)
        unit, _ = unit_scale(key_raw[part])
        kv[place, b, 0] = jnp.where(live, turn(unit * gain_key_ref[...]), 0.0).astype(bf16)
        kv[place, b, 1] = jnp.where(live, value[part], 0.0).astype(bf16)
    gather = Gather(kv, sems)
    ready()
    gather.start()
    query_raw = jnp.dot(normed[...], w_query_ref[...], preferred_element_type=f32)
    query_raw_out[...] = query_raw
    logits_out[...] = lax.dot_general(
        normed[...], w_gate_ref[...], ROW_CONTRACT, preferred_element_type=f32
    )
    for b in range(buckets):
        for h in range(heads):
            part = query_raw[b * block : (b + 1) * block, h * size : (h + 1) * size]
            unit, _ = unit_scale(part)
            query_out[b, h * block : (h + 1) * block, :] = turn(
                unit * gain_query_ref[...]
            ).astype(bf16)
    scale = size**-0.5 * LOG2_E

    def weigh(source, b, causal):
        keys, vals = kv[source, b, 0], kv[source, b, 1]
        scores = lax.dot_general(query_out[b], keys, ROW_CONTRACT, preferred_element_type=f32)
        weights = jnp.exp2(scores * scale)
        if causal:
            spot = lax.broadcasted_iota(jnp.int32, (heads * block, block), 0) % block
            column = lax.broadcasted_iota(jnp.int32, (heads * block, block), 1)
            weights = jnp.where(column <= spot, weights, 0.0)
        there = source * block + lax.broadcasted_iota(jnp.int32, (block, size), 0)
        ones = jnp.where(there < lengths_ref[b], 1.0, 0.0).astype(bf16)
        both = jnp.concatenate([vals, ones], axis=1)
        return jnp.dot(weights.astype(bf16), both, preferred_element_type=f32)

    load_given.wait()
    make_seed(lengths_ref, given, seed, own_seed_out)
    save_seed = pltpu.make_async_copy(seed, seed_out, out_sems.at[3])
    save_seed.start()
    for b in range(buckets):
        sums[b] = weigh(place, b, True)
    for number, offsets in enumerate(STAGES):
        gather.stage(number)

        def one(n, carry):
            which, b = n // buckets, n % buckets
            dx = choose(which, [o[0] for o in offsets])
            dy = choose(which, [o[1] for o in offsets])
            source = lax.rem(y + dy, 4) * 4 + lax.rem(x + dx, 4)

            @pl.when(source < place)
            def _():
                sums[b] = sums[b] + weigh(source, b, False)

            return carry

        lax.fori_loop(0, len(offsets) * buckets, one, 0)
    save_keys = pltpu.make_async_copy(kv, keys_out, out_sems.at[1])
    save_keys.start()
    gates = jax.nn.sigmoid(logits_out[...])
    for b in range(buckets):
        for h in range(heads):
            at = slice(h * block, (h + 1) * block)
            total = sums[b, at, size:]
            attended = sums[b, at, :size] / total
            here = (slice(b * block, (b + 1) * block), slice(h * size, (h + 1) * size))
            attended_out[here] = attended
            lse_out[b, at, :] = jnp.log2(total)
            gated_out[here] = (attended * gates[here[0], h : h + 1]).astype(bf16)
    share = rows // 8
    z, core, *_ = group_places()
    product = group_product((gated_out,), (w_out_ref,), (False,), share, width)

    def finish(total):
        mine = tokens_ref[pl.ds(group_rows(z, core, 0, share), share), :]
        middle = mine.astype(f32) + total
        unit, inverse = unit_scale(middle)
        middle_out[...] = middle
        inverse_out[...] = inverse
        return (unit * gain_two_ref[...]).astype(bf16)

    run_together([exchange_task(product, finish, share, ready, normed_two_out, row_refs)])
    gather.finish()
    save_normed.wait()
    save_keys.wait()
    save_seed.wait()


def params(call_id):
    return pltpu.CompilerParams(
        collective_id=call_id, has_side_effects=True, vmem_limit_bytes=VMEM_LIMIT
    )


def forward(call_id, lengths, tokens, gain, w_query, w_key, w_value, w_gate, gains, tables, w_out, gain_two, given):
    rows, width = tokens.shape
    size = gains[0].shape[1]
    buckets = lengths.shape[0]
    block = rows // buckets
    heads = w_query.shape[1] // size
    places = lax.axis_size(SEQ)
    share = rows // 8
    vmem = pl.BlockSpec(memory_space=pltpu.VMEM)
    hbm = pl.BlockSpec(memory_space=pl.ANY)
    shape = jax.ShapeDtypeStruct
    pairs = (places, buckets, 2, block, size)
    return pl.pallas_call(
        forward_kernel,
        name="forward",
        out_shape=(
            shape((rows, width), bf16),
            shape((rows, heads * size), f32),
            shape((rows, size), f32),
            shape((rows, heads), f32),
            shape((buckets, heads * block, size), bf16),
            shape(pairs, bf16),
            shape((rows, heads * size), f32),
            shape((buckets, heads * block, size), f32),
            shape((rows, heads * size), bf16),
            shape((share, width), f32),
            shape((share, 1), f32),
            shape((rows, width), bf16),
            shape((rows, width), bf16),
            shape((share, width), f32),
        ),
        in_specs=[pl.BlockSpec(memory_space=pltpu.SMEM)] + [vmem] * 12 + [hbm],
        out_specs=(hbm, vmem, vmem, vmem, vmem, hbm, vmem, vmem, vmem, vmem, vmem, hbm, hbm, vmem),
        scratch_shapes=[
            pltpu.VMEM((rows, width), bf16),
            pltpu.VMEM(pairs, bf16),
            pltpu.VMEM((buckets, heads * block, 2 * size), f32),
            pltpu.SemaphoreType.DMA((2, 40)),
            pltpu.SemaphoreType.DMA((4,)),
            pltpu.VMEM((rows, width), bf16),
            pltpu.VMEM((rows, width), bf16),
        ]
        + row_scratch(rows, share, width),
        compiler_params=params(call_id),
        cost_estimate=pl.CostEstimate(
            flops=5 * 2**30, bytes_accessed=16 * 2**20, transcendentals=2**22
        ),
    )(lengths, tokens, gain, w_query, w_key, w_value, w_gate, *gains, *tables, w_out, gain_two, given)


def feed_kernel(
    rows_ref,
    seed_hbm,
    own_seed,
    gate_hbm,
    up_hbm,
    down_hbm,
    middle_ref,
    inverse_ref,
    gain_ref,
    hidden_out,
    grad_middle_out,
    gain_out,
    shares_out,
    rows_out,
    seed,
    gates,
    ups,
    downs,
    rows_across,
    grad_gate,
    grad_up,
    terms,
    came,
    scatter_sems,
    load_sems,
    *row_refs,
):
    rows, width = rows_ref.shape
    count = gates.shape[0]
    step = gates.shape[2]
    load_seed = pltpu.make_async_copy(seed_hbm, seed, load_sems.at[0])
    load_seed.start()
    loads = []
    for n in range(count):
        cols = pl.ds(n * step, step)
        parts = (
            (gate_hbm.at[:, cols], gates.at[n]),
            (up_hbm.at[:, cols], ups.at[n]),
            (down_hbm.at[cols, :], downs.at[n]),
        )
        for k, (source, target) in enumerate(parts):
            loads.append(pltpu.make_async_copy(source, target, load_sems.at[1 + n * 3 + k]))
            loads[-1].start()
    ready = greet_sides()
    share = rows // 8
    rows_across[...] = rows_ref[...].T
    load_seed.wait()
    def activations(n):
        for copy in loads[3 * n : 3 * n + 3]:
            copy.wait()
        cols = slice(n * step, (n + 1) * step)
        gate_pre = jnp.dot(rows_ref[...], gates[n], preferred_element_type=f32)
        up_proj = jnp.dot(rows_ref[...], ups[n], preferred_element_type=f32)
        grad_hidden = lax.dot_general(
            seed[...], downs[n], ROW_CONTRACT, preferred_element_type=f32
        )
        gate_sig = jax.nn.sigmoid(gate_pre)
        silu = gate_pre * gate_sig
        hidden_out[:, cols] = (silu * up_proj).astype(bf16)
        grad_gate[n] = (
            grad_hidden * up_proj * gate_sig * (1.0 + gate_pre * (1.0 - gate_sig))
        ).astype(bf16)
        grad_up[n] = (grad_hidden * silu).astype(bf16)

    def weight_task(n):
        across = hidden_out[:, n * step : (n + 1) * step].T

        def weight_terms(k, carry):
            here = pl.ds(pl.multiple_of(k * 256, 256), 256)
            at = pl.ds(k * 2, 2)
            for side, grad in ((0, grad_gate), (1, grad_up)):
                part = jnp.dot(rows_across[here, :], grad[n], preferred_element_type=f32)
                terms[n, at, :, :, :, side * step : (side + 1) * step] = part.astype(
                    bf16
                ).reshape(2, 2, 2, 32, step)
            part = jnp.dot(across, seed[:, here], preferred_element_type=f32).astype(bf16)
            place_sides(terms.at[n], k, part, 2 * step)
            return carry

        for first in range(0, width // 256, 4):
            lax.fori_loop(first, first + 4, weight_terms, 0)
            yield
        ready()
        scatter = Scatter(terms.at[n], came.at[n], scatter_sems.at[n])
        scatters.append(scatter)

        def keep(path, halves):
            for half, value in enumerate(halves):
                shares_out[n, path, half] = value.astype(bf16)

        yield from scatter_task(scatter, keep)

    def finish_rows(total):
        unit = middle_ref[...] * inverse_ref[...]
        gain_out[...] = jnp.sum(total * unit, axis=0, keepdims=True)
        grad = own_seed[...] + norm_back(total * gain_ref[...], unit, inverse_ref[...])
        grad_middle_out[...] = grad
        return grad.astype(bf16)

    pairs = range(count)
    product = group_product(
        [grad_gate.at[n] for n in pairs] + [grad_up.at[n] for n in pairs],
        [gates.at[n] for n in pairs] + [ups.at[n] for n in pairs],
        (True,) * (2 * count),
        share,
        width,
    )
    scatters = []
    tasks = []
    for n in range(count):
        activations(n)
        tasks.append(weight_task(n))
        for _ in range(3):
            next(tasks[n])
    exchange = exchange_task(product, finish_rows, share, ready, rows_out, row_refs)
    next(exchange)
    next(tasks[0])
    run_together(tasks, exchange, 6)
    for scatter in scatters:
        scatter.finish()


def make_seed(lengths_ref, given_ref, seed, own_seed):
    rows = given_ref.shape[0]
    buckets = lengths_ref.shape[0]
    block = rows // buckets
    share = rows // 8
    y, x = plane_place()
    z, core, *_ = group_places()
    total = lengths_ref[0]
    for b in range(1, buckets):
        total = total + lengths_ref[b]
    places = lax.axis_size("seq_0") * lax.axis_size("seq_1")
    ratio = float(buckets * places * block) / jnp.full((1, 1), total, jnp.int32).astype(f32)

    def weighted(start):
        spots = (
            (y * 4 + x) * block
            + start % block
            + lax.broadcasted_iota(jnp.int32, (share, 1), 0)
        )
        live = (spots < lengths_ref[start // block]).astype(f32)
        at = pl.ds(pl.multiple_of(start, share), share)
        return at, given_ref[at, :].astype(f32) * live * ratio

    own_seed[...] = weighted(group_rows(z, core, 0, share))[1]

    def round_rows(n, carry):
        at, values = weighted(n * share)
        seed[at, :] = values.astype(bf16)
        return carry

    lax.fori_loop(0, 8, round_rows, 0)


def place_sides(target, k, block, low):
    for piece in range(2):
        part = block[:, piece * 128 : (piece + 1) * 128].reshape(2, 2, 2, 32, 128)
        for side in range(2):
            at = low + side * 128
            target[k * 2 + piece, :, :, :, at : at + 128] = part[:, :, side]


def feed_forward(call_id, rows, seed, own_seed, w_gate, w_up, w_down, middle, inverse, gain):
    count, width = rows.shape
    units = w_gate.shape[1]
    step = 256
    parts = units // step
    places = lax.axis_size(SEQ)
    share = count // 8
    vmem = pl.BlockSpec(memory_space=pltpu.VMEM)
    hbm = pl.BlockSpec(memory_space=pl.ANY)
    shape = jax.ShapeDtypeStruct
    pieces = (places, 2, 2, 32, 3 * step)
    return pl.pallas_call(
        feed_kernel,
        name="feed_forward",
        out_shape=(
            shape((count, units), bf16),
            shape((share, width), f32),
            shape((1, width), f32),
            shape((parts, *pieces[1:]), bf16),
            shape((count, width), bf16),
        ),
        in_specs=[vmem, hbm, vmem, hbm, hbm, hbm]
        + [vmem] * 3,
        out_specs=(vmem, vmem, vmem, vmem, hbm),
        scratch_shapes=[
            pltpu.VMEM((count, width), bf16),
            pltpu.VMEM((parts, width, step), bf16),
            pltpu.VMEM((parts, width, step), bf16),
            pltpu.VMEM((parts, step, width), bf16),
            pltpu.VMEM((width, count), bf16),
            pltpu.VMEM((parts, count, step), bf16),
            pltpu.VMEM((parts, count, step), bf16),
            pltpu.VMEM((parts, *pieces), bf16),
            pltpu.VMEM((parts, 2, 5, 6, *pieces[3:]), bf16),
            pltpu.SemaphoreType.DMA((parts, 2, 60)),
            pltpu.SemaphoreType.DMA((1 + 3 * parts,)),
        ]
        + row_scratch(count, share, width),
        compiler_params=params(call_id),
        cost_estimate=pl.CostEstimate(
            flops=16 * count * width * units, bytes_accessed=32 * 2**20, transcendentals=0
        ),
    )(rows, seed, own_seed, w_gate, w_up, w_down, middle, inverse, gain)


def back_kernel(
    lengths_ref,
    grad_hbm,
    w_out_hbm,
    attended_hbm,
    logits_ref,
    query_ref,
    lse_hbm,
    query_raw_hbm,
    key_raw_hbm,
    gain_query_ref,
    gain_key_ref,
    inner_ref,
    outer_ref,
    middle_ref,
    gain_ref,
    grad_middle_ref,
    gated_ref,
    ffn_gain_ref,
    shares_ref,
    w_gate_ref,
    kv_hbm,
    hidden_hbm,
    w_down_hbm,
    normed_hbm,
    tokens_hbm,
    w_query_hbm,
    w_key_hbm,
    w_value_hbm,
    mixed_out,
    tokens_out,
    sums_out,
    near_out,
    pair_out,
    small_out,
    kv,
    grads,
    recv,
    grad_attended,
    shift,
    delta,
    grad_turned,
    ahead,
    grad_logits,
    near_terms,
    near_came,
    near_share,
    pair_terms,
    pair_came,
    pair_share,
    hidden,
    w_down,
    normed,
    base,
    w_query,
    w_key,
    w_value,
    small_own,
    small_came,
    kv_sems,
    near_sems,
    pair_sems,
    gather_sems,
    small_sems,
    load_sems,
    save_sems,
    grad_ref,
    w_out_ref,
    attended_ref,
    lse_ref,
    query_raw_ref,
    key_raw_ref,
    *row_refs,
):
    ready = greet_sides()
    y, x = plane_place()
    z, core, *_ = group_places()
    share, width = middle_ref.shape
    mine = pl.ds(group_rows(z, core, 0, share), share)
    loads = {}
    for n, (name, source, target) in enumerate(
        (
            ("w_out", w_out_hbm, w_out_ref),
            ("grad", grad_hbm, grad_ref),
            ("attended", attended_hbm, attended_ref),
            ("lse", lse_hbm, lse_ref),
            ("kv", kv_hbm, kv),
            ("hidden", hidden_hbm, hidden),
            ("w_down", w_down_hbm, w_down),
            ("normed", normed_hbm, normed),
            ("base", tokens_hbm.at[mine, :], base),
            ("w_query", w_query_hbm, w_query),
            ("w_key", w_key_hbm, w_key),
            ("w_value", w_value_hbm, w_value),
            ("query_raw", query_raw_hbm, query_raw_ref),
            ("key_raw", key_raw_hbm, key_raw_ref),
        )
    ):
        loads[name] = pltpu.make_async_copy(source, target, load_sems.at[n])
        loads[name].start()
    place = y * 4 + x
    buckets = kv.shape[1]
    block, size = kv.shape[3], kv.shape[4]
    heads = w_out_ref.shape[0] // size
    parts = sums_out.shape[0]
    targets = [sums_out.at[n] for n in range(parts)] + [near_out, pair_out]
    sums = [Gather(spot, gather_sems.at[n]) for n, spot in enumerate(targets)]

    def put_share(n, source):
        copy = pltpu.make_async_copy(source, targets[n].at[place], save_sems.at[n])
        copy.start()
        return copy

    puts = [put_share(n, shares_ref.at[n]) for n in range(parts)]

    def earlier_sums(n):
        puts[n].wait()
        yield from gather_task(sums[n])

    def own_weights(n, scatter, share_ref):
        def keep(path, halves):
            for half, value in enumerate(halves):
                share_ref[path, half] = value.astype(bf16)

        yield from scatter_task(scatter, keep)
        put_share(n, share_ref).wait()
        yield from gather_task(sums[n])

    def mixed_rows():
        loads["hidden"].wait()
        loads["w_down"].wait()
        product = group_product((hidden,), (w_down,), (False,), share, width)

        def finish(total):
            return (middle_ref[...] + total).astype(bf16)

        yield from exchange_task(product, finish, share, ready, mixed_out, row_refs[:11])

    ready()
    beside = in_turn([earlier_sums(0), earlier_sums(1), earlier_sums(2)])
    mixed = mixed_rows()

    def advance(steps):
        for _ in range(steps):
            next(beside, None)

    advance(3)
    for name in ("w_out", "grad", "attended", "lse"):
        loads[name].wait()
    grad_gated = lax.dot_general(
        grad_ref[...], w_out_ref[...], ROW_CONTRACT, preferred_element_type=f32
    )
    gates = jax.nn.sigmoid(logits_ref[...])
    for h in range(heads):
        cols = slice(h * size, (h + 1) * size)
        gate = gates[:, h : h + 1]
        part, attended = grad_gated[:, cols], attended_ref[:, cols]
        along = jnp.sum(part * attended, axis=1, keepdims=True)
        grad_logits[:, h : h + 1] = (along * gate * (1.0 - gate)).astype(bf16)
        low = (part * gate).astype(bf16)
        inner = jnp.sum(low.astype(f32) * attended, axis=1, keepdims=True)
        wide = jnp.broadcast_to(inner, (inner.shape[0], size))
        for b in range(buckets):
            rows = slice(b * block, (b + 1) * block)
            at = slice(h * block, (h + 1) * block)
            grad_attended[b, at, :] = low[rows]
            delta[b, :, at] = wide[rows].T[:8]
    for b in range(buckets):
        shift[b] = lse_ref[b].T[:8]
    grad_turned[...] = jnp.zeros_like(grad_turned)
    next(mixed)
    loads["kv"].wait()
    scale = size**-0.5

    def back(source, b, causal):
        keys, vals = kv[source, b, 0], kv[source, b, 1]
        query = query_ref[b]
        given = grad_attended[b]
        scores = lax.dot_general(keys, query, ROW_CONTRACT, preferred_element_type=f32)
        weights = jnp.exp2(scores * (scale * LOG2_E) - shift[b, 0:1, :])
        if causal:
            spot = lax.broadcasted_iota(jnp.int32, (block, heads * block), 1) % block
            key_spot = lax.broadcasted_iota(jnp.int32, (block, heads * block), 0)
            weights = jnp.where(key_spot <= spot, weights, 0.0)
        grad_weights = lax.dot_general(vals, given, ROW_CONTRACT, preferred_element_type=f32)
        grad_scores = (weights * (grad_weights - delta[b, 0:1, :])).astype(bf16)
        grad_keys = jnp.dot(grad_scores, query, preferred_element_type=f32) * scale
        grad_vals = jnp.dot(weights.astype(bf16), given, preferred_element_type=f32)
        grads[source, b, 0] = grad_keys.astype(bf16)
        grads[source, b, 1] = grad_vals.astype(bf16)
        grad_turned[b] += lax.dot_general(
            keys, grad_scores, COL_CONTRACT, preferred_element_type=f32
        )

    def visit(source, b):
        @pl.when(source < place)
        def _():
            back(source, b, False)

        @pl.when(source > place)
        def _():
            grads[source, b] = jnp.zeros_like(grads[source, b])

    scatter = Scatter(grads, recv, kv_sems)
    order = (2, 1, 3, 0)
    for ring in order:
        for path in (0, 1):

            def one(n, carry):
                visit(place_at(path, ring, choose(n, [2, 1, 3])), path)
                return carry

            lax.fori_loop(0, 3, one, 0)
            scatter.start(path, ring)
            next(mixed, None)
        advance(1)
        if ring != 2:
            previous = order[order.index(ring) - 1]
            for path in (0, 1):
                scatter.forward(path, previous)
    for path in (0, 1):

        def own(n, carry):
            visit(place_at(path, choose(n, [2, 1, 3]), 0), path)
            return carry

        lax.fori_loop(0, 3, own, 0)
    for path in (0, 1):
        scatter.forward(path, 0)
    next(mixed, None)
    advance(1)
    for ring in (2, 1, 3):
        for path in (0, 1):
            scatter.settle(path, ring)
    for path in (0, 1):
        scatter.start(path, 4)
    for b in range(buckets):
        back(place, b, True)
    next(mixed, None)
    advance(1)
    for path in (0, 1):
        scatter.settle(path, 0)
        scatter.forward(path, 4)
    cosine, sine = local_angles(inner_ref, outer_ref, place)

    def turn_back(values):
        return values * cosine - turned(values) * sine

    loads["query_raw"].wait()
    loads["key_raw"].wait()
    gain_sum = jnp.zeros((1, size), f32)
    for b in range(buckets):
        rows = slice(b * block, (b + 1) * block)
        grad_rot = grad_turned[b].T * scale
        for h in range(heads):
            cols = slice(h * size, (h + 1) * size)
            unit, inverse = unit_scale(query_raw_ref[rows, cols])
            straight = turn_back(grad_rot[h * block : (h + 1) * block])
            gain_sum += jnp.sum(straight * unit, axis=0, keepdims=True)
            ahead[rows, cols] = norm_back(
                straight * gain_query_ref[...], unit, inverse
            ).astype(bf16)
    query_gain = gain_sum
    loads["normed"].wait()
    near = heads * size

    def near_weights(n, carry):
        cols = pl.ds(pl.multiple_of(n * 256, 256), 256)
        block = lax.dot_general(
            normed[:, cols], ahead[:, :near], COL_CONTRACT, preferred_element_type=f32
        )
        near_terms[pl.ds(n * 2, 2), :, :, :, 0:near] = block.astype(bf16).reshape(
            2, 2, 2, 32, near
        )
        block = lax.dot_general(
            gated_ref[...], grad_ref[:, cols], COL_CONTRACT, preferred_element_type=f32
        ).astype(bf16)
        place_sides(near_terms, n, block, near)
        return carry

    for n in range(4):
        lax.fori_loop(2 * n, 2 * n + 2, near_weights, 0)
    advance(2)
    near_scatter = Scatter(near_terms, near_came, near_sems)
    near_task = own_weights(parts, near_scatter, near_share)
    next(near_task)
    gain_sum = jnp.zeros((1, size), f32)
    spots = place * block + lax.broadcasted_iota(jnp.int32, (block, size), 0)
    for b in range(buckets):
        rows = slice(b * block, (b + 1) * block)
        live = spots < lengths_ref[b]
        grad_keys, grad_vals = scatter.total(b, 4)
        ahead[rows, (heads + 1) * size :] = jnp.where(live, grad_vals, 0.0).astype(bf16)
        unit, inverse = unit_scale(key_raw_ref[rows, :])
        straight = turn_back(jnp.where(live, grad_keys, 0.0))
        gain_sum += jnp.sum(straight * unit, axis=0, keepdims=True)
        ahead[rows, heads * size : (heads + 1) * size] = norm_back(
            straight * gain_key_ref[...], unit, inverse
        ).astype(bf16)
    key_gain = gain_sum
    split = ahead.shape[1]

    def pair_weights(n, carry):
        cols = pl.ds(pl.multiple_of(n * 256, 256), 256)
        block = lax.dot_general(
            normed[:, cols], ahead[:, near:], COL_CONTRACT, preferred_element_type=f32
        )
        pair_terms[pl.ds(n * 2, 2)] = block.astype(bf16).reshape(2, 2, 2, 32, split - near)
        return carry

    lax.fori_loop(0, width // 256, pair_weights, 0)
    pair_scatter = Scatter(pair_terms, pair_came, pair_sems)
    pair_task = own_weights(parts + 1, pair_scatter, pair_share)
    state = {}

    def token_rows():
        for name in ("w_query", "w_key", "w_value", "base"):
            loads[name].wait()
        cuts = (0, heads * size, (heads + 1) * size, split)
        lefts = [ahead.at[:, a:b] for a, b in zip(cuts, cuts[1:])]
        product = group_product(
            (*lefts, grad_logits),
            (w_query, w_key, w_value, w_gate_ref),
            (True, True, True, False),
            share,
            width,
        )

        def finish(total):
            unit, inverse = unit_scale(base[...].astype(f32))
            state["gain"] = jnp.sum(total * unit, axis=0, keepdims=True)
            back_rows = norm_back(total * gain_ref[...], unit, inverse)
            return (grad_middle_ref[...] + back_rows).astype(bf16)

        yield from exchange_task(product, finish, share, ready, tokens_out, row_refs[11:])

    def small_sums():
        gates = lax.dot_general(
            grad_logits[...], normed[...], COL_CONTRACT, preferred_element_type=f32
        )
        while "gain" not in state:
            yield
        filler = jnp.zeros((1, width - 2 * size), f32)
        both = jnp.concatenate([query_gain, key_gain, filler], axis=1)
        unused = jnp.zeros((5 - gates.shape[0], width), f32)
        value = jnp.concatenate([ffn_gain_ref[...], state["gain"], both, gates, unused], axis=0)
        small_out[...] = yield from spread_small(value, small_own, small_came, small_sems)

    tasks = [pair_task, token_rows(), near_task, beside, small_sums(), mixed]
    run_together(tasks)
    scatter.finish()
    near_scatter.finish()
    pair_scatter.finish()
    for gather in sums:
        gather.finish()


LATE = (0, 1, 2, 5, 6, 7)


def attend_back(call_id, small_operands, large_operands, lengths, query, kv, shares):
    places, buckets, _, block, size = kv.shape
    rows = buckets * block
    hidden, w_down = large_operands[1:3]
    heads = query.shape[1] // block
    width = w_down.shape[1]
    share = rows // 8
    vmem = pl.BlockSpec(memory_space=pltpu.VMEM)
    hbm = pl.BlockSpec(memory_space=pl.ANY)
    shape = jax.ShapeDtypeStruct
    parts = shares.shape[0]
    ahead = (heads + 2) * size
    near = (places, *shares.shape[1:4], 2 * heads * size)
    pair = (places, *shares.shape[1:4], 2 * size)
    dma = pltpu.SemaphoreType.DMA
    return pl.pallas_call(
        back_kernel,
        name="attend_back",
        out_shape=(
            shape((rows, width), bf16),
            shape((rows, width), bf16),
            shape((parts, places, *shares.shape[1:]), bf16),
            shape(near, bf16),
            shape(pair, bf16),
            shape((8, width), f32),
        ),
        in_specs=[pl.BlockSpec(memory_space=pltpu.SMEM)]
        + [hbm if n in LATE else vmem for n in range(len(small_operands))]
        + [hbm] * len(large_operands),
        out_specs=(hbm,) * 5 + (vmem,),
        scratch_shapes=[
            pltpu.VMEM(kv.shape, bf16),
            pltpu.VMEM(kv.shape, bf16),
            pltpu.VMEM((2, 5, 6, block, size), bf16),
            pltpu.VMEM((buckets, heads * block, size), bf16),
            pltpu.VMEM((buckets, 8, heads * block), f32),
            pltpu.VMEM((buckets, 8, heads * block), f32),
            pltpu.VMEM((buckets, size, heads * block), f32),
            pltpu.VMEM((rows, ahead), bf16),
            pltpu.VMEM((rows, heads), bf16),
            pltpu.VMEM(near, bf16),
            pltpu.VMEM((2, 5, 6, *near[3:]), bf16),
            pltpu.VMEM(near[1:], bf16),
            pltpu.VMEM(pair, bf16),
            pltpu.VMEM((2, 5, 6, *pair[3:]), bf16),
            pltpu.VMEM(pair[1:], bf16),
            pltpu.VMEM(hidden.shape, bf16),
            pltpu.VMEM(w_down.shape, bf16),
            pltpu.VMEM((rows, width), bf16),
            pltpu.VMEM((share, width), bf16),
            pltpu.VMEM((width, heads * size), bf16),
            pltpu.VMEM((width, size), bf16),
            pltpu.VMEM((width, size), bf16),
            pltpu.VMEM((8, width), f32),
            pltpu.VMEM((10, 8, width), f32),
            dma((2, 60)),
            dma((2, 60)),
            dma((2, 60)),
            dma((parts + 2, 2, 40)),
            dma((2, 10)),
            dma((14,)),
            dma((parts + 2,)),
        ]
        + [pltpu.VMEM(small_operands[n].shape, small_operands[n].dtype) for n in LATE]
        + row_scratch(rows, share, width)
        + row_scratch(rows, share, width),
        compiler_params=params(call_id),
        cost_estimate=pl.CostEstimate(
            flops=12 * 2**30, bytes_accessed=2**26, transcendentals=2**22
        ),
    )(lengths, *small_operands, *large_operands)


def scatter_task(scatter, finish):
    order = (2, 1, 3, 0)
    both = (0, 1)
    for ring in order:
        for path in both:
            scatter.start(path, ring)
    yield
    for ring in order:
        for path in both:
            scatter.forward(path, ring)
    yield
    for ring in order:
        for path in both:
            scatter.settle(path, ring)
    for path in both:
        scatter.start(path, 4)
    yield
    for path in both:
        scatter.forward(path, 4)
    yield
    for path in both:
        finish(path, scatter.total(path, 4))


def gather_task(gather):
    gather.start()
    for number in range(len(STAGES)):
        yield
        gather.stage(number)


def spread_small(value, own, came, sems):
    first = lax.broadcasted_iota(jnp.int32, value.shape, 0) < 3
    slot = 0
    for axis in ("grp_1", "grp_0", "seq_1", "seq_0"):
        size = lax.axis_size(axis)
        at = lax.axis_index(axis)
        own[...] = value
        copies = []
        for far in range(1, size):
            to = {axis: lax.rem(at + far, size)}
            copies.append(send(own, came.at[slot], sems, slot, to))
            slot += 1
        yield
        for n, copy in enumerate(copies):
            copy.wait_recv()
            part = came[slot - len(copies) + n]
            value = value + (part if axis in SEQ else jnp.where(first, part, 0.0))
        for copy in copies:
            copy.wait_send()
    return value


def spread_kernel(
    feed_ref,
    near_ref,
    pair_ref,
    small_ref,
    gate_out,
    up_out,
    down_out,
    query_out,
    key_out,
    value_out,
    out_out,
    norm_two_out,
    norm_one_out,
    norm_query_out,
    norm_key_out,
    logits_out,
):
    step = feed_ref.shape[-1] // 3
    near = query_out.shape[1]
    single = key_out.shape[1]
    for k in range(near_ref.shape[0]):
        rows = slice(k * 128, (k + 1) * 128)
        for n in range(3):
            cols = slice(n * step, (n + 1) * step)
            part = feed_ref[n, k].reshape(128, 3 * step).astype(f32)
            gate_out[rows, cols] = part[:, :step]
            up_out[rows, cols] = part[:, step : 2 * step]
            down_out[cols, rows] = unplaced(part[:, 2 * step :])
        part = near_ref[k].reshape(128, 2 * near).astype(f32)
        query_out[rows, :] = part[:, :near]
        out_out[:, rows] = unplaced(part[:, near:])
        part = pair_ref[k].reshape(128, 2 * single).astype(f32)
        key_out[rows, :] = part[:, :single]
        value_out[rows, :] = part[:, single:]
    size = norm_query_out.shape[1]
    norm_two_out[...] = small_ref[0:1]
    norm_one_out[...] = small_ref[1:2]
    norm_query_out[...] = small_ref[2:3, :size]
    norm_key_out[...] = small_ref[2:3, size : 2 * size]
    logits_out[...] = small_ref[3 : 3 + logits_out.shape[0]]


def unplaced(part):
    pairs = part.reshape(4, 32, 256)
    return jnp.stack([pairs[:, :, :128], pairs[:, :, 128:]], axis=1).reshape(256, 128)


def spread(parts, near, pair, small, units, query_cols, key_cols, heads):
    count, places = parts.shape[:2]
    width = small.shape[1]
    pace = 2
    block = pace * width // places
    shape = jax.ShapeDtypeStruct

    def strip(cols):
        return pl.BlockSpec((block, cols), lambda s: (s, 0))

    def fixed(rows, cols):
        return pl.BlockSpec((rows, cols), lambda s: (0, 0))

    def column(rows):
        return pl.BlockSpec((rows, block), lambda s: (0, s))

    return pl.pallas_call(
        spread_kernel,
        name="spread",
        grid=(places // pace,),
        in_specs=[
            pl.BlockSpec((count, pace, *parts.shape[2:]), lambda s: (0, s, 0, 0, 0, 0)),
            pl.BlockSpec((pace, *near.shape[1:]), lambda s: (s, 0, 0, 0, 0)),
            pl.BlockSpec((pace, *pair.shape[1:]), lambda s: (s, 0, 0, 0, 0)),
            fixed(*small.shape),
        ],
        out_specs=(
            strip(units),
            strip(units),
            column(units),
            strip(query_cols),
            strip(key_cols),
            strip(key_cols),
            column(query_cols),
            fixed(1, width),
            fixed(1, width),
            fixed(1, key_cols),
            fixed(1, key_cols),
            fixed(heads, width),
        ),
        out_shape=(
            shape((width, units), f32),
            shape((width, units), f32),
            shape((units, width), f32),
            shape((width, query_cols), f32),
            shape((width, key_cols), f32),
            shape((width, key_cols), f32),
            shape((query_cols, width), f32),
            shape((1, width), f32),
            shape((1, width), f32),
            shape((1, key_cols), f32),
            shape((1, key_cols), f32),
            shape((heads, width), f32),
        ),
        compiler_params=pltpu.CompilerParams(vmem_limit_bytes=VMEM_LIMIT),
        cost_estimate=pl.CostEstimate(flops=0, bytes_accessed=36 * 2**20, transcendentals=0),
    )(parts, near, pair, small)


def local(
    tokens,
    lengths,
    norm_attn,
    w_query,
    w_key,
    w_value,
    w_gate,
    norm_query,
    norm_key,
    w_out,
    norm_ffn,
    w_ffn_gate,
    w_ffn_up,
    w_down,
    cotangent,
):
    buckets, per_device, model_width = tokens.shape
    head_count = w_gate.shape[1]
    head_size = norm_query.shape[0]
    total_rows = buckets * per_device
    share_rows = total_rows // lax.axis_size(GRP)
    flat = tokens.reshape(total_rows, model_width)
    tables = angle_tables(per_device, head_size, lax.axis_size(SEQ))
    gains = (norm_query.reshape(1, -1), norm_key.reshape(1, -1))
    gain_one = norm_attn.reshape(1, -1)
    gain_two = norm_ffn.reshape(1, -1)
    gate_rows = w_gate.T
    (
        normed,
        query_raw,
        key_raw,
        logits,
        query_low,
        pairs,
        attended,
        lse,
        gated,
        middle,
        inverse_two,
        normed_two,
        seed,
        own_seed,
    ) = forward(
        1,
        lengths,
        flat,
        gain_one,
        w_query,
        w_key,
        w_value,
        gate_rows,
        gains,
        tables,
        w_out,
        gain_two,
        cotangent.reshape(total_rows, model_width),
    )
    hidden, grad_middle, ffn_gain, shares, grad_attn_low = feed_forward(
        2,
        normed_two,
        seed,
        own_seed,
        w_ffn_gate,
        w_ffn_up,
        w_down,
        middle,
        inverse_two,
        gain_two,
    )
    mixed, grad_tokens, feed_sums, near_sums, pair_sums, small = attend_back(
        3,
        (
            grad_attn_low,
            w_out,
            attended,
            logits,
            query_low,
            lse,
            query_raw,
            key_raw,
            *gains,
            *tables,
            middle,
            gain_one,
            grad_middle,
            gated,
            ffn_gain,
            shares,
            gate_rows,
        ),
        (pairs, hidden, w_down, normed, flat, w_query, w_key, w_value),
        lengths,
        query_low,
        pairs,
        shares,
    )
    (
        grad_gate,
        grad_up,
        grad_down,
        grad_w_query,
        grad_w_key,
        grad_w_value,
        grad_w_out,
        grad_norm_ffn,
        grad_norm_attn,
        grad_norm_query,
        grad_norm_key,
        grad_w_gate,
    ) = spread(
        feed_sums,
        near_sums,
        pair_sums,
        small,
        w_down.shape[0],
        w_query.shape[1],
        w_key.shape[1],
        head_count,
    )
    return (
        mixed.reshape(buckets, per_device, model_width),
        grad_tokens.reshape(buckets, per_device, model_width),
        grad_norm_attn.reshape(-1),
        grad_w_query,
        grad_w_key,
        grad_w_value,
        grad_w_gate.T,
        grad_norm_query.reshape(-1),
        grad_norm_key.reshape(-1),
        grad_w_out,
        grad_norm_ffn.reshape(-1),
        grad_gate,
        grad_up,
        grad_down,
    )


def solution(mesh):
    finer = Mesh(mesh.devices.reshape(4, 4, 4, 2), ("seq_0", "seq_1", "grp_0", "grp_1"))
    return jax.shard_map(
        local,
        mesh=finer,
        in_specs=(
            P(None, SEQ, None),
            P(),
            P(),
            P(None, GRP),
            P(None, GRP),
            P(None, GRP),
            P(None, GRP),
            P(),
            P(),
            P(GRP, None),
            P(),
            P(None, GRP),
            P(None, GRP),
            P(GRP, None),
            P(None, SEQ, None),
        ),
        out_specs=(
            P(None, SEQ, None),
            P(None, SEQ, None),
            P(),
            P(None, GRP),
            P(None, GRP),
            P(None, GRP),
            P(None, GRP),
            P(),
            P(),
            P(GRP, None),
            P(),
            P(None, GRP),
            P(None, GRP),
            P(GRP, None),
        ),
        check_vma=False,
    )
```

```python
import jax
import jax.numpy as jnp
import numpy as np
from jax import lax
from jax.experimental import pallas as pl
from jax.experimental.pallas import tpu as pltpu
from jax.sharding import Mesh
from jax.sharding import PartitionSpec as P

GRP = ("grp_0", "grp_1")
SEQ = ("seq_0", "seq_1")
MESH = pl.DeviceIdType.MESH
VMEM_LIMIT = 60 * 2**20

f32 = jnp.float32
bf16 = jnp.bfloat16


epsilon = 1e-06
rope_base = 1000000.0


def unit_scale(values):
    inverse = lax.rsqrt(jnp.mean(values * values, axis=-1, keepdims=True) + epsilon)
    return (values * inverse, inverse)


def norm_back(grad_unit, unit, inverse):
    return inverse * (grad_unit - unit * jnp.mean(grad_unit * unit, axis=-1, keepdims=True))


ROW_CONTRACT = (((1,), (1,)), ((), ()))
COL_CONTRACT = (((0,), (0,)), ((), ()))


def send(source, target, sems, slot, to):
    copy = pltpu.make_async_remote_copy(
        src_ref=source,
        dst_ref=target,
        send_sem=sems.at[0, slot],
        recv_sem=sems.at[1, slot],
        device_id=to,
        device_id_type=MESH,
    )
    copy.start()
    return copy


def group_places():
    z = lax.axis_index("grp_0")
    core = lax.axis_index("grp_1")
    ring = lax.axis_size("grp_0")
    above = {"grp_0": lax.rem(z + 1, ring)}
    below = {"grp_0": lax.rem(z + ring - 1, ring)}
    twin = {"grp_1": 1 - core}
    return z, core, above, below, twin


def greet(places):
    barrier = pltpu.get_barrier_semaphore()
    for place in places:
        pl.semaphore_signal(barrier, inc=1, device_id=place, device_id_type=MESH)
    return lambda: pl.semaphore_wait(barrier, len(places))


def group_rows(z, core, far, share):
    return pl.multiple_of((lax.rem(z + far, 4) * 2 + core) * share, share)


FAR = (2, 1, 3, 0)


def run_together(tasks, urgent=None, pace=1):
    tasks = list(tasks)
    while tasks:
        for task in list(tasks):
            if urgent is not None:
                for _ in range(pace):
                    next(urgent, None)
            if next(task, tasks) is tasks:
                tasks.remove(task)
    for _ in urgent or ():
        pass


def in_turn(tasks):
    tasks = list(tasks)
    while tasks:
        for task in list(tasks):
            try:
                next(task)
            except StopIteration:
                tasks.remove(task)
            yield


def sum_rows(product, share, ready, scratch):
    mine, twin_out, twin_in, low, ring, twin_sems, ring_sems = scratch
    z, core, above, below, twin = group_places()
    half = share // 2
    top, bottom = pl.ds(0, half), pl.ds(half, half)

    def put_twin(cols, block):
        twin_out[:, :, cols] = block.astype(bf16)

    def put_mine(cols, block):
        mine[:, :, cols] = block

    product(1 - core, put_twin)
    ready()
    pairs = [send(twin_out.at[k], twin_in.at[k], twin_sems, k, twin) for k in range(4)]
    product(core, put_mine)

    def joined(k, rows):
        return mine[k, rows, :] + twin_in[k, rows, :].astype(f32)

    yield
    pairs[0].wait_recv()
    low[0] = joined(0, pl.ds(0, share)).astype(bf16)
    steps = [
        send(low.at[0, top], ring.at[0], ring_sems, 0, above),
        send(low.at[0, bottom], ring.at[1], ring_sems, 1, below),
    ]
    pairs[1].wait_recv()
    low[1, bottom, :] = joined(1, bottom).astype(bf16)
    steps.append(send(low.at[1, bottom], ring.at[2], ring_sems, 2, above))
    pairs[2].wait_recv()
    low[2, top, :] = joined(2, top).astype(bf16)
    steps.append(send(low.at[2, top], ring.at[3], ring_sems, 3, below))
    yield
    steps[0].wait_recv()
    low[1, top, :] = (joined(1, top) + ring[0].astype(f32)).astype(bf16)
    steps.append(send(low.at[1, top], ring.at[4], ring_sems, 4, above))
    yield
    steps[1].wait_recv()
    low[2, bottom, :] = (joined(2, bottom) + ring[1].astype(f32)).astype(bf16)
    steps.append(send(low.at[2, bottom], ring.at[5], ring_sems, 5, below))
    pairs[3].wait_recv()
    yield
    for step in steps[2:]:
        step.wait_recv()
    total = jnp.concatenate(
        [
            joined(3, top) + ring[3].astype(f32) + ring[4].astype(f32),
            joined(3, bottom) + ring[2].astype(f32) + ring[5].astype(f32),
        ],
        axis=0,
    )
    return total, pairs + steps


def join_rows(whole, share, twin_sems, ring_sems):
    z, core, above, below, twin = group_places()
    half = share // 2

    def part(far, side):
        start = group_rows(z, core, far, share)
        return whole.at[pl.ds(pl.multiple_of(start + side * half, half), half), :]

    def hand(far, side, sems, slot, to):
        block = part(far, side)
        return send(block, block, sems, slot, to)

    own = whole.at[pl.ds(group_rows(z, core, 0, share), share), :]
    up = [hand(0, 0, ring_sems, 0, above), hand(0, 1, ring_sems, 1, above)]
    down = [hand(0, 1, ring_sems, 2, below), hand(0, 0, ring_sems, 3, below)]
    across = [send(own, own, twin_sems, 0, twin)]
    yield
    up[0].wait_recv()
    up.append(hand(3, 0, ring_sems, 4, above))
    across.append(hand(3, 0, twin_sems, 1, twin))
    yield
    down[0].wait_recv()
    down.append(hand(1, 1, ring_sems, 5, below))
    across.append(hand(1, 1, twin_sems, 2, twin))
    yield
    up[1].wait_recv()
    across.append(hand(3, 1, twin_sems, 3, twin))
    down[1].wait_recv()
    across.append(hand(1, 0, twin_sems, 4, twin))
    yield
    up[2].wait_recv()
    across.append(hand(2, 0, twin_sems, 5, twin))
    down[2].wait_recv()
    across.append(hand(2, 1, twin_sems, 6, twin))
    yield
    for copy in across:
        copy.wait_recv()
    for copy in up + down + across:
        copy.wait_send()


def row_scratch(rows, share, width):
    return [
        pltpu.VMEM((4, share, width), f32),
        pltpu.VMEM((4, share, width), bf16),
        pltpu.VMEM((4, share, width), bf16),
        pltpu.VMEM((3, share, width), bf16),
        pltpu.VMEM((6, share // 2, width), bf16),
        pltpu.SemaphoreType.DMA((2, 4)),
        pltpu.SemaphoreType.DMA((2, 6)),
        pltpu.VMEM((rows, width), bf16),
        pltpu.SemaphoreType.DMA((2, 7)),
        pltpu.SemaphoreType.DMA((2, 6)),
        pltpu.SemaphoreType.DMA((1,)),
    ]


def group_product(lefts, rights, across, share, width):
    z = lax.axis_index("grp_0")
    step = 512

    def product(core, put):
        picked = []
        for left in lefts:
            blocks = [left[pl.ds(group_rows(z, core, far, share), share), :] for far in FAR]
            picked.append(jnp.concatenate(blocks, axis=0))
        for at in range(0, width, step):
            cols = pl.ds(at, step)
            total = None
            for left, right, flip in zip(picked, rights, across):
                if flip:
                    term = lax.dot_general(
                        left, right[cols, :], ROW_CONTRACT, preferred_element_type=f32
                    )
                else:
                    term = jnp.dot(left, right[:, cols], preferred_element_type=f32)
                total = term if total is None else total + term
            put(cols, total.reshape(4, share, step))

    return product


LOG2_E = 1.4426950408889634
STAGES = (
    ((1, 0), (3, 0), (0, 1), (0, 3)),
    ((2, 0), (0, 2)),
    ((1, 1), (1, 3), (3, 1), (3, 3)),
    ((1, 2), (3, 2), (2, 1), (2, 3)),
    ((2, 2),),
)


def angle_tables(block, size, count):
    half = size // 2
    freq = rope_base ** (-np.arange(half, dtype=np.float64) * (2.0 / size))
    inner = np.arange(block)[:, None] * freq[None, :]
    outer = (np.arange(count) * block)[:, None] * freq[None, :]

    def table(angle):
        sine = np.sin(angle)
        cosine = np.cos(angle)
        both = np.stack(
            [
                np.concatenate([cosine, cosine], axis=1),
                np.concatenate([-sine, sine], axis=1),
            ]
        )
        return both.astype(np.float32)

    return table(inner), table(outer)


def local_angles(inner, outer, place):
    cos_in, sin_in = inner[0], inner[1]
    cos_out = outer[0, pl.ds(place, 1), :]
    sin_out = outer[1, pl.ds(place, 1), :]
    return cos_in * cos_out - sin_in * sin_out, sin_in * cos_out + cos_in * sin_out


def turned(values):
    return pltpu.roll(values, values.shape[-1] // 2, axis=values.ndim - 1)


def plane_place():
    return lax.axis_index("seq_0"), lax.axis_index("seq_1")


def plane_sides(axis):
    at = lax.axis_index(axis)
    size = lax.axis_size(axis)
    return {axis: lax.rem(at + 1, size)}, {axis: lax.rem(at + size - 1, size)}


AXES = (("seq_1", "seq_0"), ("seq_0", "seq_1"))


def place_at(path, first, second):
    y, x = plane_place()
    dx, dy = (first, second) if path == 0 else (second, first)
    return lax.rem(y + dy, 4) * 4 + lax.rem(x + dx, 4)


def pass_start(block, axis, sems, slot):
    up, down = plane_sides(axis)
    return [send(block, block, sems, slot, up), send(block, block, sems, slot + 1, down)]


def pass_on(copies, before, after, axis, sems, slot):
    up, down = plane_sides(axis)
    copies[0].wait_recv()
    copies.append(send(before.at[0], before.at[0], sems, slot + 2, up))
    copies[1].wait_recv()
    copies.append(send(after.at[1], after.at[1], sems, slot + 3, down))


def pass_end(copies):
    copies[2].wait_recv()
    copies[3].wait_recv()


class Gather:
    def __init__(self, buffer, sems):
        self.buffer, self.sems = buffer, sems
        self.rings = [{}, {}]

    def block(self, path, first, second):
        return self.buffer.at[place_at(path, first, second), path]

    def slot(self, path, ring):
        return path * 20 + (4 if ring == "first" else ring) * 4

    def begin(self, path, ring):
        axis = AXES[path][0] if ring == "first" else AXES[path][1]
        block = self.block(path, 0 if ring == "first" else ring, 0)
        self.rings[path][ring] = pass_start(block, axis, self.sems, self.slot(path, ring))

    def forward(self, path, ring):
        if ring == "first":
            axis, before, after = AXES[path][0], self.block(path, 3, 0), self.block(path, 1, 0)
        else:
            axis = AXES[path][1]
            before, after = self.block(path, ring, 3), self.block(path, ring, 1)
        pass_on(self.rings[path][ring], before, after, axis, self.sems, self.slot(path, ring))

    def end(self, path, ring):
        pass_end(self.rings[path][ring])

    def start(self):
        for path in (0, 1):
            self.begin(path, "first")
        for path in (0, 1):
            self.begin(path, 0)

    def stage(self, number):
        for path in (0, 1):
            if number == 0:
                self.forward(path, "first")
                self.begin(path, 1)
                self.begin(path, 3)
                self.forward(path, 0)
            elif number == 1:
                self.end(path, "first")
                self.begin(path, 2)
                self.end(path, 0)
            elif number == 2:
                self.forward(path, 1)
                self.forward(path, 3)
            elif number == 3:
                self.end(path, 1)
                self.end(path, 3)
                self.forward(path, 2)
            else:
                self.end(path, 2)

    def finish(self):
        for rings in self.rings:
            for copies in rings.values():
                for copy in copies:
                    copy.wait_send()


class Scatter:
    def __init__(self, buffer, recv, sems):
        self.buffer, self.recv, self.sems = buffer, recv, sems
        self.copies = {}

    def block(self, path, ring, step):
        if ring == 4:
            return self.buffer.at[place_at(path, step, 0), path]
        return self.buffer.at[place_at(path, ring, step), path]

    def sides(self, path, ring):
        return plane_sides(AXES[path][0] if ring == 4 else AXES[path][1])

    def push(self, path, ring, half_ref, slot, to):
        at = (path * 5 + ring) * 6 + slot
        copy = send(half_ref, self.recv.at[path, ring, slot], self.sems, at, to)
        self.copies.setdefault((path, ring), []).append(copy)

    def start(self, path, ring):
        up, down = self.sides(path, ring)
        far = self.block(path, ring, 2)
        self.push(path, ring, far.at[0], 0, up)
        self.push(path, ring, far.at[1], 1, down)
        self.push(path, ring, self.block(path, ring, 1).at[1], 2, up)
        self.push(path, ring, self.block(path, ring, 3).at[0], 3, down)

    def forward(self, path, ring):
        up, down = self.sides(path, ring)
        for slot, step, half, to in ((0, 1, 0, up), (1, 3, 1, down)):
            self.copies[path, ring][slot].wait_recv()
            part = self.block(path, ring, step).at[half]
            came = self.recv[path, ring, slot]
            part[...] = (part[...].astype(f32) + came.astype(f32)).astype(bf16)
            self.push(path, ring, part, slot + 4, to)

    def total(self, path, ring):
        for copy in self.copies[path, ring][2:]:
            copy.wait_recv()
        own = self.block(path, ring, 0)
        out = []
        for half, slots in ((0, (3, 4)), (1, (2, 5))):
            value = own[half].astype(f32)
            for slot in slots:
                value = value + self.recv[path, ring, slot].astype(f32)
            out.append(value)
        return out

    def settle(self, path, ring):
        own = self.block(path, ring, 0)
        for half, value in enumerate(self.total(path, ring)):
            own[half] = value.astype(bf16)

    def finish(self):
        for copies in self.copies.values():
            for copy in copies:
                copy.wait_send()


def greet_plane():
    places = [*plane_sides("seq_0"), *plane_sides("seq_1")]
    return greet(places)


def choose(index, options):
    value = options[-1]
    for n in range(len(options) - 2, -1, -1):
        value = jnp.where(index == n, options[n], value)
    return value


def once(action):
    done = []

    def call():
        if not done:
            done.append(True)
            action()

    return call


def greet_sides():
    z, core, above, below, twin = group_places()
    places = [*plane_sides("seq_0"), *plane_sides("seq_1"), above, below, twin]
    return once(greet(places))


def exchange_task(product, finish, share, ready, out, scratch):
    z, core, *_ = group_places()
    total, copies = yield from sum_rows(product, share, ready, scratch[:7])
    whole, twin_sems, ring_sems, out_sem = scratch[7:11]
    whole[pl.ds(group_rows(z, core, 0, share), share), :] = finish(total)
    yield from join_rows(whole, share, twin_sems, ring_sems)
    done = pltpu.make_async_copy(whole, out, out_sem.at[0])
    done.start()
    for copy in copies:
        copy.wait_send()
    yield
    done.wait()


def forward_kernel(
    lengths_ref,
    tokens_ref,
    gain_ref,
    w_query_hbm,
    w_key_ref,
    w_value_ref,
    w_gate_ref,
    gain_query_ref,
    gain_key_ref,
    inner_ref,
    outer_ref,
    w_out_hbm,
    gain_two_ref,
    given_hbm,
    normed_out,
    query_raw_out,
    key_raw_out,
    logits_out,
    query_out,
    keys_out,
    attended_out,
    lse_out,
    gated_out,
    middle_out,
    inverse_out,
    normed_two_out,
    seed_out,
    own_seed_out,
    normed,
    kv,
    sums,
    sems,
    out_sems,
    given,
    seed,
    w_query_ref,
    w_out_ref,
    *row_refs,
):
    ready = greet_sides()
    load_given = pltpu.make_async_copy(given_hbm, given, out_sems.at[2])
    load_given.start()
    load_query = pltpu.make_async_copy(w_query_hbm, w_query_ref, out_sems.at[4])
    load_query.start()
    load_out = pltpu.make_async_copy(w_out_hbm, w_out_ref, out_sems.at[5])
    load_out.start()
    y, x = plane_place()
    place = y * 4 + x
    rows, width = tokens_ref.shape
    buckets = kv.shape[1]
    block, size = kv.shape[3], kv.shape[4]
    heads = w_query_ref.shape[1] // size
    step = 64

    def norm_rows(n, carry):
        at = pl.ds(pl.multiple_of(n * step, step), step)
        unit, _ = unit_scale(tokens_ref[at, :].astype(f32))
        normed[at, :] = (unit * gain_ref[...]).astype(bf16)
        return carry

    lax.fori_loop(0, rows // step, norm_rows, 0)
    save_normed = pltpu.make_async_copy(normed, normed_out, out_sems.at[0])
    save_normed.start()
    cosine, sine = local_angles(inner_ref, outer_ref, place)

    def turn(values):
        return values * cosine + turned(values) * sine

    key_raw = jnp.dot(normed[...], w_key_ref[...], preferred_element_type=f32)
    value = jnp.dot(normed[...], w_value_ref[...], preferred_element_type=f32)
    key_raw_out[...] = key_raw
    spots = place * block + lax.broadcasted_iota(jnp.int32, (block, size), 0)
    for b in range(buckets):
        live = spots < lengths_ref[b]
        part = slice(b * block, (b + 1) * block)
        unit, _ = unit_scale(key_raw[part])
        kv[place, b, 0] = jnp.where(live, turn(unit * gain_key_ref[...]), 0.0).astype(bf16)
        kv[place, b, 1] = jnp.where(live, value[part], 0.0).astype(bf16)
    gather = Gather(kv, sems)
    ready()
    gather.start()
    load_query.wait()
    query_raw = jnp.dot(normed[...], w_query_ref[...], preferred_element_type=f32)
    query_raw_out[...] = query_raw
    logits_out[...] = lax.dot_general(
        normed[...], w_gate_ref[...], ROW_CONTRACT, preferred_element_type=f32
    )
    for b in range(buckets):
        for h in range(heads):
            part = query_raw[b * block : (b + 1) * block, h * size : (h + 1) * size]
            unit, _ = unit_scale(part)
            query_out[b, h * block : (h + 1) * block, :] = turn(
                unit * gain_query_ref[...]
            ).astype(bf16)
    scale = size**-0.5 * LOG2_E

    def weigh(source, b, causal):
        keys, vals = kv[source, b, 0], kv[source, b, 1]
        scores = lax.dot_general(query_out[b], keys, ROW_CONTRACT, preferred_element_type=f32)
        weights = jnp.exp2(scores * scale)
        if causal:
            spot = lax.broadcasted_iota(jnp.int32, (heads * block, block), 0) % block
            column = lax.broadcasted_iota(jnp.int32, (heads * block, block), 1)
            weights = jnp.where(column <= spot, weights, 0.0)
        there = source * block + lax.broadcasted_iota(jnp.int32, (block, size), 0)
        ones = jnp.where(there < lengths_ref[b], 1.0, 0.0).astype(bf16)
        both = jnp.concatenate([vals, ones], axis=1)
        return jnp.dot(weights.astype(bf16), both, preferred_element_type=f32)

    load_given.wait()
    make_seed(lengths_ref, given, seed, own_seed_out)
    save_seed = pltpu.make_async_copy(seed, seed_out, out_sems.at[3])
    save_seed.start()
    for b in range(buckets):
        sums[b] = weigh(place, b, True)
    for number, offsets in enumerate(STAGES):
        gather.stage(number)

        def one(n, carry):
            which, b = n // buckets, n % buckets
            dx = choose(which, [o[0] for o in offsets])
            dy = choose(which, [o[1] for o in offsets])
            source = lax.rem(y + dy, 4) * 4 + lax.rem(x + dx, 4)

            @pl.when(source < place)
            def _():
                sums[b] = sums[b] + weigh(source, b, False)

            return carry

        lax.fori_loop(0, len(offsets) * buckets, one, 0)
    save_keys = pltpu.make_async_copy(kv, keys_out, out_sems.at[1])
    save_keys.start()
    gates = jax.nn.sigmoid(logits_out[...])
    for b in range(buckets):
        for h in range(heads):
            at = slice(h * block, (h + 1) * block)
            total = sums[b, at, size:]
            attended = sums[b, at, :size] / total
            here = (slice(b * block, (b + 1) * block), slice(h * size, (h + 1) * size))
            attended_out[here] = attended
            lse_out[b, at, :] = jnp.log2(total)
            gated_out[here] = (attended * gates[here[0], h : h + 1]).astype(bf16)
    share = rows // 8
    z, core, *_ = group_places()
    load_out.wait()
    product = group_product((gated_out,), (w_out_ref,), (False,), share, width)

    def finish(total):
        mine = tokens_ref[pl.ds(group_rows(z, core, 0, share), share), :]
        middle = mine.astype(f32) + total
        unit, inverse = unit_scale(middle)
        middle_out[...] = middle
        inverse_out[...] = inverse
        return (unit * gain_two_ref[...]).astype(bf16)

    run_together([exchange_task(product, finish, share, ready, normed_two_out, row_refs)])
    gather.finish()
    save_normed.wait()
    save_keys.wait()
    save_seed.wait()


def params(call_id):
    return pltpu.CompilerParams(
        collective_id=call_id, has_side_effects=True, vmem_limit_bytes=VMEM_LIMIT
    )


def forward(call_id, lengths, tokens, gain, w_query, w_key, w_value, w_gate, gains, tables, w_out, gain_two, given):
    rows, width = tokens.shape
    size = gains[0].shape[1]
    buckets = lengths.shape[0]
    block = rows // buckets
    heads = w_query.shape[1] // size
    places = lax.axis_size(SEQ)
    share = rows // 8
    vmem = pl.BlockSpec(memory_space=pltpu.VMEM)
    hbm = pl.BlockSpec(memory_space=pl.ANY)
    shape = jax.ShapeDtypeStruct
    pairs = (places, buckets, 2, block, size)
    return pl.pallas_call(
        forward_kernel,
        name="forward",
        out_shape=(
            shape((rows, width), bf16),
            shape((rows, heads * size), f32),
            shape((rows, size), f32),
            shape((rows, heads), f32),
            shape((buckets, heads * block, size), bf16),
            shape(pairs, bf16),
            shape((rows, heads * size), f32),
            shape((buckets, heads * block, size), f32),
            shape((rows, heads * size), bf16),
            shape((share, width), f32),
            shape((share, 1), f32),
            shape((rows, width), bf16),
            shape((rows, width), bf16),
            shape((share, width), f32),
        ),
        in_specs=[pl.BlockSpec(memory_space=pltpu.SMEM)] + [vmem] * 2
        + [hbm]
        + [vmem] * 7
        + [hbm, vmem, hbm],
        out_specs=(hbm, vmem, vmem, vmem, vmem, hbm, vmem, vmem, vmem, vmem, vmem, hbm, hbm, vmem),
        scratch_shapes=[
            pltpu.VMEM((rows, width), bf16),
            pltpu.VMEM(pairs, bf16),
            pltpu.VMEM((buckets, heads * block, 2 * size), f32),
            pltpu.SemaphoreType.DMA((2, 40)),
            pltpu.SemaphoreType.DMA((6,)),
            pltpu.VMEM((rows, width), bf16),
            pltpu.VMEM((rows, width), bf16),
            pltpu.VMEM(w_query.shape, bf16),
            pltpu.VMEM(w_out.shape, bf16),
        ]
        + row_scratch(rows, share, width),
        compiler_params=params(call_id),
        cost_estimate=pl.CostEstimate(
            flops=5 * 2**30, bytes_accessed=16 * 2**20, transcendentals=2**22
        ),
    )(lengths, tokens, gain, w_query, w_key, w_value, w_gate, *gains, *tables, w_out, gain_two, given)


def feed_kernel(
    rows_ref,
    seed_hbm,
    own_seed,
    gate_hbm,
    up_hbm,
    down_hbm,
    middle_ref,
    inverse_ref,
    gain_ref,
    hidden_out,
    grad_middle_out,
    gain_out,
    shares_out,
    rows_out,
    seed,
    gates,
    ups,
    downs,
    rows_across,
    grad_gate,
    grad_up,
    terms,
    came,
    scatter_sems,
    load_sems,
    *row_refs,
):
    rows, width = rows_ref.shape
    count = gates.shape[0]
    step = gates.shape[2]
    load_seed = pltpu.make_async_copy(seed_hbm, seed, load_sems.at[0])
    load_seed.start()
    loads = []
    for n in range(count):
        cols = pl.ds(n * step, step)
        parts = (
            (gate_hbm.at[:, cols], gates.at[n]),
            (up_hbm.at[:, cols], ups.at[n]),
            (down_hbm.at[cols, :], downs.at[n]),
        )
        for k, (source, target) in enumerate(parts):
            loads.append(pltpu.make_async_copy(source, target, load_sems.at[1 + n * 3 + k]))
            loads[-1].start()
    ready = greet_sides()
    share = rows // 8
    rows_across[...] = rows_ref[...].T
    load_seed.wait()
    def activations(n):
        for copy in loads[3 * n : 3 * n + 3]:
            copy.wait()
        cols = slice(n * step, (n + 1) * step)
        gate_pre = jnp.dot(rows_ref[...], gates[n], preferred_element_type=f32)
        up_proj = jnp.dot(rows_ref[...], ups[n], preferred_element_type=f32)
        grad_hidden = lax.dot_general(
            seed[...], downs[n], ROW_CONTRACT, preferred_element_type=f32
        )
        gate_sig = jax.nn.sigmoid(gate_pre)
        silu = gate_pre * gate_sig
        hidden_out[:, cols] = (silu * up_proj).astype(bf16)
        grad_gate[n] = (
            grad_hidden * up_proj * gate_sig * (1.0 + gate_pre * (1.0 - gate_sig))
        ).astype(bf16)
        grad_up[n] = (grad_hidden * silu).astype(bf16)

    def weight_task(n):
        across = hidden_out[:, n * step : (n + 1) * step].T

        def weight_terms(k, carry):
            here = pl.ds(pl.multiple_of(k * 256, 256), 256)
            at = pl.ds(k * 2, 2)
            for side, grad in ((0, grad_gate), (1, grad_up)):
                part = jnp.dot(rows_across[here, :], grad[n], preferred_element_type=f32)
                terms[n, at, :, :, :, side * step : (side + 1) * step] = part.astype(
                    bf16
                ).reshape(2, 2, 2, 32, step)
            part = jnp.dot(across, seed[:, here], preferred_element_type=f32).astype(bf16)
            place_sides(terms.at[n], k, part, 2 * step)
            return carry

        for first in range(0, width // 256, 4):
            lax.fori_loop(first, first + 4, weight_terms, 0)
            yield
        ready()
        scatter = Scatter(terms.at[n], came.at[n], scatter_sems.at[n])
        scatters.append(scatter)

        def keep(path, halves):
            for half, value in enumerate(halves):
                shares_out[n, path, half] = value.astype(bf16)

        yield from scatter_task(scatter, keep)

    def finish_rows(total):
        unit = middle_ref[...] * inverse_ref[...]
        gain_out[...] = jnp.sum(total * unit, axis=0, keepdims=True)
        grad = own_seed[...] + norm_back(total * gain_ref[...], unit, inverse_ref[...])
        grad_middle_out[...] = grad
        return grad.astype(bf16)

    pairs = range(count)
    product = group_product(
        [grad_gate.at[n] for n in pairs] + [grad_up.at[n] for n in pairs],
        [gates.at[n] for n in pairs] + [ups.at[n] for n in pairs],
        (True,) * (2 * count),
        share,
        width,
    )
    scatters = []
    tasks = []
    for n in range(count):
        activations(n)
        tasks.append(weight_task(n))
        for _ in range(3):
            next(tasks[n])
    exchange = exchange_task(product, finish_rows, share, ready, rows_out, row_refs)
    next(exchange)
    next(tasks[0])
    run_together(tasks, exchange, 6)
    for scatter in scatters:
        scatter.finish()


def make_seed(lengths_ref, given_ref, seed, own_seed):
    rows = given_ref.shape[0]
    buckets = lengths_ref.shape[0]
    block = rows // buckets
    share = rows // 8
    y, x = plane_place()
    z, core, *_ = group_places()
    total = lengths_ref[0]
    for b in range(1, buckets):
        total = total + lengths_ref[b]
    places = lax.axis_size("seq_0") * lax.axis_size("seq_1")
    ratio = float(buckets * places * block) / jnp.full((1, 1), total, jnp.int32).astype(f32)

    def weighted(start):
        spots = (
            (y * 4 + x) * block
            + start % block
            + lax.broadcasted_iota(jnp.int32, (share, 1), 0)
        )
        live = (spots < lengths_ref[start // block]).astype(f32)
        at = pl.ds(pl.multiple_of(start, share), share)
        return at, given_ref[at, :].astype(f32) * live * ratio

    own_seed[...] = weighted(group_rows(z, core, 0, share))[1]

    def round_rows(n, carry):
        at, values = weighted(n * share)
        seed[at, :] = values.astype(bf16)
        return carry

    lax.fori_loop(0, 8, round_rows, 0)


def place_sides(target, k, block, low):
    for piece in range(2):
        part = block[:, piece * 128 : (piece + 1) * 128].reshape(2, 2, 2, 32, 128)
        for side in range(2):
            at = low + side * 128
            target[k * 2 + piece, :, :, :, at : at + 128] = part[:, :, side]


def feed_forward(call_id, rows, seed, own_seed, w_gate, w_up, w_down, middle, inverse, gain):
    count, width = rows.shape
    units = w_gate.shape[1]
    step = 256
    parts = units // step
    places = lax.axis_size(SEQ)
    share = count // 8
    vmem = pl.BlockSpec(memory_space=pltpu.VMEM)
    hbm = pl.BlockSpec(memory_space=pl.ANY)
    shape = jax.ShapeDtypeStruct
    pieces = (places, 2, 2, 32, 3 * step)
    return pl.pallas_call(
        feed_kernel,
        name="feed_forward",
        out_shape=(
            shape((count, units), bf16),
            shape((share, width), f32),
            shape((1, width), f32),
            shape((parts, *pieces[1:]), bf16),
            shape((count, width), bf16),
        ),
        in_specs=[vmem, hbm, vmem, hbm, hbm, hbm]
        + [vmem] * 3,
        out_specs=(vmem, vmem, vmem, vmem, hbm),
        scratch_shapes=[
            pltpu.VMEM((count, width), bf16),
            pltpu.VMEM((parts, width, step), bf16),
            pltpu.VMEM((parts, width, step), bf16),
            pltpu.VMEM((parts, step, width), bf16),
            pltpu.VMEM((width, count), bf16),
            pltpu.VMEM((parts, count, step), bf16),
            pltpu.VMEM((parts, count, step), bf16),
            pltpu.VMEM((parts, *pieces), bf16),
            pltpu.VMEM((parts, 2, 5, 6, *pieces[3:]), bf16),
            pltpu.SemaphoreType.DMA((parts, 2, 60)),
            pltpu.SemaphoreType.DMA((1 + 3 * parts,)),
        ]
        + row_scratch(count, share, width),
        compiler_params=params(call_id),
        cost_estimate=pl.CostEstimate(
            flops=16 * count * width * units, bytes_accessed=32 * 2**20, transcendentals=0
        ),
    )(rows, seed, own_seed, w_gate, w_up, w_down, middle, inverse, gain)


def back_kernel(
    lengths_ref,
    grad_hbm,
    w_out_hbm,
    attended_hbm,
    logits_ref,
    query_ref,
    lse_hbm,
    query_raw_hbm,
    key_raw_hbm,
    gain_query_ref,
    gain_key_ref,
    inner_ref,
    outer_ref,
    middle_ref,
    gain_ref,
    grad_middle_ref,
    gated_ref,
    ffn_gain_ref,
    shares_ref,
    w_gate_ref,
    kv_hbm,
    hidden_hbm,
    w_down_hbm,
    normed_hbm,
    tokens_hbm,
    w_query_hbm,
    w_key_hbm,
    w_value_hbm,
    mixed_out,
    tokens_out,
    sums_out,
    near_out,
    pair_out,
    small_out,
    kv,
    grads,
    recv,
    grad_attended,
    shift,
    delta,
    grad_turned,
    ahead,
    grad_logits,
    near_terms,
    near_came,
    near_share,
    pair_terms,
    pair_came,
    pair_share,
    hidden,
    w_down,
    normed,
    base,
    w_query,
    w_key,
    w_value,
    small_own,
    small_came,
    kv_sems,
    near_sems,
    pair_sems,
    gather_sems,
    small_sems,
    load_sems,
    save_sems,
    grad_ref,
    w_out_ref,
    attended_ref,
    lse_ref,
    query_raw_ref,
    key_raw_ref,
    *row_refs,
):
    ready = greet_sides()
    y, x = plane_place()
    z, core, *_ = group_places()
    share, width = middle_ref.shape
    mine = pl.ds(group_rows(z, core, 0, share), share)
    loads = {}
    for n, (name, source, target) in enumerate(
        (
            ("w_out", w_out_hbm, w_out_ref),
            ("grad", grad_hbm, grad_ref),
            ("attended", attended_hbm, attended_ref),
            ("lse", lse_hbm, lse_ref),
            ("kv", kv_hbm, kv),
            ("hidden", hidden_hbm, hidden),
            ("w_down", w_down_hbm, w_down),
            ("normed", normed_hbm, normed),
            ("base", tokens_hbm.at[mine, :], base),
            ("w_query", w_query_hbm, w_query),
            ("w_key", w_key_hbm, w_key),
            ("w_value", w_value_hbm, w_value),
            ("query_raw", query_raw_hbm, query_raw_ref),
            ("key_raw", key_raw_hbm, key_raw_ref),
        )
    ):
        loads[name] = pltpu.make_async_copy(source, target, load_sems.at[n])
        loads[name].start()
    place = y * 4 + x
    buckets = kv.shape[1]
    block, size = kv.shape[3], kv.shape[4]
    heads = w_out_ref.shape[0] // size
    parts = sums_out.shape[0]
    targets = [sums_out.at[n] for n in range(parts)] + [near_out, pair_out]
    sums = [Gather(spot, gather_sems.at[n]) for n, spot in enumerate(targets)]

    def put_share(n, source):
        copy = pltpu.make_async_copy(source, targets[n].at[place], save_sems.at[n])
        copy.start()
        return copy

    puts = [put_share(n, shares_ref.at[n]) for n in range(parts)]

    def earlier_sums(n):
        puts[n].wait()
        yield from gather_task(sums[n])

    def own_weights(n, scatter, share_ref):
        def keep(path, halves):
            for half, value in enumerate(halves):
                share_ref[path, half] = value.astype(bf16)

        yield from scatter_task(scatter, keep)
        put_share(n, share_ref).wait()
        yield from gather_task(sums[n])

    def mixed_rows():
        loads["hidden"].wait()
        loads["w_down"].wait()
        product = group_product((hidden,), (w_down,), (False,), share, width)

        def finish(total):
            return (middle_ref[...] + total).astype(bf16)

        yield from exchange_task(product, finish, share, ready, mixed_out, row_refs[:11])

    ready()
    beside = in_turn([earlier_sums(0), earlier_sums(1), earlier_sums(2)])
    mixed = mixed_rows()

    def advance(steps):
        for _ in range(steps):
            next(beside, None)

    advance(3)
    for name in ("w_out", "grad", "attended", "lse"):
        loads[name].wait()
    grad_gated = lax.dot_general(
        grad_ref[...], w_out_ref[...], ROW_CONTRACT, preferred_element_type=f32
    )
    gates = jax.nn.sigmoid(logits_ref[...])
    for h in range(heads):
        cols = slice(h * size, (h + 1) * size)
        gate = gates[:, h : h + 1]
        part, attended = grad_gated[:, cols], attended_ref[:, cols]
        along = jnp.sum(part * attended, axis=1, keepdims=True)
        grad_logits[:, h : h + 1] = (along * gate * (1.0 - gate)).astype(bf16)
        low = (part * gate).astype(bf16)
        inner = jnp.sum(low.astype(f32) * attended, axis=1, keepdims=True)
        wide = jnp.broadcast_to(inner, (inner.shape[0], size))
        for b in range(buckets):
            rows = slice(b * block, (b + 1) * block)
            at = slice(h * block, (h + 1) * block)
            grad_attended[b, at, :] = low[rows]
            delta[b, :, at] = wide[rows].T[:8]
    for b in range(buckets):
        shift[b] = lse_ref[b].T[:8]
    grad_turned[...] = jnp.zeros_like(grad_turned)
    next(mixed)
    loads["kv"].wait()
    scale = size**-0.5

    def back(source, b, causal):
        keys, vals = kv[source, b, 0], kv[source, b, 1]
        query = query_ref[b]
        given = grad_attended[b]
        scores = lax.dot_general(keys, query, ROW_CONTRACT, preferred_element_type=f32)
        weights = jnp.exp2(scores * (scale * LOG2_E) - shift[b, 0:1, :])
        if causal:
            spot = lax.broadcasted_iota(jnp.int32, (block, heads * block), 1) % block
            key_spot = lax.broadcasted_iota(jnp.int32, (block, heads * block), 0)
            weights = jnp.where(key_spot <= spot, weights, 0.0)
        grad_weights = lax.dot_general(vals, given, ROW_CONTRACT, preferred_element_type=f32)
        grad_scores = (weights * (grad_weights - delta[b, 0:1, :])).astype(bf16)
        grad_keys = jnp.dot(grad_scores, query, preferred_element_type=f32) * scale
        grad_vals = jnp.dot(weights.astype(bf16), given, preferred_element_type=f32)
        grads[source, b, 0] = grad_keys.astype(bf16)
        grads[source, b, 1] = grad_vals.astype(bf16)
        grad_turned[b] += lax.dot_general(
            keys, grad_scores, COL_CONTRACT, preferred_element_type=f32
        )

    def visit(source, b):
        @pl.when(source < place)
        def _():
            back(source, b, False)

        @pl.when(source > place)
        def _():
            grads[source, b] = jnp.zeros_like(grads[source, b])

    scatter = Scatter(grads, recv, kv_sems)
    order = (2, 1, 3, 0)
    for ring in order:
        for path in (0, 1):

            def one(n, carry):
                visit(place_at(path, ring, choose(n, [2, 1, 3])), path)
                return carry

            lax.fori_loop(0, 3, one, 0)
            scatter.start(path, ring)
            next(mixed, None)
        advance(1)
        if ring != 2:
            previous = order[order.index(ring) - 1]
            for path in (0, 1):
                scatter.forward(path, previous)
    for path in (0, 1):

        def own(n, carry):
            visit(place_at(path, choose(n, [2, 1, 3]), 0), path)
            return carry

        lax.fori_loop(0, 3, own, 0)
    for path in (0, 1):
        scatter.forward(path, 0)
    next(mixed, None)
    advance(1)
    for ring in (2, 1, 3):
        for path in (0, 1):
            scatter.settle(path, ring)
    for path in (0, 1):
        scatter.start(path, 4)
    for b in range(buckets):
        back(place, b, True)
    next(mixed, None)
    advance(1)
    for path in (0, 1):
        scatter.settle(path, 0)
        scatter.forward(path, 4)
    cosine, sine = local_angles(inner_ref, outer_ref, place)

    def turn_back(values):
        return values * cosine - turned(values) * sine

    loads["query_raw"].wait()
    loads["key_raw"].wait()
    gain_sum = jnp.zeros((1, size), f32)
    for b in range(buckets):
        rows = slice(b * block, (b + 1) * block)
        grad_rot = grad_turned[b].T * scale
        for h in range(heads):
            cols = slice(h * size, (h + 1) * size)
            unit, inverse = unit_scale(query_raw_ref[rows, cols])
            straight = turn_back(grad_rot[h * block : (h + 1) * block])
            gain_sum += jnp.sum(straight * unit, axis=0, keepdims=True)
            ahead[rows, cols] = norm_back(
                straight * gain_query_ref[...], unit, inverse
            ).astype(bf16)
    query_gain = gain_sum
    loads["normed"].wait()
    near = heads * size

    def near_weights(n, carry):
        cols = pl.ds(pl.multiple_of(n * 256, 256), 256)
        block = lax.dot_general(
            normed[:, cols], ahead[:, :near], COL_CONTRACT, preferred_element_type=f32
        )
        near_terms[pl.ds(n * 2, 2), :, :, :, 0:near] = block.astype(bf16).reshape(
            2, 2, 2, 32, near
        )
        block = lax.dot_general(
            gated_ref[...], grad_ref[:, cols], COL_CONTRACT, preferred_element_type=f32
        ).astype(bf16)
        place_sides(near_terms, n, block, near)
        return carry

    for n in range(4):
        lax.fori_loop(2 * n, 2 * n + 2, near_weights, 0)
    advance(2)
    near_scatter = Scatter(near_terms, near_came, near_sems)
    near_task = own_weights(parts, near_scatter, near_share)
    next(near_task)
    gain_sum = jnp.zeros((1, size), f32)
    spots = place * block + lax.broadcasted_iota(jnp.int32, (block, size), 0)
    for b in range(buckets):
        rows = slice(b * block, (b + 1) * block)
        live = spots < lengths_ref[b]
        grad_keys, grad_vals = scatter.total(b, 4)
        ahead[rows, (heads + 1) * size :] = jnp.where(live, grad_vals, 0.0).astype(bf16)
        unit, inverse = unit_scale(key_raw_ref[rows, :])
        straight = turn_back(jnp.where(live, grad_keys, 0.0))
        gain_sum += jnp.sum(straight * unit, axis=0, keepdims=True)
        ahead[rows, heads * size : (heads + 1) * size] = norm_back(
            straight * gain_key_ref[...], unit, inverse
        ).astype(bf16)
    key_gain = gain_sum
    split = ahead.shape[1]

    def pair_weights(n, carry):
        cols = pl.ds(pl.multiple_of(n * 256, 256), 256)
        block = lax.dot_general(
            normed[:, cols], ahead[:, near:], COL_CONTRACT, preferred_element_type=f32
        )
        pair_terms[pl.ds(n * 2, 2)] = block.astype(bf16).reshape(2, 2, 2, 32, split - near)
        return carry

    lax.fori_loop(0, width // 256, pair_weights, 0)
    pair_scatter = Scatter(pair_terms, pair_came, pair_sems)
    pair_task = own_weights(parts + 1, pair_scatter, pair_share)
    state = {}

    def token_rows():
        for name in ("w_query", "w_key", "w_value", "base"):
            loads[name].wait()
        cuts = (0, heads * size, (heads + 1) * size, split)
        lefts = [ahead.at[:, a:b] for a, b in zip(cuts, cuts[1:])]
        product = group_product(
            (*lefts, grad_logits),
            (w_query, w_key, w_value, w_gate_ref),
            (True, True, True, False),
            share,
            width,
        )

        def finish(total):
            unit, inverse = unit_scale(base[...].astype(f32))
            state["gain"] = jnp.sum(total * unit, axis=0, keepdims=True)
            back_rows = norm_back(total * gain_ref[...], unit, inverse)
            return (grad_middle_ref[...] + back_rows).astype(bf16)

        yield from exchange_task(product, finish, share, ready, tokens_out, row_refs[11:])

    def small_sums():
        gates = lax.dot_general(
            grad_logits[...], normed[...], COL_CONTRACT, preferred_element_type=f32
        )
        while "gain" not in state:
            yield
        filler = jnp.zeros((1, width - 2 * size), f32)
        both = jnp.concatenate([query_gain, key_gain, filler], axis=1)
        unused = jnp.zeros((5 - gates.shape[0], width), f32)
        value = jnp.concatenate([ffn_gain_ref[...], state["gain"], both, gates, unused], axis=0)
        small_out[...] = yield from spread_small(value, small_own, small_came, small_sems)

    tasks = [pair_task, token_rows(), near_task, beside, small_sums(), mixed]
    run_together(tasks)
    scatter.finish()
    near_scatter.finish()
    pair_scatter.finish()
    for gather in sums:
        gather.finish()


LATE = (0, 1, 2, 5, 6, 7)


def attend_back(call_id, small_operands, large_operands, lengths, query, kv, shares):
    places, buckets, _, block, size = kv.shape
    rows = buckets * block
    hidden, w_down = large_operands[1:3]
    heads = query.shape[1] // block
    width = w_down.shape[1]
    share = rows // 8
    vmem = pl.BlockSpec(memory_space=pltpu.VMEM)
    hbm = pl.BlockSpec(memory_space=pl.ANY)
    shape = jax.ShapeDtypeStruct
    parts = shares.shape[0]
    ahead = (heads + 2) * size
    near = (places, *shares.shape[1:4], 2 * heads * size)
    pair = (places, *shares.shape[1:4], 2 * size)
    dma = pltpu.SemaphoreType.DMA
    return pl.pallas_call(
        back_kernel,
        name="attend_back",
        out_shape=(
            shape((rows, width), bf16),
            shape((rows, width), bf16),
            shape((parts, places, *shares.shape[1:]), bf16),
            shape(near, bf16),
            shape(pair, bf16),
            shape((8, width), f32),
        ),
        in_specs=[pl.BlockSpec(memory_space=pltpu.SMEM)]
        + [hbm if n in LATE else vmem for n in range(len(small_operands))]
        + [hbm] * len(large_operands),
        out_specs=(hbm,) * 5 + (vmem,),
        scratch_shapes=[
            pltpu.VMEM(kv.shape, bf16),
            pltpu.VMEM(kv.shape, bf16),
            pltpu.VMEM((2, 5, 6, block, size), bf16),
            pltpu.VMEM((buckets, heads * block, size), bf16),
            pltpu.VMEM((buckets, 8, heads * block), f32),
            pltpu.VMEM((buckets, 8, heads * block), f32),
            pltpu.VMEM((buckets, size, heads * block), f32),
            pltpu.VMEM((rows, ahead), bf16),
            pltpu.VMEM((rows, heads), bf16),
            pltpu.VMEM(near, bf16),
            pltpu.VMEM((2, 5, 6, *near[3:]), bf16),
            pltpu.VMEM(near[1:], bf16),
            pltpu.VMEM(pair, bf16),
            pltpu.VMEM((2, 5, 6, *pair[3:]), bf16),
            pltpu.VMEM(pair[1:], bf16),
            pltpu.VMEM(hidden.shape, bf16),
            pltpu.VMEM(w_down.shape, bf16),
            pltpu.VMEM((rows, width), bf16),
            pltpu.VMEM((share, width), bf16),
            pltpu.VMEM((width, heads * size), bf16),
            pltpu.VMEM((width, size), bf16),
            pltpu.VMEM((width, size), bf16),
            pltpu.VMEM((8, width), f32),
            pltpu.VMEM((10, 8, width), f32),
            dma((2, 60)),
            dma((2, 60)),
            dma((2, 60)),
            dma((parts + 2, 2, 40)),
            dma((2, 10)),
            dma((14,)),
            dma((parts + 2,)),
        ]
        + [pltpu.VMEM(small_operands[n].shape, small_operands[n].dtype) for n in LATE]
        + row_scratch(rows, share, width)
        + row_scratch(rows, share, width),
        compiler_params=params(call_id),
        cost_estimate=pl.CostEstimate(
            flops=12 * 2**30, bytes_accessed=2**26, transcendentals=2**22
        ),
    )(lengths, *small_operands, *large_operands)


def scatter_task(scatter, finish):
    order = (2, 1, 3, 0)
    both = (0, 1)
    for ring in order:
        for path in both:
            scatter.start(path, ring)
    yield
    for ring in order:
        for path in both:
            scatter.forward(path, ring)
    yield
    for ring in order:
        for path in both:
            scatter.settle(path, ring)
    for path in both:
        scatter.start(path, 4)
    yield
    for path in both:
        scatter.forward(path, 4)
    yield
    for path in both:
        finish(path, scatter.total(path, 4))


def gather_task(gather):
    gather.start()
    for number in range(len(STAGES)):
        yield
        gather.stage(number)


def spread_small(value, own, came, sems):
    first = lax.broadcasted_iota(jnp.int32, value.shape, 0) < 3
    slot = 0
    for axis in ("grp_1", "grp_0", "seq_1", "seq_0"):
        size = lax.axis_size(axis)
        at = lax.axis_index(axis)
        own[...] = value
        copies = []
        for far in range(1, size):
            to = {axis: lax.rem(at + far, size)}
            copies.append(send(own, came.at[slot], sems, slot, to))
            slot += 1
        yield
        for n, copy in enumerate(copies):
            copy.wait_recv()
            part = came[slot - len(copies) + n]
            value = value + (part if axis in SEQ else jnp.where(first, part, 0.0))
        for copy in copies:
            copy.wait_send()
    return value


def spread_kernel(
    feed_ref,
    near_ref,
    pair_ref,
    small_ref,
    gate_out,
    up_out,
    down_out,
    query_out,
    key_out,
    value_out,
    out_out,
    norm_two_out,
    norm_one_out,
    norm_query_out,
    norm_key_out,
    logits_out,
):
    step = feed_ref.shape[-1] // 3
    near = query_out.shape[1]
    single = key_out.shape[1]
    for k in range(near_ref.shape[0]):
        rows = slice(k * 128, (k + 1) * 128)
        for n in range(3):
            cols = slice(n * step, (n + 1) * step)
            part = feed_ref[n, k].reshape(128, 3 * step).astype(f32)
            gate_out[rows, cols] = part[:, :step]
            up_out[rows, cols] = part[:, step : 2 * step]
            down_out[cols, rows] = unplaced(part[:, 2 * step :])
        part = near_ref[k].reshape(128, 2 * near).astype(f32)
        query_out[rows, :] = part[:, :near]
        out_out[:, rows] = unplaced(part[:, near:])
        part = pair_ref[k].reshape(128, 2 * single).astype(f32)
        key_out[rows, :] = part[:, :single]
        value_out[rows, :] = part[:, single:]
    size = norm_query_out.shape[1]
    norm_two_out[...] = small_ref[0:1]
    norm_one_out[...] = small_ref[1:2]
    norm_query_out[...] = small_ref[2:3, :size]
    norm_key_out[...] = small_ref[2:3, size : 2 * size]
    logits_out[...] = small_ref[3 : 3 + logits_out.shape[0]]


def unplaced(part):
    pairs = part.reshape(4, 32, 256)
    return jnp.stack([pairs[:, :, :128], pairs[:, :, 128:]], axis=1).reshape(256, 128)


def spread(parts, near, pair, small, units, query_cols, key_cols, heads):
    count, places = parts.shape[:2]
    width = small.shape[1]
    pace = 4
    block = pace * width // places
    shape = jax.ShapeDtypeStruct

    def strip(cols):
        return pl.BlockSpec((block, cols), lambda s: (s, 0))

    def fixed(rows, cols):
        return pl.BlockSpec((rows, cols), lambda s: (0, 0))

    def column(rows):
        return pl.BlockSpec((rows, block), lambda s: (0, s))

    return pl.pallas_call(
        spread_kernel,
        name="spread",
        grid=(places // pace,),
        in_specs=[
            pl.BlockSpec((count, pace, *parts.shape[2:]), lambda s: (0, s, 0, 0, 0, 0)),
            pl.BlockSpec((pace, *near.shape[1:]), lambda s: (s, 0, 0, 0, 0)),
            pl.BlockSpec((pace, *pair.shape[1:]), lambda s: (s, 0, 0, 0, 0)),
            fixed(*small.shape),
        ],
        out_specs=(
            strip(units),
            strip(units),
            column(units),
            strip(query_cols),
            strip(key_cols),
            strip(key_cols),
            column(query_cols),
            fixed(1, width),
            fixed(1, width),
            fixed(1, key_cols),
            fixed(1, key_cols),
            fixed(heads, width),
        ),
        out_shape=(
            shape((width, units), f32),
            shape((width, units), f32),
            shape((units, width), f32),
            shape((width, query_cols), f32),
            shape((width, key_cols), f32),
            shape((width, key_cols), f32),
            shape((query_cols, width), f32),
            shape((1, width), f32),
            shape((1, width), f32),
            shape((1, key_cols), f32),
            shape((1, key_cols), f32),
            shape((heads, width), f32),
        ),
        compiler_params=pltpu.CompilerParams(vmem_limit_bytes=VMEM_LIMIT),
        cost_estimate=pl.CostEstimate(flops=0, bytes_accessed=36 * 2**20, transcendentals=0),
    )(parts, near, pair, small)


def local(
    tokens,
    lengths,
    norm_attn,
    w_query,
    w_key,
    w_value,
    w_gate,
    norm_query,
    norm_key,
    w_out,
    norm_ffn,
    w_ffn_gate,
    w_ffn_up,
    w_down,
    cotangent,
):
    buckets, per_device, model_width = tokens.shape
    head_count = w_gate.shape[1]
    head_size = norm_query.shape[0]
    total_rows = buckets * per_device
    share_rows = total_rows // lax.axis_size(GRP)
    flat = tokens.reshape(total_rows, model_width)
    tables = angle_tables(per_device, head_size, lax.axis_size(SEQ))
    gains = (norm_query.reshape(1, -1), norm_key.reshape(1, -1))
    gain_one = norm_attn.reshape(1, -1)
    gain_two = norm_ffn.reshape(1, -1)
    gate_rows = w_gate.T
    (
        normed,
        query_raw,
        key_raw,
        logits,
        query_low,
        pairs,
        attended,
        lse,
        gated,
        middle,
        inverse_two,
        normed_two,
        seed,
        own_seed,
    ) = forward(
        1,
        lengths,
        flat,
        gain_one,
        w_query,
        w_key,
        w_value,
        gate_rows,
        gains,
        tables,
        w_out,
        gain_two,
        cotangent.reshape(total_rows, model_width),
    )
    hidden, grad_middle, ffn_gain, shares, grad_attn_low = feed_forward(
        2,
        normed_two,
        seed,
        own_seed,
        w_ffn_gate,
        w_ffn_up,
        w_down,
        middle,
        inverse_two,
        gain_two,
    )
    mixed, grad_tokens, feed_sums, near_sums, pair_sums, small = attend_back(
        3,
        (
            grad_attn_low,
            w_out,
            attended,
            logits,
            query_low,
            lse,
            query_raw,
            key_raw,
            *gains,
            *tables,
            middle,
            gain_one,
            grad_middle,
            gated,
            ffn_gain,
            shares,
            gate_rows,
        ),
        (pairs, hidden, w_down, normed, flat, w_query, w_key, w_value),
        lengths,
        query_low,
        pairs,
        shares,
    )
    (
        grad_gate,
        grad_up,
        grad_down,
        grad_w_query,
        grad_w_key,
        grad_w_value,
        grad_w_out,
        grad_norm_ffn,
        grad_norm_attn,
        grad_norm_query,
        grad_norm_key,
        grad_w_gate,
    ) = spread(
        feed_sums,
        near_sums,
        pair_sums,
        small,
        w_down.shape[0],
        w_query.shape[1],
        w_key.shape[1],
        head_count,
    )
    return (
        mixed.reshape(buckets, per_device, model_width),
        grad_tokens.reshape(buckets, per_device, model_width),
        grad_norm_attn.reshape(-1),
        grad_w_query,
        grad_w_key,
        grad_w_value,
        grad_w_gate.T,
        grad_norm_query.reshape(-1),
        grad_norm_key.reshape(-1),
        grad_w_out,
        grad_norm_ffn.reshape(-1),
        grad_gate,
        grad_up,
        grad_down,
    )


def solution(mesh):
    finer = Mesh(mesh.devices.reshape(4, 4, 4, 2), ("seq_0", "seq_1", "grp_0", "grp_1"))
    return jax.shard_map(
        local,
        mesh=finer,
        in_specs=(
            P(None, SEQ, None),
            P(),
            P(),
            P(None, GRP),
            P(None, GRP),
            P(None, GRP),
            P(None, GRP),
            P(),
            P(),
            P(GRP, None),
            P(),
            P(None, GRP),
            P(None, GRP),
            P(GRP, None),
            P(None, SEQ, None),
        ),
        out_specs=(
            P(None, SEQ, None),
            P(None, SEQ, None),
            P(),
            P(None, GRP),
            P(None, GRP),
            P(None, GRP),
            P(None, GRP),
            P(),
            P(),
            P(GRP, None),
            P(),
            P(None, GRP),
            P(None, GRP),
            P(GRP, None),
        ),
        check_vma=False,
    )
```
